512 devices in a mesh: seq: 128 (over z, x, core), ch: 4 (over y).
Axes of the slice: x: 4, y: 4, z: 16, core: 2. Of those that a mesh axis runs over, the one named last changes fastest.
Arguments:
- out_grad: float32 [128, 524288], P('ch', 'seq'), may hold values from -6 to 6
- gated_input: float32 [128, 524288], P('ch', 'seq'), may hold values from -6 to 6
- features: float32 [64, 524288], P(None, 'seq'), may hold values from -1 to 1
- filter_weight: float32 [64, 128], replicated, may hold values from -0.001953125 to 0.001953125
- rates: float32 [128], replicated, may hold values from 3 to 15
- skip_bias: float32 [128], replicated, may hold values from -3 to 3
Outputs:
- in_grad: float32 [128, 524288], P('ch', 'seq')
- feat_grad: float32 [64, 524288], P(None, ('seq', 'ch'))
The draws below stay inside these ranges and needn't reach their ends.
All inputs are finite; a program needn't handle non-finite values.
Results may differ from the reference program's by a relative error of at most 0.0003.
Values sent between devices are 32-bit elements; how exact they have to be, the bound alone decides.
No kernel may reach another device: no remote copies, remote signals or barrier semaphores. Data moves between devices by JAX's collectives and lax.ppermute only.
A program may use at most 128 MiB of HBM per device.

```python
import math
import jax
import jax.numpy as jnp
from jax import lax

CH = 128
FO = 64
L = 524288


def block_levels(own_key, shape, pieces, least, largest):
    loudness, own = 1.0, jax.random.fold_in(own_key, 6)
    for dim, parts in pieces:
        steps = jnp.exp(jax.random.uniform(jax.random.fold_in(own, dim), (parts,), jnp.float32, least / len(pieces), largest / len(pieces)))
        loudness = loudness * jnp.repeat(steps, shape[dim] // parts).reshape([-1 if axis == dim else 1 for axis in range(len(shape))])
    return loudness


def normal_values(rng, shape, spread, most, split=(), held_as=jnp.bfloat16):
    values = jax.random.normal(rng, shape, jnp.float32) * spread
    if len(split) > 0:
        values = block_levels(rng, shape, split, -0.22, 0.18) * values
    return jnp.clip(values, min=-most, max=most).astype(held_as)


def setup_inputs(seed: int = 0) -> dict:
    key_of = jax.random.split(jax.random.key(seed), 7)
    return {
        "out_grad": normal_values(key_of[0], (CH, L), 1.0, 6.0, ((0, 4), (1, 128)), jnp.float32),
        "gated_input": normal_values(key_of[1], (CH, L), 1.0, 6.0, ((0, 4), (1, 128)), jnp.float32),
        "features": jnp.clip(jax.random.uniform(key_of[2], (FO, L), jnp.float32, -1.0, 1.0) * block_levels(key_of[2], (FO, L), ((1, 128),), -0.4, 0.0), -1.0, 1.0),
        "filter_weight": normal_values(key_of[3], (FO, CH), (FO * L // 4) ** -0.5, 0.001953125, (), jnp.float32),
        "rates": jnp.clip(jnp.exp(jax.random.uniform(key_of[4], (CH,), jnp.float32, math.log(3.0), math.log(15.0))), 3.0, 15.0),
        "skip_bias": normal_values(key_of[5], (CH,), 1.0, 3.0, (), jnp.float32),
    }


shift_term = 0.05


def reference(out_grad, gated_input, features, filter_weight, rates, skip_bias):
    steps_t = jnp.arange(L).astype(jnp.float32) / L
    window = jnp.exp(-rates[:, None] * steps_t[None, :]) + shift_term
    filter_vals = jnp.dot(filter_weight.T, features, precision=lax.Precision.HIGHEST, preferred_element_type=jnp.float32) * window
    group_size = math.gcd(CH, 8)
    padded_len = 2 * L

    def one_group(operands):
        grad_block, input_block, filter_block = operands
        grad_spec = jnp.fft.rfft(grad_block, n=padded_len, axis=-1)
        input_spec = jnp.fft.rfft(input_block, n=padded_len, axis=-1)
        filter_spec = jnp.fft.rfft(filter_block, n=padded_len, axis=-1)
        conv_part = jnp.fft.irfft(jnp.conj(filter_spec) * grad_spec, n=padded_len, axis=-1)[:, :L]
        lag_part = jnp.fft.irfft(jnp.conj(input_spec) * grad_spec, n=padded_len, axis=-1)[:, :L]
        return conv_part.astype(jnp.float32), lag_part.astype(jnp.float32)

    def stacked(values):
        return values.reshape(CH // group_size, group_size, L)

    conv_grad, filt_grad = lax.map(one_group, (stacked(out_grad), stacked(gated_input), stacked(filter_vals)))
    conv_grad = conv_grad.reshape(CH, L)
    filt_grad = filt_grad.reshape(CH, L)
    in_grad = conv_grad + skip_bias[:, None] * out_grad
    feat_grad = jnp.dot(filter_weight, filt_grad * window, precision=lax.Precision.HIGHEST, preferred_element_type=jnp.float32)
    return in_grad, feat_grad
```

```python
import functools
import math

import jax
import jax.numpy as jnp
import numpy as np
from jax import lax
from jax.experimental import pallas as pl
from jax.experimental.pallas import tpu as pltpu
from jax.sharding import PartitionSpec as P

SHIFT = 0.05
LANES = 128
ROWS = 32
BLOCK = ROWS * LANES
HALF = ROWS // 2
QUART = HALF // 2
CHUNK = HALF + QUART
VMEM_BYTES = 40 * 1024 * 1024


def as_pair(values):
    high = values.astype(jnp.bfloat16)
    return high, (values - high.astype(np.float32)).astype(jnp.bfloat16)


@functools.lru_cache(maxsize=None)
def tables(seq_count):
    points = seq_count // 2
    angle = 2.0 * np.pi
    mix_in, mix_out, twist = [], [], []
    dev = np.arange(seq_count)
    pos = np.arange(BLOCK)
    for half in range(2):
        freq = 4 * (2 * np.arange(points) + half) + 1
        step = angle * (np.outer(freq, dev) % (4 * seq_count)) / (4 * seq_count)
        forward = np.concatenate([np.cos(step), -np.sin(step)]).astype(np.float32)
        backward = forward.T / np.float32(seq_count * BLOCK)
        for out, matrix in ((mix_in, forward), (mix_out, backward)):
            high, low = as_pair(matrix)
            out.append(
                np.concatenate(
                    [
                        np.concatenate([high, high], axis=1),
                        np.concatenate([low, np.zeros_like(low)], axis=1),
                    ]
                )
            )
        turn = angle * (np.outer(freq, pos) / (4.0 * seq_count * BLOCK))
        turn = turn.reshape(points, ROWS, LANES).transpose(1, 0, 2)
        twist.append(np.stack([np.cos(turn), -np.sin(turn)]).astype(np.float32))
    inner = angle * np.outer(np.arange(ROWS), np.arange(LANES)) / BLOCK
    inner = np.stack([np.cos(inner), -np.sin(inner)]).astype(np.float32)
    lane = angle * (np.outer(np.arange(LANES), np.arange(LANES)) % LANES) / LANES
    cos, sin = np.cos(lane), np.sin(lane)
    lane_mat = np.block([[cos, -sin], [sin, cos]]).astype(np.float32)
    return (
        np.stack(mix_in),
        np.stack(mix_out),
        np.stack(twist),
        inner,
        np.stack(as_pair(lane_mat)),
        np.stack(as_pair(np.ascontiguousarray(lane_mat.T))),
    )


def dot(left, right):
    return jnp.dot(left, right, preferred_element_type=jnp.float32)


def split(values):
    high = values.astype(jnp.bfloat16)
    low = (values - high.astype(jnp.float32)).astype(jnp.bfloat16)
    return high, low


def times(a, b, re, im):
    return a * re - b * im, a * im + b * re


def scaled(a, b, number, sign):
    re, im = math.cos(number), sign * math.sin(number)
    if abs(im) < 1e-12 and re > 0:
        return a, b
    if abs(re) < 1e-12:
        return (-b, a) if im > 0 else (b, -a)
    return a * re - b * im, a * im + b * re


def four_points(vals, sign):
    (ar, ai), (br, bi), (cr, ci), (dr, di) = vals
    sr, si = ar + cr, ai + ci
    tr, ti = ar - cr, ai - ci
    ur, ui = br + dr, bi + di
    vr, vi = br - dr, bi - di
    if sign < 0:
        vr, vi = vi, -vr
    else:
        vr, vi = -vi, vr
    return [(sr + ur, si + ui), (tr + vr, ti + vi), (sr - ur, si - ui), (tr - vr, ti - vi)]


def eight_points(vals, sign):
    even = four_points(vals[0::2], sign)
    odd = four_points(vals[1::2], sign)
    low, high = [], []
    for index in range(4):
        er, ei = even[index]
        tr, ti = scaled(*odd[index], 2.0 * math.pi * index / 8, sign)
        low.append((er + tr, ei + ti))
        high.append((er - tr, ei - ti))
    return low + high


def short_transform(re_ref, im_ref, points, sign, finish):
    def tile(index, carry):
        rows = pl.ds(pl.multiple_of(index * 8, 8), 8)
        for second in range(8):
            vals = [(re_ref[8 * n + second, rows, :], im_ref[8 * n + second, rows, :]) for n in range(4)]
            vals = four_points(vals, sign)
            for k in range(4):
                re, im = scaled(*vals[k], 2.0 * math.pi * k * second / ROWS, sign)
                re_ref[8 * k + second, rows, :] = re
                im_ref[8 * k + second, rows, :] = im
        for k in range(4):
            vals = [(re_ref[8 * k + n, rows, :], im_ref[8 * k + n, rows, :]) for n in range(8)]
            vals = eight_points(vals, sign)
            for j in range(8):
                finish(k + 4 * j, rows, *vals[j])
        return carry

    lax.fori_loop(0, points // 8, tile, 0)


def forward(load, points, mix_ref, twist_ref, inner_ref, re_ref, im_ref, lane_in_ref):
    count = 2 * points
    for row in range(HALF):
        high, low = split(jnp.concatenate(load(row), axis=1))
        full = dot(mix_ref[0], jnp.concatenate([high, low], axis=0))
        full = full[:count] + full[count:]
        for part in range(2):
            place = row + part * HALF
            lanes = slice(part * LANES, (part + 1) * LANES)
            re, im = times(
                full[:points, lanes],
                full[points:, lanes],
                twist_ref[0, 0, place],
                twist_ref[0, 1, place],
            )
            re_ref[place] = re
            im_ref[place] = im

    def finish(k, rows, re, im):
        re, im = times(re, im, inner_ref[0, k : k + 1, :], inner_ref[1, k : k + 1, :])
        lane_in_ref[k, rows, :LANES] = re
        lane_in_ref[k, rows, LANES:] = im

    short_transform(re_ref, im_ref, points, -1.0, finish)


def lane_product(values, lane_ref):
    high, low = split(values)
    return dot(high, lane_ref[0]) + dot(low, lane_ref[0]) + dot(high, lane_ref[1])


def spread_rows(ids, values):
    return jnp.broadcast_to(values, (LANES, values.shape[1])).T


def window_tile(rate_tile, first, row, total):
    lane = lax.broadcasted_iota(jnp.int32, rate_tile.shape, 1)
    place = (first + row * LANES + lane).astype(jnp.float32) * (1.0 / total)
    return jnp.exp(-rate_tile * place) + SHIFT


def prepare_kernel(
    total, ids, grad_ref, input_ref, feat_ref, weight_ref, rates_ref, out_ref, weight_t, rate_t
):
    channels = grad_ref.shape[0]
    first = ids[3] * BLOCK
    own = pl.ds(pl.multiple_of(ids[2] * channels, 8), channels)
    weight_t[...] = weight_ref[...].T
    rate_t[...] = spread_rows(ids, rates_ref[...])
    high, low = split(weight_t[own, :])
    both = jnp.concatenate([high, low], axis=0)
    rate_tile = rate_t[own, :]
    wide = 2 * LANES
    for pair in range(BLOCK // wide):
        lanes = slice(pair * wide, (pair + 1) * wide)
        feat_high, feat_low = split(feat_ref[:, lanes])
        full = dot(both, feat_high)
        full = full[:channels] + full[channels:] + dot(high, feat_low)
        for part in range(2):
            row = 2 * pair + part
            half, quart = row // HALF, (row // QUART) % 2
            filt = full[:, part * LANES : (part + 1) * LANES]
            filt = filt * window_tile(rate_tile, first, row, total)
            here = slice(row * LANES, (row + 1) * LANES)
            base = half * CHUNK + row % HALF
            out_ref[pl.ds(base, channels, stride=4 * CHUNK), :] = filt
            base = 2 * CHUNK + half * CHUNK + row % HALF
            out_ref[pl.ds(base, channels, stride=4 * CHUNK), :] = input_ref[:, here]
            base = quart * 2 * CHUNK + half * CHUNK + HALF + row % QUART
            out_ref[pl.ds(base, channels, stride=4 * CHUNK), :] = grad_ref[:, here]


def first_kernel(
    ids, own_ref, other_ref, mix_ref, twist_ref, inner_ref, lane_ref, out_ref, re_ref, im_ref, mid_ref
):
    count = own_ref.shape[0] // HALF
    points = count // 2
    upper = ids[0] == 1

    def load(row):
        own = own_ref[pl.ds(row, count, stride=HALF), :]
        other = other_ref[pl.ds(row, count, stride=HALF), :]
        return [jnp.where(upper, other, own), jnp.where(upper, own, other)]

    forward(load, points, mix_ref, twist_ref, inner_ref, re_ref, im_ref, mid_ref)
    step = max(1, 256 // points)
    for k in range(0, ROWS, step):
        values = mid_ref[k : k + step].reshape(step * points, 2 * LANES)
        out_ref[k * points : (k + step) * points, :] = lane_product(values, lane_ref)


def second_kernel(
    ids,
    near_ref,
    near_pair_ref,
    far_ref,
    far_pair_ref,
    spec_ref,
    mix_ref,
    back_ref,
    twist_ref,
    inner_ref,
    lane_ref,
    lane_back_ref,
    own_ref,
    other_ref,
    re_ref,
    im_ref,
    mid_ref,
):
    count = near_ref.shape[0] // QUART
    points = count // 2
    upper = ids[0] == 1
    second = ids[1] == 1

    def load(row):
        here = pl.ds(row % QUART, count, stride=QUART)
        swap = second if row < QUART else jnp.logical_not(second)
        near = jnp.where(swap, near_pair_ref[here, :], near_ref[here, :])
        far = jnp.where(swap, far_pair_ref[here, :], far_ref[here, :])
        return [jnp.where(upper, far, near), jnp.where(upper, near, far)]

    forward(load, points, mix_ref, twist_ref, inner_ref, re_ref, im_ref, mid_ref)
    step = max(1, 256 // points)
    for k in range(0, ROWS, step):
        values = mid_ref[k : k + step].reshape(step * points, 2 * LANES)
        values = lane_product(values, lane_ref)
        spec = spec_ref[k * points : (k + step) * points, :]
        re, im = times(
            values[:, :LANES], values[:, LANES:], spec[:, :LANES], -spec[:, LANES:]
        )
        values = lane_product(jnp.concatenate([re, im], axis=1), lane_back_ref)
        for j in range(step):
            rows = slice(j * points, (j + 1) * points)
            re, im = times(
                values[rows, :LANES],
                values[rows, LANES:],
                inner_ref[0, k + j : k + j + 1, :],
                -inner_ref[1, k + j : k + j + 1, :],
            )
            re_ref[k + j] = re
            im_ref[k + j] = im

    def finish(k, rows, re, im):
        re, im = times(re, im, twist_ref[0, 0, k, rows, :], -twist_ref[0, 1, k, rows, :])
        mid_ref[k, rows, :LANES] = re
        mid_ref[k, rows, LANES:] = im

    short_transform(re_ref, im_ref, points, 1.0, finish)
    for row in range(HALF):
        both = []
        for place in (row, row + HALF):
            both.append(
                jnp.concatenate([mid_ref[place, :, :LANES], mid_ref[place, :, LANES:]], axis=0)
            )
        high, low = split(jnp.concatenate(both, axis=1))
        full = dot(back_ref[0], jnp.concatenate([high, low], axis=0))
        full = full[:count] + full[count:]
        first_half, second_half = full[:, :LANES], full[:, LANES:]
        here = pl.ds(row, count, stride=HALF)
        own_ref[here, :] = jnp.where(upper, second_half, first_half)
        other_ref[here, :] = jnp.where(upper, first_half, second_half)


def finish_kernel(
    total, ids, back_ref, grad_ref, rates_ref, bias_ref, in_grad_ref, weighted_ref, rate_t, bias_t
):
    channels = grad_ref.shape[0]
    first = ids[3] * BLOCK
    own = pl.ds(pl.multiple_of(ids[2] * channels, 8), channels)
    rate_t[...] = spread_rows(ids, rates_ref[...])
    bias_t[...] = spread_rows(ids, bias_ref[...])
    rate_tile = rate_t[own, :]
    bias_tile = bias_t[own, :]
    per_group = weighted_ref.shape[2] // LANES
    for row in range(ROWS):
        here = slice(row * LANES, (row + 1) * LANES)
        conv = back_ref[pl.ds(row, channels, stride=4 * HALF), :]
        lag = back_ref[pl.ds(2 * HALF + row, channels, stride=4 * HALF), :]
        in_grad_ref[:, here] = conv + bias_tile * grad_ref[:, here]
        lanes = slice((row % per_group) * LANES, (row % per_group + 1) * LANES)
        weighted_ref[row // per_group, :, lanes] = lag * window_tile(rate_tile, first, row, total)


def project_kernel(weight_ref, values_ref, out_ref):
    rows = weight_ref.shape[0]
    high, low = split(weight_ref[...])
    both = jnp.concatenate([high, low], axis=0)
    wide = 2 * LANES
    for start in range(0, values_ref.shape[1], wide):
        value_high, value_low = split(values_ref[:, start : start + wide])
        full = dot(both, value_high)
        out_ref[:, start : start + wide] = full[:rows] + full[rows:] + dot(high, value_low)


def whole(array):
    return pl.BlockSpec(array.shape, lambda i, ids: (0,) * array.ndim)


def by_core(array):
    return pl.BlockSpec((1,) + array.shape[1:], lambda i, ids: (ids[0],) + (0,) * (array.ndim - 1))


def call(kernel, ids, operands, per_core, out_shapes, scratch):
    specs = [by_core(a) if flag else whole(a) for a, flag in zip(operands, per_core)]
    outs = [jax.ShapeDtypeStruct(shape, jnp.float32) for shape in out_shapes]
    out_specs = [whole(out) for out in outs]
    return pl.pallas_call(
        kernel,
        grid_spec=pltpu.PrefetchScalarGridSpec(
            num_scalar_prefetch=1,
            grid=(1,),
            in_specs=specs,
            out_specs=out_specs,
            scratch_shapes=[pltpu.VMEM(shape, jnp.float32) for shape in scratch],
        ),
        out_shape=outs,
        compiler_params=pltpu.CompilerParams(vmem_limit_bytes=VMEM_BYTES),
    )(ids, *operands)


def local(out_grad, gated_input, features, filter_weight, rates, skip_bias):
    channels = out_grad.shape[0]
    seq_count = lax.axis_size("seq")
    groups = lax.axis_size("ch")
    all_channels = channels * groups
    points = seq_count // 2
    total = seq_count * BLOCK
    place = lax.axis_index("seq")
    ids = jnp.stack([place % 2, (place // 2) % 2, lax.axis_index("ch"), place]).astype(jnp.int32)
    mix_in, mix_out, twist, inner, lane_in, lane_out = (
        jnp.asarray(table) for table in tables(seq_count)
    )
    swap_core = [(i, i ^ 1) for i in range(seq_count)]
    swap_chip = [(i, i ^ 2) for i in range(seq_count)]
    rates = rates.reshape(1, all_channels)
    skip_bias = skip_bias.reshape(1, all_channels)

    (packed,) = call(
        functools.partial(prepare_kernel, total),
        ids,
        (out_grad, gated_input, features, filter_weight, rates),
        (0, 0, 0, 0, 0),
        [(seq_count * CHUNK, LANES)],
        [(all_channels, features.shape[0]), (all_channels, LANES)],
    )
    packed = packed.reshape(seq_count, CHUNK, LANES)
    received = lax.all_to_all(packed, "seq", split_axis=0, concat_axis=0, tiled=True)
    near = received[:, HALF:]
    near_pair = lax.ppermute(near, "seq", swap_chip)
    own = received[:, :HALF]
    other = lax.ppermute(own, "seq", swap_core)
    far = lax.ppermute(near, "seq", swap_core)
    far_pair = lax.ppermute(near_pair, "seq", swap_core)

    def flat(array):
        return array.reshape(-1, LANES)

    work = [
        (ROWS, points, LANES),
        (ROWS, points, LANES),
        (ROWS, points, 2 * LANES),
    ]
    (spec,) = call(
        first_kernel,
        ids,
        (flat(own), flat(other), mix_in, twist, inner, lane_in),
        (0, 0, 1, 1, 0, 0),
        [(ROWS * points, 2 * LANES)],
        work,
    )
    kept, given = call(
        second_kernel,
        ids,
        (
            flat(near),
            flat(near_pair),
            flat(far),
            flat(far_pair),
            spec,
            mix_in,
            mix_out,
            twist,
            inner,
            lane_in,
            lane_out,
        ),
        (0, 0, 0, 0, 0, 1, 1, 1, 0, 0, 0),
        [(seq_count * HALF, LANES), (seq_count * HALF, LANES)],
        work,
    )
    result = kept + lax.ppermute(given, "seq", swap_core)
    result = result.reshape(seq_count, HALF, LANES)
    result = lax.all_to_all(result, "seq", split_axis=0, concat_axis=0, tiled=True)
    in_grad, weighted = call(
        functools.partial(finish_kernel, total),
        ids,
        (flat(result), out_grad, rates, skip_bias),
        (0, 0, 0, 0),
        [(channels, BLOCK), (groups, channels, BLOCK // groups)],
        [(all_channels, LANES), (all_channels, LANES)],
    )
    weighted = lax.all_to_all(weighted, "ch", split_axis=0, concat_axis=0, tiled=True)
    weighted = weighted.reshape(all_channels, BLOCK // groups)
    feat_grad = pl.pallas_call(
        project_kernel,
        out_shape=jax.ShapeDtypeStruct((filter_weight.shape[0], BLOCK // groups), jnp.float32),
        compiler_params=pltpu.CompilerParams(vmem_limit_bytes=VMEM_BYTES),
    )(filter_weight, weighted)
    return (in_grad, feat_grad)


def solution(mesh):
    in_specs = (P("ch", "seq"), P("ch", "seq"), P(None, "seq"), P(), P(), P())
    out_specs = (P("ch", "seq"), P(None, ("seq", "ch")))
    return jax.shard_map(local, mesh=mesh, in_specs=in_specs, out_specs=out_specs, check_vma=False)
```

```python
import functools
import math

import jax
import jax.numpy as jnp
import numpy as np
from jax import lax
from jax.experimental import pallas as pl
from jax.experimental.pallas import tpu as pltpu
from jax.sharding import PartitionSpec as P

SHIFT = 0.05
LANES = 128
ROWS = 32
BLOCK = ROWS * LANES
HALF = ROWS // 2
QUART = HALF // 2
CHUNK = HALF + QUART
VMEM_BYTES = 40 * 1024 * 1024
VMEM_MOST = 63 * 1024 * 1024


def as_pair(values):
    high = values.astype(jnp.bfloat16)
    return high, (values - high.astype(np.float32)).astype(jnp.bfloat16)


@functools.lru_cache(maxsize=None)
def tables(seq_count):
    points = seq_count // 2
    angle = 2.0 * np.pi
    mix_in, mix_out, twist = [], [], []
    dev = np.arange(seq_count)
    pos = np.arange(BLOCK)
    for half in range(2):
        freq = 4 * (2 * np.arange(points) + half) + 1
        step = angle * (np.outer(freq, dev) % (4 * seq_count)) / (4 * seq_count)
        forward = np.concatenate([np.cos(step), -np.sin(step)]).astype(np.float32)
        backward = forward.T / np.float32(seq_count * BLOCK)
        for out, matrix in ((mix_in, forward), (mix_out, backward)):
            high, low = as_pair(matrix)
            out.append(
                np.concatenate(
                    [
                        np.concatenate([high, high], axis=1),
                        np.concatenate([low, np.zeros_like(low)], axis=1),
                    ]
                )
            )
        turn = angle * (np.outer(freq, pos) / (4.0 * seq_count * BLOCK))
        turn = turn.reshape(points, ROWS, LANES).transpose(1, 0, 2)
        twist.append(np.stack([np.cos(turn), -np.sin(turn)]).astype(np.float32))
    inner = angle * np.outer(np.arange(ROWS), np.arange(LANES)) / BLOCK
    inner = np.stack([np.cos(inner), -np.sin(inner)]).astype(np.float32)
    lane = angle * (np.outer(np.arange(LANES), np.arange(LANES)) % LANES) / LANES
    cos, sin = np.cos(lane), np.sin(lane)
    lane_mat = np.block([[cos, -sin], [sin, cos]]).astype(np.float32)
    return (
        np.stack(mix_in),
        np.stack(mix_out),
        np.stack(twist),
        inner,
        np.stack(as_pair(lane_mat)),
        np.stack(as_pair(np.ascontiguousarray(lane_mat.T))),
    )


def dot(left, right):
    return jnp.dot(left, right, preferred_element_type=jnp.float32)


def split(values):
    high = values.astype(jnp.bfloat16)
    low = (values - high.astype(jnp.float32)).astype(jnp.bfloat16)
    return high, low


def times(a, b, re, im):
    return a * re - b * im, a * im + b * re


def scaled(a, b, number, sign):
    re, im = math.cos(number), sign * math.sin(number)
    if abs(im) < 1e-12 and re > 0:
        return a, b
    if abs(re) < 1e-12:
        return (-b, a) if im > 0 else (b, -a)
    return a * re - b * im, a * im + b * re


def four_points(vals, sign):
    (ar, ai), (br, bi), (cr, ci), (dr, di) = vals
    sr, si = ar + cr, ai + ci
    tr, ti = ar - cr, ai - ci
    ur, ui = br + dr, bi + di
    vr, vi = br - dr, bi - di
    if sign < 0:
        vr, vi = vi, -vr
    else:
        vr, vi = -vi, vr
    return [(sr + ur, si + ui), (tr + vr, ti + vi), (sr - ur, si - ui), (tr - vr, ti - vi)]


def eight_points(vals, sign):
    even = four_points(vals[0::2], sign)
    odd = four_points(vals[1::2], sign)
    low, high = [], []
    for index in range(4):
        er, ei = even[index]
        tr, ti = scaled(*odd[index], 2.0 * math.pi * index / 8, sign)
        low.append((er + tr, ei + ti))
        high.append((er - tr, ei - ti))
    return low + high


def short_transform(re_ref, im_ref, points, sign, finish):
    def tile(index, carry):
        rows = pl.ds(pl.multiple_of(index * 8, 8), 8)
        for second in range(8):
            vals = [(re_ref[8 * n + second, rows, :], im_ref[8 * n + second, rows, :]) for n in range(4)]
            vals = four_points(vals, sign)
            for k in range(4):
                re, im = scaled(*vals[k], 2.0 * math.pi * k * second / ROWS, sign)
                re_ref[8 * k + second, rows, :] = re
                im_ref[8 * k + second, rows, :] = im
        for k in range(4):
            vals = [(re_ref[8 * k + n, rows, :], im_ref[8 * k + n, rows, :]) for n in range(8)]
            vals = eight_points(vals, sign)
            for j in range(8):
                finish(k + 4 * j, rows, *vals[j])
        return carry

    lax.fori_loop(0, points // 8, tile, 0)


def forward(load, points, mix_ref, twist_ref, inner_ref, re_ref, im_ref, lane_in_ref):
    count = 2 * points
    for row in range(HALF):
        high, low = split(jnp.concatenate(load(row), axis=1))
        full = dot(mix_ref[0], jnp.concatenate([high, low], axis=0))
        full = full[:count] + full[count:]
        for part in range(2):
            place = row + part * HALF
            lanes = slice(part * LANES, (part + 1) * LANES)
            re, im = times(
                full[:points, lanes],
                full[points:, lanes],
                twist_ref[0, 0, place],
                twist_ref[0, 1, place],
            )
            re_ref[place] = re
            im_ref[place] = im

    def finish(k, rows, re, im):
        re, im = times(re, im, inner_ref[0, k : k + 1, :], inner_ref[1, k : k + 1, :])
        lane_in_ref[k, rows, :LANES] = re
        lane_in_ref[k, rows, LANES:] = im

    short_transform(re_ref, im_ref, points, -1.0, finish)


def lane_product(values, lane_ref):
    high, low = split(values)
    return dot(high, lane_ref[0]) + dot(low, lane_ref[0]) + dot(high, lane_ref[1])


def spread_rows(values):
    return jnp.broadcast_to(values, (LANES, values.shape[1])).T


def window_tile(rate_tile, first, row, total):
    lane = lax.broadcasted_iota(jnp.int32, rate_tile.shape, 1)
    place = (first + row * LANES + lane).astype(jnp.float32) * (1.0 / total)
    return jnp.exp(-rate_tile * place) + SHIFT


def prepare_kernel(
    total,
    ids,
    grad_hbm,
    input_hbm,
    feat_hbm,
    weight_hbm,
    rates_hbm,
    out_ref,
    weight_t,
    rate_t,
    grad_ref,
    input_ref,
    feat_ref,
    weight_ref,
    rates_ref,
    grad_sem,
    input_sem,
    feat_sem,
    weight_sem,
    rates_sem,
):
    weight_copy = pltpu.make_async_copy(weight_hbm, weight_ref, weight_sem)
    rates_copy = pltpu.make_async_copy(rates_hbm, rates_ref, rates_sem)
    feat_copy = pltpu.make_async_copy(feat_hbm, feat_ref, feat_sem)
    input_copy = pltpu.make_async_copy(input_hbm, input_ref, input_sem)
    grad_copy = pltpu.make_async_copy(grad_hbm, grad_ref, grad_sem)
    weight_copy.start()
    rates_copy.start()
    grad_copy.start()
    input_copy.start()
    feat_copy.start()
    channels = grad_ref.shape[0]
    first = ids[3] * BLOCK
    own = pl.ds(pl.multiple_of(ids[2] * channels, 8), channels)
    weight_copy.wait()
    rates_copy.wait()
    weight_t[...] = weight_ref[...].T
    rate_t[...] = spread_rows(rates_ref[...])
    high, low = split(weight_t[own, :])
    both = jnp.concatenate([high, low], axis=0)
    rate_tile = rate_t[own, :]
    wide = 2 * LANES
    grad_copy.wait()
    input_copy.wait()
    for row in range(ROWS):
        half, quart = row // HALF, (row // QUART) % 2
        here = slice(row * LANES, (row + 1) * LANES)
        base = 2 * CHUNK + half * CHUNK + row % HALF
        out_ref[pl.ds(base, channels, stride=4 * CHUNK), :] = input_ref[:, here]
        base = quart * 2 * CHUNK + half * CHUNK + HALF + row % QUART
        out_ref[pl.ds(base, channels, stride=4 * CHUNK), :] = grad_ref[:, here]
    feat_copy.wait()
    for pair in range(BLOCK // wide):
        lanes = slice(pair * wide, (pair + 1) * wide)
        feat_high, feat_low = split(feat_ref[:, lanes])
        full = dot(both, feat_high)
        full = full[:channels] + full[channels:] + dot(high, feat_low)
        for part in range(2):
            row = 2 * pair + part
            half = row // HALF
            filt = full[:, part * LANES : (part + 1) * LANES]
            filt = filt * window_tile(rate_tile, first, row, total)
            base = half * CHUNK + row % HALF
            out_ref[pl.ds(base, channels, stride=4 * CHUNK), :] = filt


def first_kernel(
    ids, own_ref, other_ref, mix_ref, twist_ref, inner_ref, lane_ref, out_ref, re_ref, im_ref, mid_ref
):
    count = own_ref.shape[0] // CHUNK
    points = count // 2
    upper = ids[0] == 1

    def load(row):
        own = own_ref[pl.ds(row, count, stride=CHUNK), :]
        other = other_ref[pl.ds(row, count, stride=CHUNK), :]
        return [jnp.where(upper, other, own), jnp.where(upper, own, other)]

    forward(load, points, mix_ref, twist_ref, inner_ref, re_ref, im_ref, mid_ref)
    step = max(1, 256 // points)
    for k in range(0, ROWS, step):
        values = mid_ref[k : k + step].reshape(step * points, 2 * LANES)
        out_ref[k * points : (k + step) * points, :] = lane_product(values, lane_ref)


def second_kernel(
    ids,
    near_ref,
    near_pair_ref,
    far_ref,
    far_pair_ref,
    spec_ref,
    mix_ref,
    back_ref,
    twist_ref,
    inner_ref,
    lane_ref,
    lane_back_ref,
    given_ref,
    mid_ref,
    re_ref,
    im_ref,
):
    count = near_ref.shape[0] // CHUNK
    points = count // 2
    upper = ids[0] == 1
    second = ids[1] == 1

    def load(row):
        here = pl.ds(HALF + row % QUART, count, stride=CHUNK)
        pair = pl.ds(row % QUART, count, stride=QUART)
        swap = second if row < QUART else jnp.logical_not(second)
        near = jnp.where(swap, near_pair_ref[pair, :], near_ref[here, :])
        far = jnp.where(swap, far_pair_ref[pair, :], far_ref[here, :])
        return [jnp.where(upper, far, near), jnp.where(upper, near, far)]

    forward(load, points, mix_ref, twist_ref, inner_ref, re_ref, im_ref, mid_ref)
    step = max(1, 256 // points)
    for k in range(0, ROWS, step):
        values = mid_ref[k : k + step].reshape(step * points, 2 * LANES)
        values = lane_product(values, lane_ref)
        spec = spec_ref[k * points : (k + step) * points, :]
        re, im = times(
            values[:, :LANES], values[:, LANES:], spec[:, :LANES], -spec[:, LANES:]
        )
        values = lane_product(jnp.concatenate([re, im], axis=1), lane_back_ref)
        for j in range(step):
            rows = slice(j * points, (j + 1) * points)
            re, im = times(
                values[rows, :LANES],
                values[rows, LANES:],
                inner_ref[0, k + j : k + j + 1, :],
                -inner_ref[1, k + j : k + j + 1, :],
            )
            re_ref[k + j] = re
            im_ref[k + j] = im

    def finish(k, rows, re, im):
        re, im = times(re, im, twist_ref[0, 0, k, rows, :], -twist_ref[0, 1, k, rows, :])
        mid_ref[k, rows, :LANES] = re
        mid_ref[k, rows, LANES:] = im

    short_transform(re_ref, im_ref, points, 1.0, finish)
    back_half(mid_ref, back_ref, given_ref, jnp.where(upper, 0, HALF))


def back_half(mid_ref, back_ref, out_ref, first):
    count = back_ref.shape[1] // 2
    for row in range(0, HALF, 2):
        both = []
        for place in (first + row, first + row + 1):
            values = mid_ref[place]
            both.append(jnp.concatenate([values[:, :LANES], values[:, LANES:]], axis=0))
        high, low = split(jnp.concatenate(both, axis=1))
        full = dot(back_ref[0], jnp.concatenate([high, low], axis=0))
        full = full[:count] + full[count:]
        for part in range(2):
            here = pl.ds(row + part, count, stride=HALF)
            out_ref[here, :] = full[:, part * LANES : (part + 1) * LANES]


def third_kernel(ids, mid_ref, back_ref, kept_ref):
    back_half(mid_ref, back_ref, kept_ref, jnp.where(ids[0] == 1, HALF, 0))


def finish_kernel(
    total, ids, back_ref, grad_ref, rates_ref, bias_ref, in_grad_ref, weighted_ref, rate_t, bias_t
):
    channels = grad_ref.shape[0]
    first = ids[3] * BLOCK
    own = pl.ds(pl.multiple_of(ids[2] * channels, 8), channels)
    rate_t[...] = spread_rows(rates_ref[...])
    bias_t[...] = spread_rows(bias_ref[...])
    rate_tile = rate_t[own, :]
    bias_tile = bias_t[own, :]
    per_group = weighted_ref.shape[2] // LANES
    for row in range(ROWS):
        here = slice(row * LANES, (row + 1) * LANES)
        conv = back_ref[pl.ds(row, channels, stride=4 * HALF), :]
        lag = back_ref[pl.ds(2 * HALF + row, channels, stride=4 * HALF), :]
        in_grad_ref[:, here] = conv + bias_tile * grad_ref[:, here]
        lanes = slice((row % per_group) * LANES, (row % per_group + 1) * LANES)
        weighted_ref[row // per_group, :, lanes] = lag * window_tile(rate_tile, first, row, total)


def project_kernel(weight_ref, values_ref, out_ref):
    rows = weight_ref.shape[0]
    high, low = split(weight_ref[...])
    both = jnp.concatenate([high, low], axis=0)
    wide = 2 * LANES
    for start in range(0, values_ref.shape[1], wide):
        value_high, value_low = split(values_ref[:, start : start + wide])
        full = dot(both, value_high)
        out_ref[:, start : start + wide] = full[:rows] + full[rows:] + dot(high, value_low)


def whole(array):
    return pl.BlockSpec(array.shape, lambda i, ids: (0,) * array.ndim)


def by_core(array):
    return pl.BlockSpec((1,) + array.shape[1:], lambda i, ids: (ids[0],) + (0,) * (array.ndim - 1))


def call(kernel, ids, operands, kinds, out_shapes, scratch, cost_us=0):
    make = (whole, by_core, lambda array: pl.BlockSpec(memory_space=pltpu.HBM))
    specs = [make[kind](array) for array, kind in zip(operands, kinds)]
    copied = [array.shape for array, kind in zip(operands, kinds) if kind == 2]
    outs = [jax.ShapeDtypeStruct(shape, jnp.float32) for shape in out_shapes]
    out_specs = [whole(out) for out in outs]
    return pl.pallas_call(
        kernel,
        grid_spec=pltpu.PrefetchScalarGridSpec(
            num_scalar_prefetch=1,
            grid=(1,),
            in_specs=specs,
            out_specs=out_specs,
            scratch_shapes=[pltpu.VMEM(shape, jnp.float32) for shape in scratch + copied]
            + [pltpu.SemaphoreType.DMA for _ in copied],
        ),
        out_shape=outs,
        cost_estimate=pl.CostEstimate(
            flops=cost_us * 500_000_000, bytes_accessed=cost_us * 2_000_000, transcendentals=0
        ),
        compiler_params=pltpu.CompilerParams(
            vmem_limit_bytes=VMEM_MOST if copied else VMEM_BYTES
        ),
    )(ids, *operands)


def local(out_grad, gated_input, features, filter_weight, rates, skip_bias):
    channels = out_grad.shape[0]
    seq_count = lax.axis_size("seq")
    groups = lax.axis_size("ch")
    all_channels = channels * groups
    points = seq_count // 2
    total = seq_count * BLOCK
    place = lax.axis_index("seq")
    ids = jnp.stack([place % 2, (place // 2) % 2, lax.axis_index("ch"), place]).astype(jnp.int32)
    mix_in, mix_out, twist, inner, lane_in, lane_out = (
        jnp.asarray(table) for table in tables(seq_count)
    )
    swap_core = [(i, i ^ 1) for i in range(seq_count)]
    swap_chip = [(i, i ^ 2) for i in range(seq_count)]
    rates = rates.reshape(1, all_channels)
    skip_bias = skip_bias.reshape(1, all_channels)

    (packed,) = call(
        functools.partial(prepare_kernel, total),
        ids,
        (out_grad, gated_input, features, filter_weight, rates),
        (2, 2, 2, 2, 2),
        [(seq_count * CHUNK, LANES)],
        [(all_channels, features.shape[0]), (all_channels, LANES)],
    )
    packed = packed.reshape(seq_count, CHUNK, LANES)
    received = lax.all_to_all(packed, "seq", split_axis=0, concat_axis=0, tiled=True)
    def flat(array):
        return array.reshape(-1, LANES)

    near = received[:, HALF:]
    near_pair = lax.ppermute(near, "seq", swap_chip)
    partner = lax.ppermute(received, "seq", swap_core)
    shape = (ROWS, points, LANES)
    wide = (ROWS, points, 2 * LANES)
    (spec,) = call(
        first_kernel,
        ids,
        (flat(received), flat(partner), mix_in, twist, inner, lane_in),
        (0, 0, 1, 1, 0, 0),
        [(ROWS * points, 2 * LANES)],
        [shape, shape, wide],
        cost_us=4,
    )
    near_pair, spec = lax.optimization_barrier((near_pair, spec))
    far_pair = lax.ppermute(near_pair, "seq", swap_core)
    given, mid = call(
        second_kernel,
        ids,
        (
            flat(received),
            flat(near_pair),
            flat(partner),
            flat(far_pair),
            spec,
            mix_in,
            mix_out,
            twist,
            inner,
            lane_in,
            lane_out,
        ),
        (0, 0, 0, 0, 0, 1, 1, 1, 0, 0, 0),
        [(seq_count * HALF, LANES), wide],
        [shape, shape],
        cost_us=6,
    )
    (kept,) = call(
        third_kernel,
        ids,
        (mid, mix_out),
        (0, 1),
        [(seq_count * HALF, LANES)],
        [],
        cost_us=2,
    )
    result = kept + lax.ppermute(given, "seq", swap_core)
    result = result.reshape(seq_count, HALF, LANES)
    result = lax.all_to_all(result, "seq", split_axis=0, concat_axis=0, tiled=True)
    in_grad, weighted = call(
        functools.partial(finish_kernel, total),
        ids,
        (flat(result), out_grad, rates, skip_bias),
        (0, 0, 0, 0),
        [(channels, BLOCK), (groups, channels, BLOCK // groups)],
        [(all_channels, LANES), (all_channels, LANES)],
    )
    weighted = lax.all_to_all(weighted, "ch", split_axis=0, concat_axis=0, tiled=True)
    weighted = weighted.reshape(all_channels, BLOCK // groups)
    feat_grad = pl.pallas_call(
        project_kernel,
        out_shape=jax.ShapeDtypeStruct((filter_weight.shape[0], BLOCK // groups), jnp.float32),
        compiler_params=pltpu.CompilerParams(vmem_limit_bytes=VMEM_BYTES),
    )(filter_weight, weighted)
    return (in_grad, feat_grad)


def solution(mesh):
    in_specs = (P("ch", "seq"), P("ch", "seq"), P(None, "seq"), P(), P(), P())
    out_specs = (P("ch", "seq"), P(None, ("seq", "ch")))
    return jax.shard_map(local, mesh=mesh, in_specs=in_specs, out_specs=out_specs, check_vma=False)
```

```python
import functools
import math

import jax
import jax.numpy as jnp
import numpy as np
from jax import lax
from jax.experimental import pallas as pl
from jax.experimental.pallas import tpu as pltpu
from jax.sharding import PartitionSpec as P

SHIFT = 0.05
LANES = 128
ROWS = 32
BLOCK = ROWS * LANES
HALF = ROWS // 2
QUART = HALF // 2
CHUNK = HALF + QUART
VMEM_BYTES = 40 * 1024 * 1024
VMEM_MOST = 63 * 1024 * 1024


@functools.lru_cache(maxsize=None)
def tables(seq_count):
    points = seq_count // 2
    circle = 2.0 * np.pi

    def waves(turns):
        return np.stack([np.cos(circle * turns), -np.sin(circle * turns)]).astype(np.float32)

    dev, lane, row = np.arange(seq_count), np.arange(LANES), np.arange(ROWS)
    across, by_lane, by_row = [], [], []
    for half in range(2):
        freq = 4 * (2 * np.arange(points) + half) + 1
        step = np.outer(freq, dev) % (4 * seq_count) / (4.0 * seq_count)
        across.append(np.concatenate(list(waves(step))))
        by_lane.append(waves(np.outer(freq, lane) / (4.0 * seq_count * BLOCK)))
        by_row.append(waves(np.outer(freq, row) / (4.0 * seq_count * ROWS)))
    inner = waves(np.outer(row, lane) / BLOCK)
    lanes = waves(np.outer(lane, lane) % LANES / LANES)
    return np.stack(across), np.stack(by_lane), np.stack(by_row), inner, lanes


def stack_pair(matrix, out_ref):
    rows, columns = matrix.shape
    high, low = split(matrix)
    out_ref[:rows, :columns] = high
    out_ref[:rows, columns:] = high
    out_ref[rows:, :columns] = low
    out_ref[rows:, columns:] = jnp.zeros_like(low)


def build_tables(
    across_ref, by_lane_ref, by_row_ref, lanes_ref, mix_ref, back_ref, twist_ref, lane_ref, lane_back_ref
):
    across = across_ref[0]
    stack_pair(across, mix_ref)
    stack_pair(across.T * (1.0 / (across.shape[0] * BLOCK)), back_ref)
    cos, sin = lanes_ref[0], lanes_ref[1]
    for part, (c, s, t) in enumerate(zip(split(cos), split(sin), split(-sin))):
        lane_ref[part, :LANES, :LANES] = c
        lane_ref[part, :LANES, LANES:] = s
        lane_ref[part, LANES:, :LANES] = t
        lane_ref[part, LANES:, LANES:] = c
        lane_back_ref[part, :LANES, :LANES] = c
        lane_back_ref[part, :LANES, LANES:] = t
        lane_back_ref[part, LANES:, :LANES] = s
        lane_back_ref[part, LANES:, LANES:] = c
    lane_re, lane_im = by_lane_ref[0, 0], by_lane_ref[0, 1]
    row_re, row_im = by_row_ref[0, 0], by_row_ref[0, 1]
    for row in range(ROWS):
        re, im = times(lane_re, lane_im, row_re[:, row : row + 1], row_im[:, row : row + 1])
        twist_ref[0, row] = re
        twist_ref[1, row] = im


def dot(left, right):
    return jnp.dot(left, right, preferred_element_type=jnp.float32)


def split(values):
    high = values.astype(jnp.bfloat16)
    low = (values - high.astype(jnp.float32)).astype(jnp.bfloat16)
    return high, low


def times(a, b, re, im):
    return a * re - b * im, a * im + b * re


def scaled(a, b, number, sign):
    re, im = math.cos(number), sign * math.sin(number)
    if abs(im) < 1e-12 and re > 0:
        return a, b
    if abs(re) < 1e-12:
        return (-b, a) if im > 0 else (b, -a)
    return a * re - b * im, a * im + b * re


def four_points(vals, sign):
    (ar, ai), (br, bi), (cr, ci), (dr, di) = vals
    sr, si = ar + cr, ai + ci
    tr, ti = ar - cr, ai - ci
    ur, ui = br + dr, bi + di
    vr, vi = br - dr, bi - di
    if sign < 0:
        vr, vi = vi, -vr
    else:
        vr, vi = -vi, vr
    return [(sr + ur, si + ui), (tr + vr, ti + vi), (sr - ur, si - ui), (tr - vr, ti - vi)]


def eight_points(vals, sign):
    even = four_points(vals[0::2], sign)
    odd = four_points(vals[1::2], sign)
    low, high = [], []
    for index in range(4):
        er, ei = even[index]
        tr, ti = scaled(*odd[index], 2.0 * math.pi * index / 8, sign)
        low.append((er + tr, ei + ti))
        high.append((er - tr, ei - ti))
    return low + high


def short_transform(re_ref, im_ref, points, sign, finish):
    def tile(index, carry):
        rows = pl.ds(pl.multiple_of(index * 8, 8), 8)
        for second in range(8):
            vals = [(re_ref[8 * n + second, rows, :], im_ref[8 * n + second, rows, :]) for n in range(4)]
            vals = four_points(vals, sign)
            for k in range(4):
                re, im = scaled(*vals[k], 2.0 * math.pi * k * second / ROWS, sign)
                re_ref[8 * k + second, rows, :] = re
                im_ref[8 * k + second, rows, :] = im
        for k in range(4):
            vals = [(re_ref[8 * k + n, rows, :], im_ref[8 * k + n, rows, :]) for n in range(8)]
            vals = eight_points(vals, sign)
            for j in range(8):
                finish(k + 4 * j, rows, *vals[j])
        return carry

    lax.fori_loop(0, points // 8, tile, 0)


def forward(load, points, mix_ref, twist_ref, inner_ref, re_ref, im_ref, lane_in_ref):
    count = 2 * points
    for row in range(HALF):
        high, low = split(jnp.concatenate(load(row), axis=1))
        full = dot(mix_ref[...], jnp.concatenate([high, low], axis=0))
        full = full[:count] + full[count:]
        for part in range(2):
            place = row + part * HALF
            lanes = slice(part * LANES, (part + 1) * LANES)
            re, im = times(
                full[:points, lanes],
                full[points:, lanes],
                twist_ref[0, place],
                twist_ref[1, place],
            )
            re_ref[place] = re
            im_ref[place] = im

    def finish(k, rows, re, im):
        re, im = times(re, im, inner_ref[0, k : k + 1, :], inner_ref[1, k : k + 1, :])
        lane_in_ref[k, rows, :LANES] = re
        lane_in_ref[k, rows, LANES:] = im

    short_transform(re_ref, im_ref, points, -1.0, finish)


def lane_product(values, lane_ref):
    high, low = split(values)
    return dot(high, lane_ref[0]) + dot(low, lane_ref[0]) + dot(high, lane_ref[1])


def spread_rows(values):
    return jnp.broadcast_to(values, (LANES, values.shape[1])).T


def window_tile(rate_tile, first, row, total):
    lane = lax.broadcasted_iota(jnp.int32, rate_tile.shape, 1)
    place = (first + row * LANES + lane).astype(jnp.float32) * (1.0 / total)
    return jnp.exp(-rate_tile * place) + SHIFT


def prepare_kernel(
    total,
    ids,
    grad_hbm,
    input_hbm,
    feat_hbm,
    weight_hbm,
    rates_hbm,
    out_ref,
    weight_t,
    rate_t,
    grad_ref,
    input_ref,
    feat_ref,
    weight_ref,
    rates_ref,
    grad_sem,
    input_sem,
    feat_sem,
    weight_sem,
    rates_sem,
):
    weight_copy = pltpu.make_async_copy(weight_hbm, weight_ref, weight_sem)
    rates_copy = pltpu.make_async_copy(rates_hbm, rates_ref, rates_sem)
    feat_copy = pltpu.make_async_copy(feat_hbm, feat_ref, feat_sem)
    input_copy = pltpu.make_async_copy(input_hbm, input_ref, input_sem)
    grad_copy = pltpu.make_async_copy(grad_hbm, grad_ref, grad_sem)
    weight_copy.start()
    rates_copy.start()
    grad_copy.start()
    input_copy.start()
    feat_copy.start()
    channels = grad_ref.shape[0]
    first = ids[3] * BLOCK
    own = pl.ds(pl.multiple_of(ids[2] * channels, 8), channels)
    weight_copy.wait()
    rates_copy.wait()
    weight_t[...] = weight_ref[...].T
    rate_t[...] = spread_rows(rates_ref[...])
    high, low = split(weight_t[own, :])
    both = jnp.concatenate([high, low], axis=0)
    rate_tile = rate_t[own, :]
    wide = 2 * LANES
    grad_copy.wait()
    input_copy.wait()
    for row in range(ROWS):
        half, quart = row // HALF, (row // QUART) % 2
        here = slice(row * LANES, (row + 1) * LANES)
        base = 2 * CHUNK + half * CHUNK + row % HALF
        out_ref[pl.ds(base, channels, stride=4 * CHUNK), :] = input_ref[:, here]
        base = quart * 2 * CHUNK + half * CHUNK + HALF + row % QUART
        out_ref[pl.ds(base, channels, stride=4 * CHUNK), :] = grad_ref[:, here]
    feat_copy.wait()
    for pair in range(BLOCK // wide):
        lanes = slice(pair * wide, (pair + 1) * wide)
        feat_high, feat_low = split(feat_ref[:, lanes])
        full = dot(both, feat_high)
        full = full[:channels] + full[channels:] + dot(high, feat_low)
        for part in range(2):
            row = 2 * pair + part
            half = row // HALF
            filt = full[:, part * LANES : (part + 1) * LANES]
            filt = filt * window_tile(rate_tile, first, row, total)
            base = half * CHUNK + row % HALF
            out_ref[pl.ds(base, channels, stride=4 * CHUNK), :] = filt


def first_kernel(
    ids,
    own_ref,
    other_ref,
    across_ref,
    by_lane_ref,
    by_row_ref,
    inner_ref,
    lanes_ref,
    out_ref,
    mix_ref,
    back_ref,
    twist_ref,
    lane_ref,
    lane_back_ref,
    re_ref,
    im_ref,
    mid_ref,
):
    build_tables(
        across_ref,
        by_lane_ref,
        by_row_ref,
        lanes_ref,
        mix_ref,
        back_ref,
        twist_ref,
        lane_ref,
        lane_back_ref,
    )
    count = own_ref.shape[0] // CHUNK
    points = count // 2
    upper = ids[0] == 1

    def load(row):
        own = own_ref[pl.ds(row, count, stride=CHUNK), :]
        other = other_ref[pl.ds(row, count, stride=CHUNK), :]
        return [jnp.where(upper, other, own), jnp.where(upper, own, other)]

    forward(load, points, mix_ref, twist_ref, inner_ref, re_ref, im_ref, mid_ref)
    step = max(1, 256 // points)
    for k in range(0, ROWS, step):
        values = mid_ref[k : k + step].reshape(step * points, 2 * LANES)
        out_ref[k * points : (k + step) * points, :] = lane_product(values, lane_ref)


def second_kernel(
    ids,
    near_ref,
    near_pair_ref,
    far_ref,
    far_pair_ref,
    spec_ref,
    mix_ref,
    back_ref,
    twist_ref,
    inner_ref,
    lane_ref,
    lane_back_ref,
    given_ref,
    mid_ref,
    re_ref,
    im_ref,
):
    count = near_ref.shape[0] // CHUNK
    points = count // 2
    upper = ids[0] == 1
    second = ids[1] == 1

    def load(row):
        here = pl.ds(HALF + row % QUART, count, stride=CHUNK)
        pair = pl.ds(row % QUART, count, stride=QUART)
        swap = second if row < QUART else jnp.logical_not(second)
        near = jnp.where(swap, near_pair_ref[pair, :], near_ref[here, :])
        far = jnp.where(swap, far_pair_ref[pair, :], far_ref[here, :])
        return [jnp.where(upper, far, near), jnp.where(upper, near, far)]

    forward(load, points, mix_ref, twist_ref, inner_ref, re_ref, im_ref, mid_ref)
    step = max(1, 256 // points)
    for k in range(0, ROWS, step):
        values = mid_ref[k : k + step].reshape(step * points, 2 * LANES)
        values = lane_product(values, lane_ref)
        spec = spec_ref[k * points : (k + step) * points, :]
        re, im = times(
            values[:, :LANES], values[:, LANES:], spec[:, :LANES], -spec[:, LANES:]
        )
        values = lane_product(jnp.concatenate([re, im], axis=1), lane_back_ref)
        for j in range(step):
            rows = slice(j * points, (j + 1) * points)
            re, im = times(
                values[rows, :LANES],
                values[rows, LANES:],
                inner_ref[0, k + j : k + j + 1, :],
                -inner_ref[1, k + j : k + j + 1, :],
            )
            re_ref[k + j] = re
            im_ref[k + j] = im

    def finish(k, rows, re, im):
        re, im = times(re, im, twist_ref[0, k, rows, :], -twist_ref[1, k, rows, :])
        mid_ref[k, rows, :LANES] = re
        mid_ref[k, rows, LANES:] = im

    short_transform(re_ref, im_ref, points, 1.0, finish)
    back_half(mid_ref, back_ref, given_ref, jnp.where(upper, 0, HALF))


def back_half(mid_ref, back_ref, out_ref, first):
    count = back_ref.shape[0] // 2
    for row in range(0, HALF, 2):
        both = []
        for place in (first + row, first + row + 1):
            values = mid_ref[place]
            both.append(jnp.concatenate([values[:, :LANES], values[:, LANES:]], axis=0))
        high, low = split(jnp.concatenate(both, axis=1))
        full = dot(back_ref[...], jnp.concatenate([high, low], axis=0))
        full = full[:count] + full[count:]
        for part in range(2):
            here = pl.ds(row + part, count, stride=HALF)
            out_ref[here, :] = full[:, part * LANES : (part + 1) * LANES]


def third_kernel(ids, mid_ref, back_ref, kept_ref):
    back_half(mid_ref, back_ref, kept_ref, jnp.where(ids[0] == 1, HALF, 0))


def finish_kernel(
    total, ids, back_ref, grad_ref, rates_ref, bias_ref, in_grad_ref, weighted_ref, rate_t, bias_t
):
    channels = grad_ref.shape[0]
    first = ids[3] * BLOCK
    own = pl.ds(pl.multiple_of(ids[2] * channels, 8), channels)
    rate_t[...] = spread_rows(rates_ref[...])
    bias_t[...] = spread_rows(bias_ref[...])
    rate_tile = rate_t[own, :]
    bias_tile = bias_t[own, :]
    per_group = weighted_ref.shape[2] // LANES
    for row in range(ROWS):
        here = slice(row * LANES, (row + 1) * LANES)
        conv = back_ref[pl.ds(row, channels, stride=4 * HALF), :]
        lag = back_ref[pl.ds(2 * HALF + row, channels, stride=4 * HALF), :]
        in_grad_ref[:, here] = conv + bias_tile * grad_ref[:, here]
        lanes = slice((row % per_group) * LANES, (row % per_group + 1) * LANES)
        weighted_ref[row // per_group, :, lanes] = lag * window_tile(rate_tile, first, row, total)


def project_kernel(weight_ref, values_ref, out_ref):
    rows = weight_ref.shape[0]
    high, low = split(weight_ref[...])
    both = jnp.concatenate([high, low], axis=0)
    wide = 2 * LANES
    for start in range(0, values_ref.shape[1], wide):
        value_high, value_low = split(values_ref[:, start : start + wide])
        full = dot(both, value_high)
        out_ref[:, start : start + wide] = full[:rows] + full[rows:] + dot(high, value_low)


def whole(array):
    return pl.BlockSpec(array.shape, lambda i, ids: (0,) * array.ndim)


def by_core(array):
    return pl.BlockSpec((1,) + array.shape[1:], lambda i, ids: (ids[0],) + (0,) * (array.ndim - 1))


def call(kernel, ids, operands, kinds, out_shapes, scratch, cost_us=0):
    make = (whole, by_core, lambda array: pl.BlockSpec(memory_space=pltpu.HBM))
    specs = [make[kind](array) for array, kind in zip(operands, kinds)]
    copied = [array.shape for array, kind in zip(operands, kinds) if kind == 2]
    outs = [
        jax.ShapeDtypeStruct(shape[1:], shape[0])
        if shape[0] == jnp.bfloat16
        else jax.ShapeDtypeStruct(shape, jnp.float32)
        for shape in out_shapes
    ]
    out_specs = [whole(out) for out in outs]
    return pl.pallas_call(
        kernel,
        grid_spec=pltpu.PrefetchScalarGridSpec(
            num_scalar_prefetch=1,
            grid=(1,),
            in_specs=specs,
            out_specs=out_specs,
            scratch_shapes=[pltpu.VMEM(shape, jnp.float32) for shape in scratch + copied]
            + [pltpu.SemaphoreType.DMA for _ in copied],
        ),
        out_shape=outs,
        cost_estimate=pl.CostEstimate(
            flops=cost_us * 500_000_000, bytes_accessed=cost_us * 2_000_000, transcendentals=0
        ),
        compiler_params=pltpu.CompilerParams(
            vmem_limit_bytes=VMEM_MOST if copied else VMEM_BYTES
        ),
    )(ids, *operands)


def local(out_grad, gated_input, features, filter_weight, rates, skip_bias):
    channels = out_grad.shape[0]
    seq_count = lax.axis_size("seq")
    groups = lax.axis_size("ch")
    all_channels = channels * groups
    points = seq_count // 2
    total = seq_count * BLOCK
    place = lax.axis_index("seq")
    ids = jnp.stack([place % 2, (place // 2) % 2, lax.axis_index("ch"), place]).astype(jnp.int32)
    across, by_lane, by_row, inner, lanes = (jnp.asarray(table) for table in tables(seq_count))
    swap_core = [(i, i ^ 1) for i in range(seq_count)]
    swap_chip = [(i, i ^ 2) for i in range(seq_count)]
    rates = rates.reshape(1, all_channels)
    skip_bias = skip_bias.reshape(1, all_channels)

    (packed,) = call(
        functools.partial(prepare_kernel, total),
        ids,
        (out_grad, gated_input, features, filter_weight, rates),
        (2, 2, 2, 2, 2),
        [(seq_count * CHUNK, LANES)],
        [(all_channels, features.shape[0]), (all_channels, LANES)],
    )
    packed = packed.reshape(seq_count, CHUNK, LANES)
    received = lax.all_to_all(packed, "seq", split_axis=0, concat_axis=0, tiled=True)
    def flat(array):
        return array.reshape(-1, LANES)

    received, near = lax.optimization_barrier((received, received[:, HALF:]))
    near_pair = lax.ppermute(near, "seq", swap_chip)
    partner = lax.ppermute(received, "seq", swap_core)
    shape = (ROWS, points, LANES)
    wide = (ROWS, points, 2 * LANES)
    half = jnp.bfloat16
    spec, mix_in, mix_out, twist, lane_in, lane_out = call(
        first_kernel,
        ids,
        (flat(received), flat(partner), across, by_lane, by_row, inner, lanes),
        (0, 0, 1, 1, 1, 0, 0),
        [
            (ROWS * points, 2 * LANES),
            (half, 2 * seq_count, 2 * seq_count),
            (half, 2 * seq_count, 2 * seq_count),
            (2, ROWS, points, LANES),
            (half, 2, 2 * LANES, 2 * LANES),
            (half, 2, 2 * LANES, 2 * LANES),
        ],
        [shape, shape, wide],
        cost_us=4,
    )
    near_pair, spec = lax.optimization_barrier((near_pair, spec))
    far_pair = lax.ppermute(near_pair, "seq", swap_core)
    given, mid = call(
        second_kernel,
        ids,
        (
            flat(received),
            flat(near_pair),
            flat(partner),
            flat(far_pair),
            spec,
            mix_in,
            mix_out,
            twist,
            inner,
            lane_in,
            lane_out,
        ),
        (0, 0, 0, 0, 0, 0, 0, 0, 0, 0, 0),
        [(seq_count * HALF, LANES), wide],
        [shape, shape],
        cost_us=6,
    )
    (kept,) = call(
        third_kernel,
        ids,
        (mid, mix_out),
        (0, 0),
        [(seq_count * HALF, LANES)],
        [],
        cost_us=2,
    )
    result = kept + lax.ppermute(given, "seq", swap_core)
    result = result.reshape(seq_count, HALF, LANES)
    result = lax.all_to_all(result, "seq", split_axis=0, concat_axis=0, tiled=True)
    in_grad, weighted = call(
        functools.partial(finish_kernel, total),
        ids,
        (flat(result), out_grad, rates, skip_bias),
        (0, 0, 0, 0),
        [(channels, BLOCK), (groups, channels, BLOCK // groups)],
        [(all_channels, LANES), (all_channels, LANES)],
    )
    weighted = lax.all_to_all(weighted, "ch", split_axis=0, concat_axis=0, tiled=True)
    weighted = weighted.reshape(all_channels, BLOCK // groups)
    feat_grad = pl.pallas_call(
        project_kernel,
        out_shape=jax.ShapeDtypeStruct((filter_weight.shape[0], BLOCK // groups), jnp.float32),
        compiler_params=pltpu.CompilerParams(vmem_limit_bytes=VMEM_BYTES),
    )(filter_weight, weighted)
    return (in_grad, feat_grad)


def solution(mesh):
    in_specs = (P("ch", "seq"), P("ch", "seq"), P(None, "seq"), P(), P(), P())
    out_specs = (P("ch", "seq"), P(None, ("seq", "ch")))
    return jax.shard_map(local, mesh=mesh, in_specs=in_specs, out_specs=out_specs, check_vma=False)
```

```python
import functools
import math

import jax
import jax.numpy as jnp
import numpy as np
from jax import lax
from jax.experimental import pallas as pl
from jax.experimental.pallas import tpu as pltpu
from jax.sharding import PartitionSpec as P

SHIFT = 0.05
LANES = 128
ROWS = 32
BLOCK = ROWS * LANES
HALF = ROWS // 2
QUART = HALF // 2
CHUNK = HALF + QUART
VMEM_BYTES = 40 * 1024 * 1024
VMEM_MOST = 63 * 1024 * 1024


@functools.lru_cache(maxsize=None)
def tables(seq_count):
    points = seq_count // 2
    circle = 2.0 * np.pi

    def waves(turns):
        return np.stack([np.cos(circle * turns), -np.sin(circle * turns)]).astype(np.float32)

    dev, lane, row = np.arange(seq_count), np.arange(LANES), np.arange(ROWS)
    across, by_lane, by_row = [], [], []
    for half in range(2):
        freq = 4 * (2 * np.arange(points) + half) + 1
        step = np.outer(freq, dev) % (4 * seq_count) / (4.0 * seq_count)
        across.append(np.concatenate(list(waves(step))))
        by_lane.append(waves(np.outer(freq, lane) / (4.0 * seq_count * BLOCK)))
        by_row.append(waves(np.outer(freq, row) / (4.0 * seq_count * ROWS)))
    inner = waves(np.outer(row, lane) / BLOCK)
    lanes = waves(np.outer(lane, lane) % LANES / LANES)
    return np.stack(across), np.stack(by_lane), np.stack(by_row), inner, lanes


def stack_pair(matrix, out_ref):
    rows, columns = matrix.shape
    high, low = split(matrix)
    out_ref[:rows, :columns] = high
    out_ref[:rows, columns:] = high
    out_ref[rows:, :columns] = low
    out_ref[rows:, columns:] = jnp.zeros_like(low)


def build_tables(
    across_ref, by_lane_ref, by_row_ref, lanes_ref, mix_ref, back_ref, twist_ref, lane_ref, lane_back_ref
):
    across = across_ref[0]
    stack_pair(across, mix_ref)
    stack_pair(across.T * (1.0 / (across.shape[0] * BLOCK)), back_ref)
    cos, sin = lanes_ref[0], lanes_ref[1]
    for part, (c, s, t) in enumerate(zip(split(cos), split(sin), split(-sin))):
        lane_ref[part, :LANES, :LANES] = c
        lane_ref[part, :LANES, LANES:] = s
        lane_ref[part, LANES:, :LANES] = t
        lane_ref[part, LANES:, LANES:] = c
        lane_back_ref[part, :LANES, :LANES] = c
        lane_back_ref[part, :LANES, LANES:] = t
        lane_back_ref[part, LANES:, :LANES] = s
        lane_back_ref[part, LANES:, LANES:] = c
    lane_re, lane_im = by_lane_ref[0, 0], by_lane_ref[0, 1]
    row_re, row_im = by_row_ref[0, 0], by_row_ref[0, 1]
    for row in range(ROWS):
        re, im = times(lane_re, lane_im, row_re[:, row : row + 1], row_im[:, row : row + 1])
        twist_ref[0, row] = re
        twist_ref[1, row] = im


def dot(left, right):
    return jnp.dot(left, right, preferred_element_type=jnp.float32)


def split(values):
    high = values.astype(jnp.bfloat16)
    low = (values - high.astype(jnp.float32)).astype(jnp.bfloat16)
    return high, low


def times(a, b, re, im):
    return a * re - b * im, a * im + b * re


def scaled(a, b, number, sign):
    re, im = math.cos(number), sign * math.sin(number)
    if abs(im) < 1e-12 and re > 0:
        return a, b
    if abs(re) < 1e-12:
        return (-b, a) if im > 0 else (b, -a)
    return a * re - b * im, a * im + b * re


def four_points(vals, sign):
    (ar, ai), (br, bi), (cr, ci), (dr, di) = vals
    sr, si = ar + cr, ai + ci
    tr, ti = ar - cr, ai - ci
    ur, ui = br + dr, bi + di
    vr, vi = br - dr, bi - di
    if sign < 0:
        vr, vi = vi, -vr
    else:
        vr, vi = -vi, vr
    return [(sr + ur, si + ui), (tr + vr, ti + vi), (sr - ur, si - ui), (tr - vr, ti - vi)]


def eight_points(vals, sign):
    even = four_points(vals[0::2], sign)
    odd = four_points(vals[1::2], sign)
    low, high = [], []
    for index in range(4):
        er, ei = even[index]
        tr, ti = scaled(*odd[index], 2.0 * math.pi * index / 8, sign)
        low.append((er + tr, ei + ti))
        high.append((er - tr, ei - ti))
    return low + high


def short_transform(re_ref, im_ref, points, sign, finish):
    def tile(index, carry):
        rows = pl.ds(pl.multiple_of(index * 8, 8), 8)
        for second in range(8):
            vals = [(re_ref[8 * n + second, rows, :], im_ref[8 * n + second, rows, :]) for n in range(4)]
            vals = four_points(vals, sign)
            for k in range(4):
                re, im = scaled(*vals[k], 2.0 * math.pi * k * second / ROWS, sign)
                re_ref[8 * k + second, rows, :] = re
                im_ref[8 * k + second, rows, :] = im
        for k in range(4):
            vals = [(re_ref[8 * k + n, rows, :], im_ref[8 * k + n, rows, :]) for n in range(8)]
            vals = eight_points(vals, sign)
            for j in range(8):
                finish(k + 4 * j, rows, *vals[j])
        return carry

    lax.fori_loop(0, points // 8, tile, 0)


def forward(load, points, mix_ref, twist_ref, inner_ref, re_ref, im_ref, lane_in_ref):
    count = 2 * points
    for row in range(HALF):
        high, low = split(jnp.concatenate(load(row), axis=1))
        full = dot(mix_ref[...], jnp.concatenate([high, low], axis=0))
        full = full[:count] + full[count:]
        for part in range(2):
            place = row + part * HALF
            lanes = slice(part * LANES, (part + 1) * LANES)
            re, im = times(
                full[:points, lanes],
                full[points:, lanes],
                twist_ref[0, place],
                twist_ref[1, place],
            )
            re_ref[place] = re
            im_ref[place] = im

    def finish(k, rows, re, im):
        re, im = times(re, im, inner_ref[0, k : k + 1, :], inner_ref[1, k : k + 1, :])
        lane_in_ref[k, rows, :LANES] = re
        lane_in_ref[k, rows, LANES:] = im

    short_transform(re_ref, im_ref, points, -1.0, finish)


def lane_product(values, lane_ref):
    high, low = split(values)
    return dot(high, lane_ref[0]) + dot(low, lane_ref[0]) + dot(high, lane_ref[1])


def spread_rows(values):
    return jnp.broadcast_to(values, (LANES, values.shape[1])).T


def window_tile(rate_tile, first, row, total):
    lane = lax.broadcasted_iota(jnp.int32, rate_tile.shape, 1)
    place = (first + row * LANES + lane).astype(jnp.float32) * (1.0 / total)
    return jnp.exp(-rate_tile * place) + SHIFT


def prepare_kernel(
    total,
    ids,
    grad_hbm,
    input_hbm,
    feat_hbm,
    weight_hbm,
    rates_hbm,
    out_hbm,
    grad_ref,
    input_ref,
    feat_ref,
    weight_ref,
    rates_ref,
    out_ref,
    filt_ref,
    weight_t,
    rate_t,
    small_sems,
    feat_sems,
    grad_sems,
    input_sems,
    out_sems,
):
    channels = grad_ref.shape[0]
    groups = channels // 8
    pieces = feat_sems.shape[0]
    span = BLOCK // pieces

    def copy(source, target, sems, index, *where):
        return pltpu.make_async_copy(source.at[where], target.at[where], sems.at[index])

    weight_copy = copy(weight_hbm, weight_ref, small_sems, 0)
    rates_copy = copy(rates_hbm, rates_ref, small_sems, 1)
    weight_copy.start()
    rates_copy.start()
    feat_copies = [
        copy(feat_hbm, feat_ref, feat_sems, k, slice(None), pl.ds(k * span, span))
        for k in range(pieces)
    ]
    for feat_copy in feat_copies:
        feat_copy.start()
    grad_copies = [copy(grad_hbm, grad_ref, grad_sems, g, pl.ds(g * 8, 8)) for g in range(groups)]
    input_copies = [
        copy(input_hbm, input_ref, input_sems, g, pl.ds(g * 8, 8)) for g in range(groups)
    ]
    for g in range(groups):
        input_copies[g].start()
        grad_copies[g].start()

    first = ids[3] * BLOCK
    start = pl.multiple_of(ids[2] * channels, 8)
    weight_copy.wait()
    rates_copy.wait()
    weight_t[...] = weight_ref[...].T
    rate_t[...] = spread_rows(rates_ref[...])
    high, low = split(weight_t[pl.ds(start, channels), :])
    both = jnp.concatenate([high, low], axis=0)
    wide = 2 * LANES
    for k in range(pieces):
        feat_copies[k].wait()
        for begin in range(k * span, (k + 1) * span, wide):
            feat_high, feat_low = split(feat_ref[:, begin : begin + wide])
            full = dot(both, feat_high)
            filt_ref[:, begin : begin + wide] = (
                full[:channels] + full[channels:] + dot(high, feat_low)
            )
    out_copies = []
    for g in range(groups):
        rows = slice(g * 8, g * 8 + 8)
        rate_tile = rate_t[pl.ds(start + g * 8, 8), :]
        input_copies[g].wait()
        grad_copies[g].wait()
        for row in range(ROWS):
            half, quart = row // HALF, (row // QUART) % 2
            here = slice(row * LANES, (row + 1) * LANES)
            base = g * 32 * CHUNK + half * CHUNK + row % HALF
            filt = filt_ref[rows, here] * window_tile(rate_tile, first, row, total)
            out_ref[pl.ds(base, 8, stride=4 * CHUNK), :] = filt
            base = g * 32 * CHUNK + (2 + half) * CHUNK + row % HALF
            out_ref[pl.ds(base, 8, stride=4 * CHUNK), :] = input_ref[rows, here]
            base = g * 32 * CHUNK + (2 * quart + half) * CHUNK + HALF + row % QUART
            out_ref[pl.ds(base, 8, stride=4 * CHUNK), :] = grad_ref[rows, here]
        done = copy(out_ref, out_hbm, out_sems, g, pl.ds(g * 32 * CHUNK, 32 * CHUNK))
        done.start()
        out_copies.append(done)
    for done in out_copies:
        done.wait()


def prepare(total, ids, operands, rows):
    channels, columns = operands[0].shape
    outer = pl.BlockSpec(memory_space=pltpu.HBM)
    weight_shape = operands[3].shape
    scratch = [operand.shape for operand in operands] + [
        (rows, LANES),
        (channels, columns),
        weight_shape[::-1],
        (weight_shape[1], LANES),
    ]
    return pl.pallas_call(
        functools.partial(prepare_kernel, total),
        grid_spec=pltpu.PrefetchScalarGridSpec(
            num_scalar_prefetch=1,
            grid=(1,),
            in_specs=[outer] * len(operands),
            out_specs=outer,
            scratch_shapes=[pltpu.VMEM(shape, jnp.float32) for shape in scratch]
            + [pltpu.SemaphoreType.DMA((n,)) for n in (2, 4, channels // 8, channels // 8, channels // 8)],
        ),
        out_shape=jax.ShapeDtypeStruct((rows, LANES), jnp.float32),
        compiler_params=pltpu.CompilerParams(vmem_limit_bytes=VMEM_MOST),
    )(ids, *operands)


def first_kernel(
    ids,
    halves_ref,
    across_ref,
    by_lane_ref,
    by_row_ref,
    inner_ref,
    lanes_ref,
    out_ref,
    mix_ref,
    back_ref,
    twist_ref,
    lane_ref,
    lane_back_ref,
    re_ref,
    im_ref,
    mid_ref,
):
    build_tables(
        across_ref,
        by_lane_ref,
        by_row_ref,
        lanes_ref,
        mix_ref,
        back_ref,
        twist_ref,
        lane_ref,
        lane_back_ref,
    )
    count = halves_ref.shape[0] // (2 * CHUNK)
    points = count // 2

    def load(row):
        return [
            halves_ref[pl.ds(half * count * CHUNK + row, count, stride=CHUNK), :]
            for half in range(2)
        ]

    forward(load, points, mix_ref, twist_ref, inner_ref, re_ref, im_ref, mid_ref)
    step = max(1, 256 // points)
    for k in range(0, ROWS, step):
        values = mid_ref[k : k + step].reshape(step * points, 2 * LANES)
        out_ref[k * points : (k + step) * points, :] = lane_product(values, lane_ref)


def second_kernel(
    ids,
    halves_ref,
    near_pair_ref,
    far_pair_ref,
    spec_ref,
    mix_ref,
    back_ref,
    twist_ref,
    inner_ref,
    lane_ref,
    lane_back_ref,
    given_ref,
    mid_ref,
    re_ref,
    im_ref,
):
    count = halves_ref.shape[0] // (2 * CHUNK)
    points = count // 2
    upper = ids[0] == 1
    second = ids[1] == 1

    def load(row):
        pair = pl.ds(row % QUART, count, stride=QUART)
        near, far = near_pair_ref[pair, :], far_pair_ref[pair, :]
        pairs = (jnp.where(upper, far, near), jnp.where(upper, near, far))
        swap = second if row < QUART else jnp.logical_not(second)
        tiles = []
        for half in range(2):
            start = half * count * CHUNK + HALF + row % QUART
            own = halves_ref[pl.ds(start, count, stride=CHUNK), :]
            tiles.append(jnp.where(swap, pairs[half], own))
        return tiles

    forward(load, points, mix_ref, twist_ref, inner_ref, re_ref, im_ref, mid_ref)
    step = max(1, 256 // points)
    for k in range(0, ROWS, step):
        values = mid_ref[k : k + step].reshape(step * points, 2 * LANES)
        values = lane_product(values, lane_ref)
        spec = spec_ref[k * points : (k + step) * points, :]
        re, im = times(
            values[:, :LANES], values[:, LANES:], spec[:, :LANES], -spec[:, LANES:]
        )
        values = lane_product(jnp.concatenate([re, im], axis=1), lane_back_ref)
        for j in range(step):
            rows = slice(j * points, (j + 1) * points)
            re, im = times(
                values[rows, :LANES],
                values[rows, LANES:],
                inner_ref[0, k + j : k + j + 1, :],
                -inner_ref[1, k + j : k + j + 1, :],
            )
            re_ref[k + j] = re
            im_ref[k + j] = im

    def finish(k, rows, re, im):
        re, im = times(re, im, twist_ref[0, k, rows, :], -twist_ref[1, k, rows, :])
        mid_ref[k, rows, :LANES] = re
        mid_ref[k, rows, LANES:] = im

    short_transform(re_ref, im_ref, points, 1.0, finish)
    back_half(mid_ref, back_ref, given_ref, jnp.where(upper, 0, HALF))


def back_half(mid_ref, back_ref, out_ref, first):
    count = back_ref.shape[0] // 2
    for row in range(0, HALF, 2):
        both = []
        for place in (first + row, first + row + 1):
            values = mid_ref[place]
            both.append(jnp.concatenate([values[:, :LANES], values[:, LANES:]], axis=0))
        high, low = split(jnp.concatenate(both, axis=1))
        full = dot(back_ref[...], jnp.concatenate([high, low], axis=0))
        full = full[:count] + full[count:]
        for part in range(2):
            here = pl.ds(row + part, count, stride=HALF)
            out_ref[here, :] = full[:, part * LANES : (part + 1) * LANES]


def third_kernel(ids, mid_ref, back_ref, kept_ref):
    back_half(mid_ref, back_ref, kept_ref, jnp.where(ids[0] == 1, HALF, 0))


def finish_kernel(
    total, ids, back_ref, grad_ref, rates_ref, bias_ref, in_grad_ref, weighted_ref, rate_t, bias_t
):
    channels = grad_ref.shape[0]
    first = ids[3] * BLOCK
    own = pl.ds(pl.multiple_of(ids[2] * channels, 8), channels)
    rate_t[...] = spread_rows(rates_ref[...])
    bias_t[...] = spread_rows(bias_ref[...])
    rate_tile = rate_t[own, :]
    bias_tile = bias_t[own, :]
    per_group = weighted_ref.shape[2] // LANES
    for row in range(ROWS):
        here = slice(row * LANES, (row + 1) * LANES)
        conv = back_ref[pl.ds(row, channels, stride=4 * HALF), :]
        lag = back_ref[pl.ds(2 * HALF + row, channels, stride=4 * HALF), :]
        in_grad_ref[:, here] = conv + bias_tile * grad_ref[:, here]
        lanes = slice((row % per_group) * LANES, (row % per_group + 1) * LANES)
        weighted_ref[row // per_group, :, lanes] = lag * window_tile(rate_tile, first, row, total)


def project_kernel(weight_ref, values_ref, out_ref):
    rows = weight_ref.shape[0]
    high, low = split(weight_ref[...])
    both = jnp.concatenate([high, low], axis=0)
    wide = 2 * LANES
    for start in range(0, values_ref.shape[1], wide):
        value_high, value_low = split(values_ref[:, start : start + wide])
        full = dot(both, value_high)
        out_ref[:, start : start + wide] = full[:rows] + full[rows:] + dot(high, value_low)


def whole(array):
    return pl.BlockSpec(array.shape, lambda i, ids: (0,) * array.ndim)


def by_core(array):
    return pl.BlockSpec((1,) + array.shape[1:], lambda i, ids: (ids[0],) + (0,) * (array.ndim - 1))


def call(kernel, ids, operands, kinds, out_shapes, scratch, cost_us=0):
    specs = [by_core(a) if kind else whole(a) for a, kind in zip(operands, kinds)]
    outs = [
        jax.ShapeDtypeStruct(shape[1:], shape[0])
        if shape[0] == jnp.bfloat16
        else jax.ShapeDtypeStruct(shape, jnp.float32)
        for shape in out_shapes
    ]
    out_specs = [whole(out) for out in outs]
    return pl.pallas_call(
        kernel,
        grid_spec=pltpu.PrefetchScalarGridSpec(
            num_scalar_prefetch=1,
            grid=(1,),
            in_specs=specs,
            out_specs=out_specs,
            scratch_shapes=[pltpu.VMEM(shape, jnp.float32) for shape in scratch],
        ),
        out_shape=outs,
        cost_estimate=pl.CostEstimate(
            flops=cost_us * 500_000_000, bytes_accessed=cost_us * 2_000_000, transcendentals=0
        ),
        compiler_params=pltpu.CompilerParams(vmem_limit_bytes=VMEM_BYTES),
    )(ids, *operands)


def local(out_grad, gated_input, features, filter_weight, rates, skip_bias):
    channels = out_grad.shape[0]
    seq_count = lax.axis_size("seq")
    groups = lax.axis_size("ch")
    all_channels = channels * groups
    points = seq_count // 2
    total = seq_count * BLOCK
    place = lax.axis_index("seq")
    ids = jnp.stack([place % 2, (place // 2) % 2, lax.axis_index("ch"), place]).astype(jnp.int32)
    across, by_lane, by_row, inner, lanes = (jnp.asarray(table) for table in tables(seq_count))
    swap_core = [(i, i ^ 1) for i in range(seq_count)]
    swap_chip = [(i, i ^ 2) for i in range(seq_count)]
    rates = rates.reshape(1, all_channels)
    skip_bias = skip_bias.reshape(1, all_channels)

    packed = prepare(
        total,
        ids,
        (out_grad, gated_input, features, filter_weight, rates),
        seq_count * CHUNK,
    )
    packed = packed.reshape(seq_count, CHUNK, LANES)
    received = lax.all_to_all(packed, "seq", split_axis=0, concat_axis=0, tiled=True)
    def flat(array):
        return array.reshape(-1, LANES)

    received, near = lax.optimization_barrier((received, received[:, HALF:]))
    near_pair = lax.ppermute(near, "seq", swap_chip)
    halves = lax.all_to_all(
        jnp.broadcast_to(received, (2,) + received.shape),
        "seq",
        split_axis=0,
        concat_axis=0,
        tiled=True,
        axis_index_groups=[[i, i + 1] for i in range(0, seq_count, 2)],
    )
    halves = flat(halves)
    shape = (ROWS, points, LANES)
    wide = (ROWS, points, 2 * LANES)
    half = jnp.bfloat16
    spec, mix_in, mix_out, twist, lane_in, lane_out = call(
        first_kernel,
        ids,
        (halves, across, by_lane, by_row, inner, lanes),
        (0, 1, 1, 1, 0, 0),
        [
            (ROWS * points, 2 * LANES),
            (half, 2 * seq_count, 2 * seq_count),
            (half, 2 * seq_count, 2 * seq_count),
            (2, ROWS, points, LANES),
            (half, 2, 2 * LANES, 2 * LANES),
            (half, 2, 2 * LANES, 2 * LANES),
        ],
        [shape, shape, wide],
        cost_us=4,
    )
    near_pair, spec = lax.optimization_barrier((near_pair, spec))
    far_pair = lax.ppermute(near_pair, "seq", swap_core)
    given, mid = call(
        second_kernel,
        ids,
        (
            halves,
            flat(near_pair),
            flat(far_pair),
            spec,
            mix_in,
            mix_out,
            twist,
            inner,
            lane_in,
            lane_out,
        ),
        (0,) * 10,
        [(seq_count * HALF, LANES), wide],
        [shape, shape],
        cost_us=6,
    )
    (kept,) = call(
        third_kernel,
        ids,
        (mid, mix_out),
        (0, 0),
        [(seq_count * HALF, LANES)],
        [],
        cost_us=2,
    )
    result = kept + lax.ppermute(given, "seq", swap_core)
    result = result.reshape(seq_count, HALF, LANES)
    result = lax.all_to_all(result, "seq", split_axis=0, concat_axis=0, tiled=True)
    in_grad, weighted = call(
        functools.partial(finish_kernel, total),
        ids,
        (flat(result), out_grad, rates, skip_bias),
        (0, 0, 0, 0),
        [(channels, BLOCK), (groups, channels, BLOCK // groups)],
        [(all_channels, LANES), (all_channels, LANES)],
    )
    weighted = lax.all_to_all(weighted, "ch", split_axis=0, concat_axis=0, tiled=True)
    weighted = weighted.reshape(all_channels, BLOCK // groups)
    feat_grad = pl.pallas_call(
        project_kernel,
        out_shape=jax.ShapeDtypeStruct((filter_weight.shape[0], BLOCK // groups), jnp.float32),
        compiler_params=pltpu.CompilerParams(vmem_limit_bytes=VMEM_BYTES),
    )(filter_weight, weighted)
    return (in_grad, feat_grad)


def solution(mesh):
    in_specs = (P("ch", "seq"), P("ch", "seq"), P(None, "seq"), P(), P(), P())
    out_specs = (P("ch", "seq"), P(None, ("seq", "ch")))
    return jax.shard_map(local, mesh=mesh, in_specs=in_specs, out_specs=out_specs, check_vma=False)
```

```python
import functools
import math

import jax
import jax.numpy as jnp
import numpy as np
from jax import lax
from jax.experimental import pallas as pl
from jax.experimental.pallas import tpu as pltpu
from jax.sharding import PartitionSpec as P

SHIFT = 0.05
LANES = 128
ROWS = 32
BLOCK = ROWS * LANES
HALF = ROWS // 2
QUART = HALF // 2
CHUNK = HALF + QUART
VMEM_BYTES = 40 * 1024 * 1024
VMEM_MOST = 63 * 1024 * 1024


@functools.lru_cache(maxsize=None)
def tables(seq_count):
    points = seq_count // 2
    circle = 2.0 * np.pi

    def waves(turns):
        return np.stack([np.cos(circle * turns), -np.sin(circle * turns)]).astype(np.float32)

    dev, lane, row = np.arange(seq_count), np.arange(LANES), np.arange(ROWS)
    across, by_lane, by_row = [], [], []
    for half in range(2):
        freq = 4 * (2 * np.arange(points) + half) + 1
        step = np.outer(freq, dev) % (4 * seq_count) / (4.0 * seq_count)
        across.append(np.concatenate(list(waves(step))))
        by_lane.append(waves(np.outer(freq, lane) / (4.0 * seq_count * BLOCK)))
        by_row.append(waves(np.outer(freq, row) / (4.0 * seq_count * ROWS)))
    inner = waves(np.outer(row, lane) / BLOCK)
    lanes = waves(np.outer(lane, lane) % LANES / LANES)
    return np.stack(across), np.stack(by_lane), np.stack(by_row), inner, lanes


def stack_pair(matrix, out_ref):
    rows, columns = matrix.shape
    high, low = split(matrix)
    out_ref[:rows, :columns] = high
    out_ref[:rows, columns:] = high
    out_ref[rows:, :columns] = low
    out_ref[rows:, columns:] = jnp.zeros_like(low)


def build_tables(
    across_ref, by_lane_ref, by_row_ref, lanes_ref, mix_ref, back_ref, twist_ref, lane_ref, lane_back_ref
):
    across = across_ref[0]
    stack_pair(across, mix_ref)
    stack_pair(across.T * (1.0 / (across.shape[0] * BLOCK)), back_ref)
    cos, sin = lanes_ref[0], lanes_ref[1]
    for part, (c, s, t) in enumerate(zip(split(cos), split(sin), split(-sin))):
        lane_ref[part, :LANES, :LANES] = c
        lane_ref[part, :LANES, LANES:] = s
        lane_ref[part, LANES:, :LANES] = t
        lane_ref[part, LANES:, LANES:] = c
        lane_back_ref[part, :LANES, :LANES] = c
        lane_back_ref[part, :LANES, LANES:] = t
        lane_back_ref[part, LANES:, :LANES] = s
        lane_back_ref[part, LANES:, LANES:] = c
    lane_re, lane_im = by_lane_ref[0, 0], by_lane_ref[0, 1]
    row_re, row_im = by_row_ref[0, 0], by_row_ref[0, 1]
    for row in range(ROWS):
        re, im = times(lane_re, lane_im, row_re[:, row : row + 1], row_im[:, row : row + 1])
        twist_ref[0, row] = re
        twist_ref[1, row] = im


def dot(left, right):
    return jnp.dot(left, right, preferred_element_type=jnp.float32)


def split(values):
    high = values.astype(jnp.bfloat16)
    low = (values - high.astype(jnp.float32)).astype(jnp.bfloat16)
    return high, low


def times(a, b, re, im):
    return a * re - b * im, a * im + b * re


def scaled(a, b, number, sign):
    re, im = math.cos(number), sign * math.sin(number)
    if abs(im) < 1e-12 and re > 0:
        return a, b
    if abs(re) < 1e-12:
        return (-b, a) if im > 0 else (b, -a)
    return a * re - b * im, a * im + b * re


def four_points(vals, sign):
    (ar, ai), (br, bi), (cr, ci), (dr, di) = vals
    sr, si = ar + cr, ai + ci
    tr, ti = ar - cr, ai - ci
    ur, ui = br + dr, bi + di
    vr, vi = br - dr, bi - di
    if sign < 0:
        vr, vi = vi, -vr
    else:
        vr, vi = -vi, vr
    return [(sr + ur, si + ui), (tr + vr, ti + vi), (sr - ur, si - ui), (tr - vr, ti - vi)]


def eight_points(vals, sign):
    even = four_points(vals[0::2], sign)
    odd = four_points(vals[1::2], sign)
    low, high = [], []
    for index in range(4):
        er, ei = even[index]
        tr, ti = scaled(*odd[index], 2.0 * math.pi * index / 8, sign)
        low.append((er + tr, ei + ti))
        high.append((er - tr, ei - ti))
    return low + high


def short_transform(re_ref, im_ref, points, sign, finish):
    def tile(index, carry):
        rows = pl.ds(pl.multiple_of(index * 8, 8), 8)
        for second in range(8):
            vals = [(re_ref[8 * n + second, rows, :], im_ref[8 * n + second, rows, :]) for n in range(4)]
            vals = four_points(vals, sign)
            for k in range(4):
                re, im = scaled(*vals[k], 2.0 * math.pi * k * second / ROWS, sign)
                re_ref[8 * k + second, rows, :] = re
                im_ref[8 * k + second, rows, :] = im
        for k in range(4):
            vals = [(re_ref[8 * k + n, rows, :], im_ref[8 * k + n, rows, :]) for n in range(8)]
            vals = eight_points(vals, sign)
            for j in range(8):
                finish(k + 4 * j, rows, *vals[j])
        return carry

    lax.fori_loop(0, points // 8, tile, 0)


def forward(load, points, mix_ref, twist_ref, inner_ref, re_ref, im_ref, lane_in_ref):
    count = 2 * points
    for row in range(HALF):
        high, low = split(jnp.concatenate(load(row), axis=1))
        full = dot(mix_ref[...], jnp.concatenate([high, low], axis=0))
        full = full[:count] + full[count:]
        for part in range(2):
            place = row + part * HALF
            lanes = slice(part * LANES, (part + 1) * LANES)
            re, im = times(
                full[:points, lanes],
                full[points:, lanes],
                twist_ref[0, place],
                twist_ref[1, place],
            )
            re_ref[place] = re
            im_ref[place] = im

    def finish(k, rows, re, im):
        re, im = times(re, im, inner_ref[0, k : k + 1, :], inner_ref[1, k : k + 1, :])
        lane_in_ref[k, rows, :LANES] = re
        lane_in_ref[k, rows, LANES:] = im

    short_transform(re_ref, im_ref, points, -1.0, finish)


def lane_product(values, lane_ref):
    high, low = split(values)
    return dot(high, lane_ref[0]) + dot(low, lane_ref[0]) + dot(high, lane_ref[1])


def spread_rows(values):
    return jnp.broadcast_to(values, (LANES, values.shape[1])).T


def window_tile(rate_tile, first, row, total):
    lane = lax.broadcasted_iota(jnp.int32, rate_tile.shape, 1)
    place = (first + row * LANES + lane).astype(jnp.float32) * (1.0 / total)
    return jnp.exp(-rate_tile * place) + SHIFT


def prepare_kernel(
    total,
    ids,
    grad_hbm,
    input_hbm,
    feat_hbm,
    weight_hbm,
    rates_hbm,
    out_hbm,
    grad_ref,
    input_ref,
    feat_ref,
    weight_ref,
    rates_ref,
    out_ref,
    weight_t,
    rate_t,
    small_sems,
    feat_sems,
    grad_sems,
    input_sems,
    out_sems,
):
    channels = grad_ref.shape[0]
    groups = channels // 8
    pieces = feat_sems.shape[0]
    span = BLOCK // pieces

    def copy(source, target, sems, index, *where):
        return pltpu.make_async_copy(source.at[where], target.at[where], sems.at[index])

    weight_copy = copy(weight_hbm, weight_ref, small_sems, 0)
    rates_copy = copy(rates_hbm, rates_ref, small_sems, 1)
    weight_copy.start()
    rates_copy.start()
    grad_copies = [copy(grad_hbm, grad_ref, grad_sems, g, pl.ds(g * 8, 8)) for g in range(groups)]
    input_copies = [
        copy(input_hbm, input_ref, input_sems, g, pl.ds(g * 8, 8)) for g in range(groups)
    ]
    for g in range(groups):
        input_copies[g].start()
        grad_copies[g].start()
    feat_copies = [
        copy(feat_hbm, feat_ref, feat_sems, k, slice(None), pl.ds(k * span, span))
        for k in range(pieces)
    ]
    for feat_copy in feat_copies:
        feat_copy.start()

    first = ids[3] * BLOCK
    start = pl.multiple_of(ids[2] * channels, 8)
    weight_copy.wait()
    rates_copy.wait()
    weight_t[...] = weight_ref[...].T
    rate_t[...] = spread_rows(rates_ref[...])
    high, low = split(weight_t[pl.ds(start, channels), :])
    both = jnp.concatenate([high, low], axis=0)
    rate_tile = rate_t[pl.ds(start, channels), :]
    wide = 2 * LANES
    out_copies = []

    def put(g, part, row, values):
        out_ref[part, g * 8 : g * 8 + 8, row, :] = values

    def send(g, part):
        place = g * 2 + part
        done = pltpu.make_async_copy(
            out_ref.at[part, pl.ds(g * 8, 8)], out_hbm.at[pl.ds(g * 8, 8), part], out_sems.at[place]
        )
        done.start()
        out_copies.append(done)

    for g in range(groups):
        rows = slice(g * 8, g * 8 + 8)
        input_copies[g].wait()
        grad_copies[g].wait()
        for row in range(ROWS):
            half, quart = row // HALF, (row // QUART) % 2
            here = slice(row * LANES, (row + 1) * LANES)
            put(g, 1, half * CHUNK + row % HALF, input_ref[rows, here])
            put(g, quart, half * CHUNK + HALF + row % QUART, grad_ref[rows, here])
        send(g, 1)
    for k in range(pieces):
        feat_copies[k].wait()
        for begin in range(k * span, (k + 1) * span, wide):
            feat_high, feat_low = split(feat_ref[:, begin : begin + wide])
            full = dot(both, feat_high)
            full = full[:channels] + full[channels:] + dot(high, feat_low)
            for part in range(2):
                row = begin // LANES + part
                filt = full[:, part * LANES : (part + 1) * LANES]
                filt = filt * window_tile(rate_tile, first, row, total)
                for g in range(groups):
                    put(g, 0, row // HALF * CHUNK + row % HALF, filt[g * 8 : g * 8 + 8])
    for g in range(groups):
        send(g, 0)
    for done in out_copies:
        done.wait()


def prepare(total, ids, operands):
    channels, columns = operands[0].shape
    outer = pl.BlockSpec(memory_space=pltpu.HBM)
    weight_shape = operands[3].shape
    scratch = [operand.shape for operand in operands] + [
        (2, channels, 2 * CHUNK, LANES),
        weight_shape[::-1],
        (weight_shape[1], LANES),
    ]
    return pl.pallas_call(
        functools.partial(prepare_kernel, total),
        grid_spec=pltpu.PrefetchScalarGridSpec(
            num_scalar_prefetch=1,
            grid=(1,),
            in_specs=[outer] * len(operands),
            out_specs=outer,
            scratch_shapes=[pltpu.VMEM(shape, jnp.float32) for shape in scratch]
            + [pltpu.SemaphoreType.DMA((n,)) for n in (2, 4, channels // 8, channels // 8, channels // 4)],
        ),
        out_shape=jax.ShapeDtypeStruct((channels, 2, 2 * CHUNK, LANES), jnp.float32),
        compiler_params=pltpu.CompilerParams(vmem_limit_bytes=VMEM_MOST),
    )(ids, *operands)


def first_kernel(
    ids,
    halves_ref,
    across_ref,
    by_lane_ref,
    by_row_ref,
    inner_ref,
    lanes_ref,
    out_ref,
    mix_ref,
    back_ref,
    twist_ref,
    lane_ref,
    lane_back_ref,
    re_ref,
    im_ref,
    mid_ref,
):
    build_tables(
        across_ref,
        by_lane_ref,
        by_row_ref,
        lanes_ref,
        mix_ref,
        back_ref,
        twist_ref,
        lane_ref,
        lane_back_ref,
    )
    count = halves_ref.shape[0] // (2 * CHUNK)
    points = count // 2

    def load(row):
        return [
            halves_ref[pl.ds(half * count * CHUNK + row, count, stride=CHUNK), :]
            for half in range(2)
        ]

    forward(load, points, mix_ref, twist_ref, inner_ref, re_ref, im_ref, mid_ref)
    step = max(1, 256 // points)
    for k in range(0, ROWS, step):
        values = mid_ref[k : k + step].reshape(step * points, 2 * LANES)
        out_ref[k * points : (k + step) * points, :] = lane_product(values, lane_ref)


def second_kernel(
    ids,
    halves_ref,
    near_pair_ref,
    far_pair_ref,
    spec_ref,
    mix_ref,
    back_ref,
    twist_ref,
    inner_ref,
    lane_ref,
    lane_back_ref,
    given_ref,
    mid_ref,
    re_ref,
    im_ref,
):
    count = halves_ref.shape[0] // (2 * CHUNK)
    points = count // 2
    upper = ids[0] == 1
    second = ids[1] == 1

    def load(row):
        pair = pl.ds(row % QUART, count, stride=QUART)
        near, far = near_pair_ref[pair, :], far_pair_ref[pair, :]
        pairs = (jnp.where(upper, far, near), jnp.where(upper, near, far))
        swap = second if row < QUART else jnp.logical_not(second)
        tiles = []
        for half in range(2):
            start = half * count * CHUNK + HALF + row % QUART
            own = halves_ref[pl.ds(start, count, stride=CHUNK), :]
            tiles.append(jnp.where(swap, pairs[half], own))
        return tiles

    forward(load, points, mix_ref, twist_ref, inner_ref, re_ref, im_ref, mid_ref)
    step = max(1, 256 // points)
    for k in range(0, ROWS, step):
        values = mid_ref[k : k + step].reshape(step * points, 2 * LANES)
        values = lane_product(values, lane_ref)
        spec = spec_ref[k * points : (k + step) * points, :]
        re, im = times(
            values[:, :LANES], values[:, LANES:], spec[:, :LANES], -spec[:, LANES:]
        )
        values = lane_product(jnp.concatenate([re, im], axis=1), lane_back_ref)
        for j in range(step):
            rows = slice(j * points, (j + 1) * points)
            re, im = times(
                values[rows, :LANES],
                values[rows, LANES:],
                inner_ref[0, k + j : k + j + 1, :],
                -inner_ref[1, k + j : k + j + 1, :],
            )
            re_ref[k + j] = re
            im_ref[k + j] = im

    def finish(k, rows, re, im):
        re, im = times(re, im, twist_ref[0, k, rows, :], -twist_ref[1, k, rows, :])
        mid_ref[k, rows, :LANES] = re
        mid_ref[k, rows, LANES:] = im

    short_transform(re_ref, im_ref, points, 1.0, finish)
    back_half(mid_ref, back_ref, given_ref, jnp.where(upper, 0, HALF))


def back_half(mid_ref, back_ref, out_ref, first):
    count = back_ref.shape[0] // 2
    for row in range(0, HALF, 2):
        both = []
        for place in (first + row, first + row + 1):
            values = mid_ref[place]
            both.append(jnp.concatenate([values[:, :LANES], values[:, LANES:]], axis=0))
        high, low = split(jnp.concatenate(both, axis=1))
        full = dot(back_ref[...], jnp.concatenate([high, low], axis=0))
        full = full[:count] + full[count:]
        for part in range(2):
            here = pl.ds(row + part, count, stride=HALF)
            out_ref[here, :] = full[:, part * LANES : (part + 1) * LANES]


def third_kernel(ids, mid_ref, back_ref, kept_ref):
    back_half(mid_ref, back_ref, kept_ref, jnp.where(ids[0] == 1, HALF, 0))


def finish_kernel(ids, back_ref, grad_ref, bias_ref, in_grad_ref, bias_t):
    channels = grad_ref.shape[0]
    own = pl.ds(pl.multiple_of(ids[2] * channels, 8), channels)
    bias_t[...] = spread_rows(bias_ref[...])
    bias_tile = bias_t[own, :]
    for row in range(ROWS):
        here = slice(row * LANES, (row + 1) * LANES)
        conv = back_ref[pl.ds(row, channels, stride=4 * HALF), :]
        in_grad_ref[:, here] = conv + bias_tile * grad_ref[:, here]


def project_kernel(total, ids, weight_ref, lag_ref, rates_ref, out_ref):
    rows, channels = weight_ref.shape
    per_group = lag_ref.shape[0] // channels
    first = ids[3] * BLOCK + ids[2] * (per_group * LANES)
    high, low = split(weight_ref[...])
    both = jnp.concatenate([high, low], axis=0)
    rate_tile = spread_rows(rates_ref[...])
    for row in range(0, per_group, 2):
        tiles = [
            lag_ref[pl.ds(row + part, channels, stride=per_group), :]
            * window_tile(rate_tile, first, row + part, total)
            for part in range(2)
        ]
        value_high, value_low = split(jnp.concatenate(tiles, axis=1))
        full = dot(both, value_high)
        full = full[:rows] + full[rows:] + dot(high, value_low)
        out_ref[:, row * LANES : (row + 2) * LANES] = full


def whole(array):
    return pl.BlockSpec(array.shape, lambda i, ids: (0,) * array.ndim)


def by_core(array):
    return pl.BlockSpec((1,) + array.shape[1:], lambda i, ids: (ids[0],) + (0,) * (array.ndim - 1))


def call(kernel, ids, operands, kinds, out_shapes, scratch, cost_us=0):
    specs = [by_core(a) if kind else whole(a) for a, kind in zip(operands, kinds)]
    outs = [
        jax.ShapeDtypeStruct(shape[1:], shape[0])
        if shape[0] == jnp.bfloat16
        else jax.ShapeDtypeStruct(shape, jnp.float32)
        for shape in out_shapes
    ]
    out_specs = [whole(out) for out in outs]
    return pl.pallas_call(
        kernel,
        grid_spec=pltpu.PrefetchScalarGridSpec(
            num_scalar_prefetch=1,
            grid=(1,),
            in_specs=specs,
            out_specs=out_specs,
            scratch_shapes=[pltpu.VMEM(shape, jnp.float32) for shape in scratch],
        ),
        out_shape=outs,
        cost_estimate=pl.CostEstimate(
            flops=cost_us * 500_000_000, bytes_accessed=cost_us * 2_000_000, transcendentals=0
        ),
        compiler_params=pltpu.CompilerParams(vmem_limit_bytes=VMEM_BYTES),
    )(ids, *operands)


def local(out_grad, gated_input, features, filter_weight, rates, skip_bias):
    channels = out_grad.shape[0]
    seq_count = lax.axis_size("seq")
    groups = lax.axis_size("ch")
    all_channels = channels * groups
    points = seq_count // 2
    total = seq_count * BLOCK
    place = lax.axis_index("seq")
    ids = jnp.stack([place % 2, (place // 2) % 2, lax.axis_index("ch"), place]).astype(jnp.int32)
    across, by_lane, by_row, inner, lanes = (jnp.asarray(table) for table in tables(seq_count))
    swap_core = [(i, i ^ 1) for i in range(seq_count)]
    swap_chip = [(i, i ^ 2) for i in range(seq_count)]
    rates = rates.reshape(1, all_channels)
    skip_bias = skip_bias.reshape(1, all_channels)

    packed = prepare(
        total,
        ids,
        (out_grad, gated_input, features, filter_weight, rates),
    )
    packed = packed.reshape(seq_count, CHUNK, LANES)
    received = lax.all_to_all(packed, "seq", split_axis=0, concat_axis=0, tiled=True)
    def flat(array):
        return array.reshape(-1, LANES)

    received, near = lax.optimization_barrier((received, received[:, HALF:]))
    near_pair = lax.ppermute(near, "seq", swap_chip)
    halves = lax.all_to_all(
        jnp.broadcast_to(received, (2,) + received.shape),
        "seq",
        split_axis=0,
        concat_axis=0,
        tiled=True,
        axis_index_groups=[[i, i + 1] for i in range(0, seq_count, 2)],
    )
    halves = flat(halves)
    shape = (ROWS, points, LANES)
    wide = (ROWS, points, 2 * LANES)
    half = jnp.bfloat16
    spec, mix_in, mix_out, twist, lane_in, lane_out = call(
        first_kernel,
        ids,
        (halves, across, by_lane, by_row, inner, lanes),
        (0, 1, 1, 1, 0, 0),
        [
            (ROWS * points, 2 * LANES),
            (half, 2 * seq_count, 2 * seq_count),
            (half, 2 * seq_count, 2 * seq_count),
            (2, ROWS, points, LANES),
            (half, 2, 2 * LANES, 2 * LANES),
            (half, 2, 2 * LANES, 2 * LANES),
        ],
        [shape, shape, wide],
        cost_us=4,
    )
    near_pair, spec = lax.optimization_barrier((near_pair, spec))
    far_pair = lax.ppermute(near_pair, "seq", swap_core)
    given, mid = call(
        second_kernel,
        ids,
        (
            halves,
            flat(near_pair),
            flat(far_pair),
            spec,
            mix_in,
            mix_out,
            twist,
            inner,
            lane_in,
            lane_out,
        ),
        (0,) * 10,
        [(seq_count * HALF, LANES), wide],
        [shape, shape],
        cost_us=6,
    )
    (kept,) = call(
        third_kernel,
        ids,
        (mid, mix_out),
        (0, 0),
        [(seq_count * HALF, LANES)],
        [],
        cost_us=2,
    )
    result = kept + lax.ppermute(given, "seq", swap_core)
    result = result.reshape(seq_count, HALF, LANES)
    result = lax.all_to_all(result, "seq", split_axis=0, concat_axis=0, tiled=True)
    per_group = ROWS // groups
    lag = result.reshape(channels, 2, groups, per_group, LANES)[:, 1].transpose(1, 0, 2, 3)
    lag = lax.all_to_all(lag, "ch", split_axis=0, concat_axis=0, tiled=True)
    (in_grad,) = call(
        finish_kernel,
        ids,
        (flat(result), out_grad, skip_bias),
        (0, 0, 0),
        [(channels, BLOCK)],
        [(all_channels, LANES)],
        cost_us=2,
    )
    (feat_grad,) = call(
        functools.partial(project_kernel, total),
        ids,
        (filter_weight, flat(lag), rates),
        (0, 0, 0),
        [(filter_weight.shape[0], BLOCK // groups)],
        [],
        cost_us=1,
    )
    return (in_grad, feat_grad)


def solution(mesh):
    in_specs = (P("ch", "seq"), P("ch", "seq"), P(None, "seq"), P(), P(), P())
    out_specs = (P("ch", "seq"), P(None, ("seq", "ch")))
    return jax.shard_map(local, mesh=mesh, in_specs=in_specs, out_specs=out_specs, check_vma=False)
```

```python
import functools
import math

import jax
import jax.numpy as jnp
import numpy as np
from jax import lax
from jax.experimental import pallas as pl
from jax.experimental.pallas import tpu as pltpu
from jax.sharding import PartitionSpec as P

SHIFT = 0.05
LANES = 128
ROWS = 32
BLOCK = ROWS * LANES
HALF = ROWS // 2
CHUNK = ROWS + HALF
VMEM_BYTES = 40 * 1024 * 1024
VMEM_MOST = 63 * 1024 * 1024


@functools.lru_cache(maxsize=None)
def tables(seq_count):
    points = seq_count // 2
    circle = 2.0 * np.pi

    def waves(turns):
        return np.stack([np.cos(circle * turns), -np.sin(circle * turns)]).astype(np.float32)

    dev = np.arange(seq_count).reshape(points, 2).T.reshape(-1)
    lane, row = np.arange(LANES), np.arange(ROWS)
    across, by_lane, by_row = [], [], []
    for half in range(2):
        freq = 4 * (2 * np.arange(points) + half) + 1
        step = np.outer(freq, dev) % (4 * seq_count) / (4.0 * seq_count)
        across.append(np.concatenate(list(waves(step))))
        by_lane.append(waves(np.outer(freq, lane) / (4.0 * seq_count * BLOCK)))
        by_row.append(waves(np.outer(freq, row) / (4.0 * seq_count * ROWS)))
    inner = waves(np.outer(row, lane) / BLOCK)
    lanes = waves(np.outer(lane, lane) % LANES / LANES)
    return np.stack(across), np.stack(by_lane), np.stack(by_row), inner, lanes


def stack_pair(matrix, out_ref):
    rows, columns = matrix.shape
    high, low = split(matrix)
    out_ref[:rows, :columns] = high
    out_ref[:rows, columns:] = high
    out_ref[rows:, :columns] = low
    out_ref[rows:, columns:] = jnp.zeros_like(low)


def build_tables(
    across_ref, by_lane_ref, by_row_ref, lanes_ref, mix_ref, back_ref, twist_ref, lane_ref, lane_back_ref
):
    across = across_ref[0]
    stack_pair(across, mix_ref)
    stack_pair(across.T * (1.0 / (across.shape[0] * BLOCK)), back_ref)
    cos, sin = lanes_ref[0], lanes_ref[1]
    for part, (c, s, t) in enumerate(zip(split(cos), split(sin), split(-sin))):
        lane_ref[part, :LANES, :LANES] = c
        lane_ref[part, :LANES, LANES:] = s
        lane_ref[part, LANES:, :LANES] = t
        lane_ref[part, LANES:, LANES:] = c
        lane_back_ref[part, :LANES, :LANES] = c
        lane_back_ref[part, :LANES, LANES:] = t
        lane_back_ref[part, LANES:, :LANES] = s
        lane_back_ref[part, LANES:, LANES:] = c
    lane_re, lane_im = by_lane_ref[0, 0], by_lane_ref[0, 1]
    row_re, row_im = by_row_ref[0, 0], by_row_ref[0, 1]
    for row in range(ROWS):
        re, im = times(lane_re, lane_im, row_re[:, row : row + 1], row_im[:, row : row + 1])
        twist_ref[0, row] = re
        twist_ref[1, row] = im


def dot(left, right):
    return jnp.dot(left, right, preferred_element_type=jnp.float32)


def split(values):
    high = values.astype(jnp.bfloat16)
    low = (values - high.astype(jnp.float32)).astype(jnp.bfloat16)
    return high, low


def times(a, b, re, im):
    return a * re - b * im, a * im + b * re


def scaled(a, b, number, sign):
    re, im = math.cos(number), sign * math.sin(number)
    if abs(im) < 1e-12 and re > 0:
        return a, b
    if abs(re) < 1e-12:
        return (-b, a) if im > 0 else (b, -a)
    return a * re - b * im, a * im + b * re


def four_points(vals, sign):
    (ar, ai), (br, bi), (cr, ci), (dr, di) = vals
    sr, si = ar + cr, ai + ci
    tr, ti = ar - cr, ai - ci
    ur, ui = br + dr, bi + di
    vr, vi = br - dr, bi - di
    if sign < 0:
        vr, vi = vi, -vr
    else:
        vr, vi = -vi, vr
    return [(sr + ur, si + ui), (tr + vr, ti + vi), (sr - ur, si - ui), (tr - vr, ti - vi)]


def eight_points(vals, sign):
    even = four_points(vals[0::2], sign)
    odd = four_points(vals[1::2], sign)
    low, high = [], []
    for index in range(4):
        er, ei = even[index]
        tr, ti = scaled(*odd[index], 2.0 * math.pi * index / 8, sign)
        low.append((er + tr, ei + ti))
        high.append((er - tr, ei - ti))
    return low + high


def short_transform(re_ref, im_ref, points, sign, finish):
    def tile(index, carry):
        rows = pl.ds(pl.multiple_of(index * 8, 8), 8)
        for second in range(8):
            vals = [(re_ref[8 * n + second, rows, :], im_ref[8 * n + second, rows, :]) for n in range(4)]
            vals = four_points(vals, sign)
            for k in range(4):
                re, im = scaled(*vals[k], 2.0 * math.pi * k * second / ROWS, sign)
                re_ref[8 * k + second, rows, :] = re
                im_ref[8 * k + second, rows, :] = im
        for k in range(4):
            vals = [(re_ref[8 * k + n, rows, :], im_ref[8 * k + n, rows, :]) for n in range(8)]
            vals = eight_points(vals, sign)
            for j in range(8):
                finish(k + 4 * j, rows, *vals[j])
        return carry

    lax.fori_loop(0, points // 8, tile, 0)


def forward(load, points, mix_ref, twist_ref, inner_ref, re_ref, im_ref, lane_in_ref):
    count = 2 * points
    for row in range(HALF):
        high, low = split(jnp.concatenate(load(row), axis=1))
        full = dot(mix_ref[...], jnp.concatenate([high, low], axis=0))
        full = full[:count] + full[count:]
        for part in range(2):
            place = row + part * HALF
            lanes = slice(part * LANES, (part + 1) * LANES)
            re, im = times(
                full[:points, lanes],
                full[points:, lanes],
                twist_ref[0, place],
                twist_ref[1, place],
            )
            re_ref[place] = re
            im_ref[place] = im

    def finish(k, rows, re, im):
        re, im = times(re, im, inner_ref[0, k : k + 1, :], inner_ref[1, k : k + 1, :])
        lane_in_ref[k, rows, :LANES] = re
        lane_in_ref[k, rows, LANES:] = im

    short_transform(re_ref, im_ref, points, -1.0, finish)


def lane_product(values, lane_ref):
    high, low = split(values)
    return dot(high, lane_ref[0]) + dot(low, lane_ref[0]) + dot(high, lane_ref[1])


def spread_rows(values):
    return jnp.broadcast_to(values, (LANES, values.shape[1])).T


def window_tile(rate_tile, first, row, total):
    lane = lax.broadcasted_iota(jnp.int32, rate_tile.shape, 1)
    place = (first + row * LANES + lane).astype(jnp.float32) * (1.0 / total)
    return jnp.exp(-rate_tile * place) + SHIFT


def prepare_kernel(
    total,
    ids,
    grad_hbm,
    input_hbm,
    feat_hbm,
    weight_hbm,
    rates_hbm,
    out_hbm,
    grad_ref,
    input_ref,
    feat_ref,
    weight_ref,
    rates_ref,
    out_ref,
    weight_t,
    rate_t,
    small_sems,
    feat_sems,
    grad_sems,
    input_sems,
    out_sems,
):
    channels = grad_ref.shape[0]
    groups = channels // 8
    pieces = feat_sems.shape[0]
    span = BLOCK // pieces

    def copy(source, target, sems, index, *where):
        return pltpu.make_async_copy(source.at[where], target.at[where], sems.at[index])

    weight_copy = copy(weight_hbm, weight_ref, small_sems, 0)
    rates_copy = copy(rates_hbm, rates_ref, small_sems, 1)
    weight_copy.start()
    rates_copy.start()
    grad_copies = [copy(grad_hbm, grad_ref, grad_sems, g, pl.ds(g * 8, 8)) for g in range(groups)]
    input_copies = [
        copy(input_hbm, input_ref, input_sems, g, pl.ds(g * 8, 8)) for g in range(groups)
    ]
    for g in range(groups):
        input_copies[g].start()
        grad_copies[g].start()
    feat_copies = [
        copy(feat_hbm, feat_ref, feat_sems, k, slice(None), pl.ds(k * span, span))
        for k in range(pieces)
    ]
    for feat_copy in feat_copies:
        feat_copy.start()

    first = ids[3] * BLOCK
    start = pl.multiple_of(ids[2] * channels, 8)
    weight_copy.wait()
    rates_copy.wait()
    weight_t[...] = weight_ref[...].T
    rate_t[...] = spread_rows(rates_ref[...])
    high, low = split(weight_t[pl.ds(start, channels), :])
    both = jnp.concatenate([high, low], axis=0)
    rate_tile = rate_t[pl.ds(start, channels), :]
    wide = 2 * LANES
    out_copies = []

    def put(g, part, row, values):
        out_ref[part, g * 8 : g * 8 + 8, row, :] = values

    def send(g, part):
        place = g * 2 + part
        done = pltpu.make_async_copy(
            out_ref.at[part, pl.ds(g * 8, 8)], out_hbm.at[pl.ds(g * 8, 8), part], out_sems.at[place]
        )
        done.start()
        out_copies.append(done)

    for g in range(groups):
        rows = slice(g * 8, g * 8 + 8)
        input_copies[g].wait()
        grad_copies[g].wait()
        for row in range(ROWS):
            here = slice(row * LANES, (row + 1) * LANES)
            put(g, 1, row, input_ref[rows, here])
            put(g, row // HALF, ROWS + row % HALF, grad_ref[rows, here])
        send(g, 1)
    for k in range(pieces):
        feat_copies[k].wait()
        for begin in range(k * span, (k + 1) * span, wide):
            feat_high, feat_low = split(feat_ref[:, begin : begin + wide])
            full = dot(both, feat_high)
            full = full[:channels] + full[channels:] + dot(high, feat_low)
            for part in range(2):
                row = begin // LANES + part
                filt = full[:, part * LANES : (part + 1) * LANES]
                filt = filt * window_tile(rate_tile, first, row, total)
                for g in range(groups):
                    put(g, 0, row, filt[g * 8 : g * 8 + 8])
    for g in range(groups):
        send(g, 0)
    for done in out_copies:
        done.wait()


def prepare(total, ids, operands):
    channels, columns = operands[0].shape
    outer = pl.BlockSpec(memory_space=pltpu.HBM)
    weight_shape = operands[3].shape
    scratch = [operand.shape for operand in operands] + [
        (2, channels, CHUNK, LANES),
        weight_shape[::-1],
        (weight_shape[1], LANES),
    ]
    return pl.pallas_call(
        functools.partial(prepare_kernel, total),
        grid_spec=pltpu.PrefetchScalarGridSpec(
            num_scalar_prefetch=1,
            grid=(1,),
            in_specs=[outer] * len(operands),
            out_specs=outer,
            scratch_shapes=[pltpu.VMEM(shape, jnp.float32) for shape in scratch]
            + [pltpu.SemaphoreType.DMA((n,)) for n in (2, 4, channels // 8, channels // 8, channels // 4)],
        ),
        out_shape=jax.ShapeDtypeStruct((channels, 2, CHUNK, LANES), jnp.float32),
        compiler_params=pltpu.CompilerParams(vmem_limit_bytes=VMEM_MOST),
    )(ids, *operands)


def first_kernel(
    ids,
    halves_ref,
    across_ref,
    by_lane_ref,
    by_row_ref,
    inner_ref,
    lanes_ref,
    out_ref,
    mix_ref,
    back_ref,
    twist_ref,
    lane_ref,
    lane_back_ref,
    re_ref,
    im_ref,
    mid_ref,
):
    build_tables(
        across_ref,
        by_lane_ref,
        by_row_ref,
        lanes_ref,
        mix_ref,
        back_ref,
        twist_ref,
        lane_ref,
        lane_back_ref,
    )
    count = halves_ref.shape[0] // CHUNK
    points = count // 2

    def load(row):
        return [
            halves_ref[pl.ds(place, count, stride=CHUNK), :] for place in (row, row + HALF)
        ]

    forward(load, points, mix_ref, twist_ref, inner_ref, re_ref, im_ref, mid_ref)
    step = max(1, 256 // points)
    for k in range(0, ROWS, step):
        values = mid_ref[k : k + step].reshape(step * points, 2 * LANES)
        out_ref[k * points : (k + step) * points, :] = lane_product(values, lane_ref)


def second_kernel(
    ids,
    halves_ref,
    near_pair_ref,
    far_pair_ref,
    spec_ref,
    mix_ref,
    back_ref,
    twist_ref,
    inner_ref,
    lane_ref,
    lane_back_ref,
    given_ref,
    mid_ref,
    re_ref,
    im_ref,
):
    count = halves_ref.shape[0] // CHUNK
    points = count // 2
    upper = ids[0] == 1
    second = ids[1] == 1

    def load(row):
        here = pl.ds(row, points, stride=HALF)
        near, far = near_pair_ref[here, :], far_pair_ref[here, :]
        pair = jnp.concatenate(
            [jnp.where(upper, far, near), jnp.where(upper, near, far)], axis=0
        )
        own = halves_ref[pl.ds(ROWS + row, count, stride=CHUNK), :]
        return [jnp.where(second, pair, own), jnp.where(second, own, pair)]

    forward(load, points, mix_ref, twist_ref, inner_ref, re_ref, im_ref, mid_ref)
    step = max(1, 256 // points)
    for k in range(0, ROWS, step):
        values = mid_ref[k : k + step].reshape(step * points, 2 * LANES)
        values = lane_product(values, lane_ref)
        spec = spec_ref[k * points : (k + step) * points, :]
        re, im = times(
            values[:, :LANES], values[:, LANES:], spec[:, :LANES], -spec[:, LANES:]
        )
        values = lane_product(jnp.concatenate([re, im], axis=1), lane_back_ref)
        for j in range(step):
            rows = slice(j * points, (j + 1) * points)
            re, im = times(
                values[rows, :LANES],
                values[rows, LANES:],
                inner_ref[0, k + j : k + j + 1, :],
                -inner_ref[1, k + j : k + j + 1, :],
            )
            re_ref[k + j] = re
            im_ref[k + j] = im

    def finish(k, rows, re, im):
        re, im = times(re, im, twist_ref[0, k, rows, :], -twist_ref[1, k, rows, :])
        mid_ref[k, rows, :LANES] = re
        mid_ref[k, rows, LANES:] = im

    short_transform(re_ref, im_ref, points, 1.0, finish)
    back_half(mid_ref, back_ref, given_ref, 1 - ids[0])


def back_half(mid_ref, back_ref, out_ref, core):
    count = back_ref.shape[0] // 2
    points = count // 2
    start = pl.multiple_of(core * points, points)
    matrix = jnp.concatenate(
        [back_ref[pl.ds(start, points), :], back_ref[pl.ds(count + start, points), :]], axis=0
    )
    for row in range(0, ROWS, 2):
        both = []
        for place in (row, row + 1):
            values = mid_ref[place]
            both.append(jnp.concatenate([values[:, :LANES], values[:, LANES:]], axis=0))
        high, low = split(jnp.concatenate(both, axis=1))
        full = dot(matrix, jnp.concatenate([high, low], axis=0))
        full = full[:points] + full[points:]
        for part in range(2):
            here = pl.ds(row + part, points, stride=ROWS)
            out_ref[here, :] = full[:, part * LANES : (part + 1) * LANES]


def third_kernel(ids, mid_ref, back_ref, kept_ref):
    back_half(mid_ref, back_ref, kept_ref, ids[0])


def finish_kernel(ids, back_ref, grad_ref, bias_ref, in_grad_ref, bias_t):
    channels = grad_ref.shape[0]
    own = pl.ds(pl.multiple_of(ids[2] * channels, 8), channels)
    bias_t[...] = spread_rows(bias_ref[...])
    bias_tile = bias_t[own, :]
    for row in range(ROWS):
        here = slice(row * LANES, (row + 1) * LANES)
        conv = back_ref[pl.ds(row, channels, stride=4 * HALF), :]
        in_grad_ref[:, here] = conv + bias_tile * grad_ref[:, here]


def project_kernel(total, ids, weight_ref, lag_ref, rates_ref, out_ref):
    rows, channels = weight_ref.shape
    per_group = lag_ref.shape[0] // channels
    first = ids[3] * BLOCK + ids[2] * (per_group * LANES)
    high, low = split(weight_ref[...])
    both = jnp.concatenate([high, low], axis=0)
    rate_tile = spread_rows(rates_ref[...])
    for row in range(0, per_group, 2):
        tiles = [
            lag_ref[pl.ds(row + part, channels, stride=per_group), :]
            * window_tile(rate_tile, first, row + part, total)
            for part in range(2)
        ]
        value_high, value_low = split(jnp.concatenate(tiles, axis=1))
        full = dot(both, value_high)
        full = full[:rows] + full[rows:] + dot(high, value_low)
        out_ref[:, row * LANES : (row + 2) * LANES] = full


def whole(array):
    return pl.BlockSpec(array.shape, lambda i, ids: (0,) * array.ndim)


def by_core(array):
    return pl.BlockSpec((1,) + array.shape[1:], lambda i, ids: (ids[0],) + (0,) * (array.ndim - 1))


def call(kernel, ids, operands, kinds, out_shapes, scratch, cost_us=0):
    specs = [by_core(a) if kind else whole(a) for a, kind in zip(operands, kinds)]
    outs = [
        jax.ShapeDtypeStruct(shape[1:], shape[0])
        if shape[0] == jnp.bfloat16
        else jax.ShapeDtypeStruct(shape, jnp.float32)
        for shape in out_shapes
    ]
    out_specs = [whole(out) for out in outs]
    return pl.pallas_call(
        kernel,
        grid_spec=pltpu.PrefetchScalarGridSpec(
            num_scalar_prefetch=1,
            grid=(1,),
            in_specs=specs,
            out_specs=out_specs,
            scratch_shapes=[pltpu.VMEM(shape, jnp.float32) for shape in scratch],
        ),
        out_shape=outs,
        cost_estimate=pl.CostEstimate(
            flops=cost_us * 500_000_000, bytes_accessed=cost_us * 2_000_000, transcendentals=0
        ),
        compiler_params=pltpu.CompilerParams(vmem_limit_bytes=VMEM_BYTES),
    )(ids, *operands)


def local(out_grad, gated_input, features, filter_weight, rates, skip_bias):
    channels = out_grad.shape[0]
    seq_count = lax.axis_size("seq")
    groups = lax.axis_size("ch")
    all_channels = channels * groups
    points = seq_count // 2
    total = seq_count * BLOCK
    place = lax.axis_index("seq")
    ids = jnp.stack([place % 2, (place // 2) % 2, lax.axis_index("ch"), place]).astype(jnp.int32)
    across, by_lane, by_row, inner, lanes = (jnp.asarray(table) for table in tables(seq_count))
    swap_core = [(i, i ^ 1) for i in range(seq_count)]
    swap_chip = [(i, i ^ 2) for i in range(seq_count)]
    rates = rates.reshape(1, all_channels)
    skip_bias = skip_bias.reshape(1, all_channels)

    packed = prepare(
        total,
        ids,
        (out_grad, gated_input, features, filter_weight, rates),
    )
    same_core = [list(range(core, seq_count, 2)) for core in range(2)]

    def exchange(array):
        return lax.all_to_all(
            array, "seq", split_axis=0, concat_axis=0, tiled=True, axis_index_groups=same_core
        )

    received = exchange(packed.reshape(points, CHUNK, LANES))
    def flat(array):
        return array.reshape(-1, LANES)

    received, near = lax.optimization_barrier((received, received[:, ROWS:]))
    near_pair = lax.ppermute(near, "seq", swap_chip)
    halves = lax.all_to_all(
        jnp.broadcast_to(received, (2,) + received.shape),
        "seq",
        split_axis=0,
        concat_axis=0,
        tiled=True,
        axis_index_groups=[[i, i + 1] for i in range(0, seq_count, 2)],
    )
    halves = flat(halves)
    shape = (ROWS, points, LANES)
    wide = (ROWS, points, 2 * LANES)
    half = jnp.bfloat16
    spec, mix_in, mix_out, twist, lane_in, lane_out = call(
        first_kernel,
        ids,
        (halves, across, by_lane, by_row, inner, lanes),
        (0, 1, 1, 1, 0, 0),
        [
            (ROWS * points, 2 * LANES),
            (half, 2 * seq_count, 2 * seq_count),
            (half, 2 * seq_count, 2 * seq_count),
            (2, ROWS, points, LANES),
            (half, 2, 2 * LANES, 2 * LANES),
            (half, 2, 2 * LANES, 2 * LANES),
        ],
        [shape, shape, wide],
        cost_us=4,
    )
    near_pair, spec = lax.optimization_barrier((near_pair, spec))
    far_pair = lax.ppermute(near_pair, "seq", swap_core)
    given, mid = call(
        second_kernel,
        ids,
        (
            halves,
            flat(near_pair),
            flat(far_pair),
            spec,
            mix_in,
            mix_out,
            twist,
            inner,
            lane_in,
            lane_out,
        ),
        (0,) * 10,
        [(seq_count * HALF, LANES), wide],
        [shape, shape],
        cost_us=6,
    )
    (kept,) = call(
        third_kernel,
        ids,
        (mid, mix_out),
        (0, 0),
        [(seq_count * HALF, LANES)],
        [],
        cost_us=2,
    )
    result = kept + lax.ppermute(given, "seq", swap_core)
    result = exchange(result.reshape(points, ROWS, LANES))
    per_group = ROWS // groups
    lag = result.reshape(channels, 2, groups, per_group, LANES)[:, 1].transpose(1, 0, 2, 3)
    lag = lax.all_to_all(lag, "ch", split_axis=0, concat_axis=0, tiled=True)
    (in_grad,) = call(
        finish_kernel,
        ids,
        (flat(result), out_grad, skip_bias),
        (0, 0, 0),
        [(channels, BLOCK)],
        [(all_channels, LANES)],
        cost_us=2,
    )
    (feat_grad,) = call(
        functools.partial(project_kernel, total),
        ids,
        (filter_weight, flat(lag), rates),
        (0, 0, 0),
        [(filter_weight.shape[0], BLOCK // groups)],
        [],
        cost_us=1,
    )
    return (in_grad, feat_grad)


def solution(mesh):
    in_specs = (P("ch", "seq"), P("ch", "seq"), P(None, "seq"), P(), P(), P())
    out_specs = (P("ch", "seq"), P(None, ("seq", "ch")))
    return jax.shard_map(local, mesh=mesh, in_specs=in_specs, out_specs=out_specs, check_vma=False)
```

```python
import functools
import math

import jax
import jax.numpy as jnp
import numpy as np
from jax import lax
from jax.experimental import pallas as pl
from jax.experimental.pallas import tpu as pltpu
from jax.sharding import PartitionSpec as P

SHIFT = 0.05
LANES = 128
ROWS = 32
BLOCK = ROWS * LANES
HALF = ROWS // 2
CHUNK = ROWS + HALF
VMEM_BYTES = 40 * 1024 * 1024
VMEM_MOST = 63 * 1024 * 1024


@functools.lru_cache(maxsize=None)
def tables(seq_count):
    points = seq_count // 2
    circle = 2.0 * np.pi

    def waves(turns):
        return np.stack([np.cos(circle * turns), -np.sin(circle * turns)]).astype(np.float32)

    dev = np.arange(seq_count).reshape(points, 2).T.reshape(-1)
    lane, row = np.arange(LANES), np.arange(ROWS)
    across, by_lane, by_row = [], [], []
    for half in range(2):
        freq = 4 * (2 * np.arange(points) + half) + 1
        step = np.outer(freq, dev) % (4 * seq_count) / (4.0 * seq_count)
        across.append(np.concatenate(list(waves(step))))
        by_lane.append(waves(np.outer(freq, lane) / (4.0 * seq_count * BLOCK)))
        by_row.append(waves(np.outer(freq, row) / (4.0 * seq_count * ROWS)))
    inner = waves(np.outer(row, lane) / BLOCK)
    lanes = waves(np.outer(lane, lane) % LANES / LANES)
    return np.stack(across), np.stack(by_lane), np.stack(by_row), inner, lanes


def stack_pair(matrix, out_ref):
    rows, columns = matrix.shape
    high, low = split(matrix)
    out_ref[:rows, :columns] = high
    out_ref[:rows, columns:] = high
    out_ref[rows:, :columns] = low
    out_ref[rows:, columns:] = jnp.zeros_like(low)


def build_tables(
    ids, across_ref, by_lane_ref, by_row_ref, lanes_ref, mix_ref, back_ref, twist_ref, lane_ref, lane_back_ref
):
    across = across_ref[0]
    stack_pair(across, mix_ref)
    stack_pair(across.T * (1.0 / (across.shape[0] * BLOCK)), back_ref)
    cos, sin = lanes_ref[0], lanes_ref[1]
    for part, (c, s, t) in enumerate(zip(split(cos), split(sin), split(-sin))):
        lane_ref[part, :LANES, :LANES] = c
        lane_ref[part, :LANES, LANES:] = s
        lane_ref[part, LANES:, :LANES] = t
        lane_ref[part, LANES:, LANES:] = c
        lane_back_ref[part, :LANES, :LANES] = c
        lane_back_ref[part, :LANES, LANES:] = t
        lane_back_ref[part, LANES:, :LANES] = s
        lane_back_ref[part, LANES:, LANES:] = c
    lane_re, lane_im = by_lane_ref[0, 0], by_lane_ref[0, 1]
    row_re, row_im = by_row_ref[0, 0], by_row_ref[0, 1]
    for row in range(ROWS):
        re, im = times(lane_re, lane_im, row_re[:, row : row + 1], row_im[:, row : row + 1])
        twist_ref[0, row] = re
        twist_ref[1, row] = im


def dot(left, right):
    return jnp.dot(left, right, preferred_element_type=jnp.float32)


def split(values):
    high = values.astype(jnp.bfloat16)
    low = (values - high.astype(jnp.float32)).astype(jnp.bfloat16)
    return high, low


def times(a, b, re, im):
    return a * re - b * im, a * im + b * re


def scaled(a, b, number, sign):
    re, im = math.cos(number), sign * math.sin(number)
    if abs(im) < 1e-12 and re > 0:
        return a, b
    if abs(re) < 1e-12:
        return (-b, a) if im > 0 else (b, -a)
    return a * re - b * im, a * im + b * re


def four_points(vals, sign):
    (ar, ai), (br, bi), (cr, ci), (dr, di) = vals
    sr, si = ar + cr, ai + ci
    tr, ti = ar - cr, ai - ci
    ur, ui = br + dr, bi + di
    vr, vi = br - dr, bi - di
    if sign < 0:
        vr, vi = vi, -vr
    else:
        vr, vi = -vi, vr
    return [(sr + ur, si + ui), (tr + vr, ti + vi), (sr - ur, si - ui), (tr - vr, ti - vi)]


def eight_points(vals, sign):
    even = four_points(vals[0::2], sign)
    odd = four_points(vals[1::2], sign)
    low, high = [], []
    for index in range(4):
        er, ei = even[index]
        tr, ti = scaled(*odd[index], 2.0 * math.pi * index / 8, sign)
        low.append((er + tr, ei + ti))
        high.append((er - tr, ei - ti))
    return low + high


def short_transform(re_ref, im_ref, points, sign, finish):
    def tile(index, carry):
        rows = pl.ds(pl.multiple_of(index * 8, 8), 8)
        for second in range(8):
            vals = [(re_ref[8 * n + second, rows, :], im_ref[8 * n + second, rows, :]) for n in range(4)]
            vals = four_points(vals, sign)
            for k in range(4):
                re, im = scaled(*vals[k], 2.0 * math.pi * k * second / ROWS, sign)
                re_ref[8 * k + second, rows, :] = re
                im_ref[8 * k + second, rows, :] = im
        for k in range(4):
            vals = [(re_ref[8 * k + n, rows, :], im_ref[8 * k + n, rows, :]) for n in range(8)]
            vals = eight_points(vals, sign)
            for j in range(8):
                finish(k + 4 * j, rows, *vals[j])
        return carry

    lax.fori_loop(0, points // 8, tile, 0)


def forward(load, points, mix_ref, twist_ref, inner_ref, re_ref, im_ref, lane_in_ref):
    count = 2 * points
    for row in range(HALF):
        high, low = split(jnp.concatenate(load(row), axis=1))
        full = dot(mix_ref[...], jnp.concatenate([high, low], axis=0))
        full = full[:count] + full[count:]
        for part in range(2):
            place = row + part * HALF
            lanes = slice(part * LANES, (part + 1) * LANES)
            re, im = times(
                full[:points, lanes],
                full[points:, lanes],
                twist_ref[0, place],
                twist_ref[1, place],
            )
            re_ref[place] = re
            im_ref[place] = im

    def finish(k, rows, re, im):
        re, im = times(re, im, inner_ref[0, k : k + 1, :], inner_ref[1, k : k + 1, :])
        lane_in_ref[k, rows, :LANES] = re
        lane_in_ref[k, rows, LANES:] = im

    short_transform(re_ref, im_ref, points, -1.0, finish)


def lane_product(values, lane_ref):
    high, low = split(values)
    return dot(high, lane_ref[0]) + dot(low, lane_ref[0]) + dot(high, lane_ref[1])


def spread_rows(values):
    return jnp.broadcast_to(values, (LANES, values.shape[1])).T


def window_tile(rate_tile, first, row, total):
    lane = lax.broadcasted_iota(jnp.int32, rate_tile.shape, 1)
    place = (first + row * LANES + lane).astype(jnp.float32) * (1.0 / total)
    return jnp.exp(-rate_tile * place) + SHIFT


def prepare_kernel(
    total,
    ids,
    grad_hbm,
    input_hbm,
    feat_hbm,
    weight_hbm,
    rates_hbm,
    out_hbm,
    grad_ref,
    input_ref,
    feat_ref,
    weight_ref,
    rates_ref,
    out_ref,
    weight_t,
    rate_t,
    small_sems,
    feat_sems,
    grad_sems,
    input_sems,
    out_sems,
):
    channels = grad_ref.shape[0]
    groups = channels // 8
    pieces = feat_sems.shape[0]
    span = BLOCK // pieces

    def copy(source, target, sems, index, *where):
        return pltpu.make_async_copy(source.at[where], target.at[where], sems.at[index])

    weight_copy = copy(weight_hbm, weight_ref, small_sems, 0)
    rates_copy = copy(rates_hbm, rates_ref, small_sems, 1)
    weight_copy.start()
    rates_copy.start()
    grad_copies = [copy(grad_hbm, grad_ref, grad_sems, g, pl.ds(g * 8, 8)) for g in range(groups)]
    input_copies = [
        copy(input_hbm, input_ref, input_sems, g, pl.ds(g * 8, 8)) for g in range(groups)
    ]
    for g in range(groups):
        input_copies[g].start()
        grad_copies[g].start()
    feat_copies = [
        copy(feat_hbm, feat_ref, feat_sems, k, slice(None), pl.ds(k * span, span))
        for k in range(pieces)
    ]
    for feat_copy in feat_copies:
        feat_copy.start()

    first = ids[3] * BLOCK
    start = pl.multiple_of(ids[2] * channels, 8)
    weight_copy.wait()
    rates_copy.wait()
    weight_t[...] = weight_ref[...].T
    rate_t[...] = spread_rows(rates_ref[...])
    high, low = split(weight_t[pl.ds(start, channels), :])
    both = jnp.concatenate([high, low], axis=0)
    rate_tile = rate_t[pl.ds(start, channels), :]
    wide = 2 * LANES
    out_copies = []

    def put(g, part, row, values):
        out_ref[part, g * 8 : g * 8 + 8, row, :] = values

    def send(g, part):
        place = g * 2 + part
        done = pltpu.make_async_copy(
            out_ref.at[part, pl.ds(g * 8, 8)], out_hbm.at[pl.ds(g * 8, 8), part], out_sems.at[place]
        )
        done.start()
        out_copies.append(done)

    for g in range(groups):
        rows = slice(g * 8, g * 8 + 8)
        input_copies[g].wait()
        grad_copies[g].wait()
        for row in range(ROWS):
            here = slice(row * LANES, (row + 1) * LANES)
            put(g, 1, row, input_ref[rows, here])
            put(g, row // HALF, ROWS + row % HALF, grad_ref[rows, here])
        send(g, 1)
    for k in range(pieces):
        feat_copies[k].wait()
        for begin in range(k * span, (k + 1) * span, wide):
            feat_high, feat_low = split(feat_ref[:, begin : begin + wide])
            full = dot(both, feat_high)
            full = full[:channels] + full[channels:] + dot(high, feat_low)
            for part in range(2):
                row = begin // LANES + part
                filt = full[:, part * LANES : (part + 1) * LANES]
                filt = filt * window_tile(rate_tile, first, row, total)
                for g in range(groups):
                    put(g, 0, row, filt[g * 8 : g * 8 + 8])
    for g in range(groups):
        send(g, 0)
    for done in out_copies:
        done.wait()


def prepare(total, ids, operands):
    channels, columns = operands[0].shape
    outer = pl.BlockSpec(memory_space=pltpu.HBM)
    weight_shape = operands[3].shape
    scratch = [operand.shape for operand in operands] + [
        (2, channels, CHUNK, LANES),
        weight_shape[::-1],
        (weight_shape[1], LANES),
    ]
    return pl.pallas_call(
        functools.partial(prepare_kernel, total),
        grid_spec=pltpu.PrefetchScalarGridSpec(
            num_scalar_prefetch=1,
            grid=(1,),
            in_specs=[outer] * len(operands),
            out_specs=outer,
            scratch_shapes=[pltpu.VMEM(shape, jnp.float32) for shape in scratch]
            + [pltpu.SemaphoreType.DMA((n,)) for n in (2, 4, channels // 8, channels // 8, channels // 4)],
        ),
        out_shape=jax.ShapeDtypeStruct((channels, 2, CHUNK, LANES), jnp.float32),
        compiler_params=pltpu.CompilerParams(vmem_limit_bytes=VMEM_MOST),
    )(ids, *operands)


def first_kernel(
    ids, halves_ref, mix_ref, twist_ref, inner_ref, lane_ref, out_ref, re_ref, im_ref, mid_ref
):
    count = halves_ref.shape[0] // CHUNK
    points = count // 2

    def load(row):
        return [
            halves_ref[pl.ds(place, count, stride=CHUNK), :] for place in (row, row + HALF)
        ]

    forward(load, points, mix_ref, twist_ref, inner_ref, re_ref, im_ref, mid_ref)
    step = max(1, 256 // points)
    for k in range(0, ROWS, step):
        values = mid_ref[k : k + step].reshape(step * points, 2 * LANES)
        out_ref[k * points : (k + step) * points, :] = lane_product(values, lane_ref)


def second_kernel(
    ids,
    halves_ref,
    near_pair_ref,
    far_pair_ref,
    spec_ref,
    mix_ref,
    back_ref,
    twist_ref,
    inner_ref,
    lane_ref,
    lane_back_ref,
    given_ref,
    mid_ref,
    re_ref,
    im_ref,
):
    count = halves_ref.shape[0] // CHUNK
    points = count // 2
    upper = ids[0] == 1
    second = ids[1] == 1

    def load(row):
        here = pl.ds(row, points, stride=HALF)
        near, far = near_pair_ref[here, :], far_pair_ref[here, :]
        pair = jnp.concatenate(
            [jnp.where(upper, far, near), jnp.where(upper, near, far)], axis=0
        )
        own = halves_ref[pl.ds(ROWS + row, count, stride=CHUNK), :]
        return [jnp.where(second, pair, own), jnp.where(second, own, pair)]

    forward(load, points, mix_ref, twist_ref, inner_ref, re_ref, im_ref, mid_ref)
    step = max(1, 256 // points)
    for k in range(0, ROWS, step):
        values = mid_ref[k : k + step].reshape(step * points, 2 * LANES)
        values = lane_product(values, lane_ref)
        spec = spec_ref[k * points : (k + step) * points, :]
        re, im = times(
            values[:, :LANES], values[:, LANES:], spec[:, :LANES], -spec[:, LANES:]
        )
        values = lane_product(jnp.concatenate([re, im], axis=1), lane_back_ref)
        for j in range(step):
            rows = slice(j * points, (j + 1) * points)
            re, im = times(
                values[rows, :LANES],
                values[rows, LANES:],
                inner_ref[0, k + j : k + j + 1, :],
                -inner_ref[1, k + j : k + j + 1, :],
            )
            re_ref[k + j] = re
            im_ref[k + j] = im

    def finish(k, rows, re, im):
        re, im = times(re, im, twist_ref[0, k, rows, :], -twist_ref[1, k, rows, :])
        mid_ref[k, rows, :LANES] = re
        mid_ref[k, rows, LANES:] = im

    short_transform(re_ref, im_ref, points, 1.0, finish)
    back_half(mid_ref, back_ref, given_ref, 1 - ids[0])


def back_half(mid_ref, back_ref, out_ref, core):
    count = back_ref.shape[0] // 2
    points = count // 2
    start = pl.multiple_of(core * points, points)
    matrix = jnp.concatenate(
        [back_ref[pl.ds(start, points), :], back_ref[pl.ds(count + start, points), :]], axis=0
    )
    for row in range(0, ROWS, 2):
        both = []
        for place in (row, row + 1):
            values = mid_ref[place]
            both.append(jnp.concatenate([values[:, :LANES], values[:, LANES:]], axis=0))
        high, low = split(jnp.concatenate(both, axis=1))
        full = dot(matrix, jnp.concatenate([high, low], axis=0))
        full = full[:points] + full[points:]
        for part in range(2):
            here = pl.ds(row + part, points, stride=ROWS)
            out_ref[here, :] = full[:, part * LANES : (part + 1) * LANES]


def third_kernel(ids, mid_ref, back_ref, kept_ref):
    back_half(mid_ref, back_ref, kept_ref, ids[0])


def finish_kernel(ids, back_ref, grad_ref, bias_ref, in_grad_ref, bias_t):
    channels = grad_ref.shape[0]
    own = pl.ds(pl.multiple_of(ids[2] * channels, 8), channels)
    bias_t[...] = spread_rows(bias_ref[...])
    bias_tile = bias_t[own, :]
    for row in range(ROWS):
        here = slice(row * LANES, (row + 1) * LANES)
        conv = back_ref[pl.ds(row, channels, stride=4 * HALF), :]
        in_grad_ref[:, here] = conv + bias_tile * grad_ref[:, here]


def project_kernel(total, ids, weight_ref, lag_ref, rates_ref, out_ref):
    rows, channels = weight_ref.shape
    per_group = lag_ref.shape[0] // channels
    first = ids[3] * BLOCK + ids[2] * (per_group * LANES)
    high, low = split(weight_ref[...])
    both = jnp.concatenate([high, low], axis=0)
    rate_tile = spread_rows(rates_ref[...])
    for row in range(0, per_group, 2):
        tiles = [
            lag_ref[pl.ds(row + part, channels, stride=per_group), :]
            * window_tile(rate_tile, first, row + part, total)
            for part in range(2)
        ]
        value_high, value_low = split(jnp.concatenate(tiles, axis=1))
        full = dot(both, value_high)
        full = full[:rows] + full[rows:] + dot(high, value_low)
        out_ref[:, row * LANES : (row + 2) * LANES] = full


def whole(array):
    return pl.BlockSpec(array.shape, lambda i, ids: (0,) * array.ndim)


def by_core(array):
    return pl.BlockSpec((1,) + array.shape[1:], lambda i, ids: (ids[0],) + (0,) * (array.ndim - 1))


def call(kernel, ids, operands, kinds, out_shapes, scratch, cost_us=0):
    specs = [by_core(a) if kind else whole(a) for a, kind in zip(operands, kinds)]
    outs = [
        jax.ShapeDtypeStruct(shape[1:], shape[0])
        if shape[0] == jnp.bfloat16
        else jax.ShapeDtypeStruct(shape, jnp.float32)
        for shape in out_shapes
    ]
    out_specs = [whole(out) for out in outs]
    return pl.pallas_call(
        kernel,
        grid_spec=pltpu.PrefetchScalarGridSpec(
            num_scalar_prefetch=1,
            grid=(1,),
            in_specs=specs,
            out_specs=out_specs,
            scratch_shapes=[pltpu.VMEM(shape, jnp.float32) for shape in scratch],
        ),
        out_shape=outs,
        cost_estimate=pl.CostEstimate(
            flops=cost_us * 500_000_000, bytes_accessed=cost_us * 2_000_000, transcendentals=0
        ),
        compiler_params=pltpu.CompilerParams(vmem_limit_bytes=VMEM_BYTES),
    )(ids, *operands)


def local(out_grad, gated_input, features, filter_weight, rates, skip_bias):
    channels = out_grad.shape[0]
    seq_count = lax.axis_size("seq")
    groups = lax.axis_size("ch")
    all_channels = channels * groups
    points = seq_count // 2
    total = seq_count * BLOCK
    place = lax.axis_index("seq")
    ids = jnp.stack([place % 2, (place // 2) % 2, lax.axis_index("ch"), place]).astype(jnp.int32)
    across, by_lane, by_row, inner, lanes = (jnp.asarray(table) for table in tables(seq_count))
    swap_core = [(i, i ^ 1) for i in range(seq_count)]
    swap_chip = [(i, i ^ 2) for i in range(seq_count)]
    rates = rates.reshape(1, all_channels)
    skip_bias = skip_bias.reshape(1, all_channels)

    half = jnp.bfloat16
    mix_in, mix_out, twist, lane_in, lane_out = call(
        build_tables,
        ids,
        (across, by_lane, by_row, lanes),
        (1, 1, 1, 0),
        [
            (half, 2 * seq_count, 2 * seq_count),
            (half, 2 * seq_count, 2 * seq_count),
            (2, ROWS, points, LANES),
            (half, 2, 2 * LANES, 2 * LANES),
            (half, 2, 2 * LANES, 2 * LANES),
        ],
        [],
        cost_us=1,
    )
    packed = prepare(
        total,
        ids,
        (out_grad, gated_input, features, filter_weight, rates),
    )
    same_core = [list(range(core, seq_count, 2)) for core in range(2)]

    def exchange(array):
        return lax.all_to_all(
            array, "seq", split_axis=0, concat_axis=0, tiled=True, axis_index_groups=same_core
        )

    received = exchange(packed.reshape(points, CHUNK, LANES))
    def flat(array):
        return array.reshape(-1, LANES)

    received, near = lax.optimization_barrier((received, received[:, ROWS:]))
    near_pair = lax.ppermute(near, "seq", swap_chip)
    halves = lax.all_to_all(
        jnp.broadcast_to(received, (2,) + received.shape),
        "seq",
        split_axis=0,
        concat_axis=0,
        tiled=True,
        axis_index_groups=[[i, i + 1] for i in range(0, seq_count, 2)],
    )
    halves = flat(halves)
    shape = (ROWS, points, LANES)
    wide = (ROWS, points, 2 * LANES)
    (spec,) = call(
        first_kernel,
        ids,
        (halves, mix_in, twist, inner, lane_in),
        (0, 0, 0, 0, 0),
        [(ROWS * points, 2 * LANES)],
        [shape, shape, wide],
        cost_us=4,
    )
    near_pair, spec = lax.optimization_barrier((near_pair, spec))
    far_pair = lax.ppermute(near_pair, "seq", swap_core)
    given, mid = call(
        second_kernel,
        ids,
        (
            halves,
            flat(near_pair),
            flat(far_pair),
            spec,
            mix_in,
            mix_out,
            twist,
            inner,
            lane_in,
            lane_out,
        ),
        (0,) * 10,
        [(seq_count * HALF, LANES), wide],
        [shape, shape],
        cost_us=6,
    )
    (kept,) = call(
        third_kernel,
        ids,
        (mid, mix_out),
        (0, 0),
        [(seq_count * HALF, LANES)],
        [],
        cost_us=2,
    )
    result = kept + lax.ppermute(given, "seq", swap_core)
    result = exchange(result.reshape(points, ROWS, LANES))
    per_group = ROWS // groups
    lag = result.reshape(channels, 2, groups, per_group, LANES)[:, 1].transpose(1, 0, 2, 3)
    lag = lax.all_to_all(lag, "ch", split_axis=0, concat_axis=0, tiled=True)
    (in_grad,) = call(
        finish_kernel,
        ids,
        (flat(result), out_grad, skip_bias),
        (0, 0, 0),
        [(channels, BLOCK)],
        [(all_channels, LANES)],
        cost_us=2,
    )
    (feat_grad,) = call(
        functools.partial(project_kernel, total),
        ids,
        (filter_weight, flat(lag), rates),
        (0, 0, 0),
        [(filter_weight.shape[0], BLOCK // groups)],
        [],
        cost_us=1,
    )
    return (in_grad, feat_grad)


def solution(mesh):
    in_specs = (P("ch", "seq"), P("ch", "seq"), P(None, "seq"), P(), P(), P())
    out_specs = (P("ch", "seq"), P(None, ("seq", "ch")))
    return jax.shard_map(local, mesh=mesh, in_specs=in_specs, out_specs=out_specs, check_vma=False)
```

```python
import functools
import math

import jax
import jax.numpy as jnp
import numpy as np
from jax import lax
from jax.experimental import pallas as pl
from jax.experimental.pallas import tpu as pltpu
from jax.sharding import PartitionSpec as P

SHIFT = 0.05
LANES = 128
ROWS = 32
BLOCK = ROWS * LANES
HALF = ROWS // 2
CHUNK = ROWS + HALF
VMEM_BYTES = 40 * 1024 * 1024
VMEM_MOST = 63 * 1024 * 1024


@functools.lru_cache(maxsize=None)
def tables(seq_count):
    points = seq_count // 2
    circle = 2.0 * np.pi

    def waves(turns):
        return np.stack([np.cos(circle * turns), -np.sin(circle * turns)]).astype(np.float32)

    dev = np.arange(seq_count).reshape(points, 2).T.reshape(-1)
    lane, row = np.arange(LANES), np.arange(ROWS)
    across, by_lane, by_row = [], [], []
    for half in range(2):
        freq = 4 * (2 * np.arange(points) + half) + 1
        step = np.outer(freq, dev) % (4 * seq_count) / (4.0 * seq_count)
        across.append(np.concatenate(list(waves(step))))
        by_lane.append(waves(np.outer(freq, lane) / (4.0 * seq_count * BLOCK)))
        by_row.append(waves(np.outer(freq, row) / (4.0 * seq_count * ROWS)))
    inner = waves(np.outer(row, lane) / BLOCK)
    lanes = waves(np.outer(lane, lane) % LANES / LANES)
    return np.stack(across), np.stack(by_lane), np.stack(by_row), inner, lanes


def stack_pair(matrix, out_ref):
    rows, columns = matrix.shape
    high, low = split(matrix)
    out_ref[:rows, :columns] = high
    out_ref[:rows, columns:] = high
    out_ref[rows:, :columns] = low
    out_ref[rows:, columns:] = jnp.zeros_like(low)


def build_tables(
    ids, across_ref, by_lane_ref, by_row_ref, lanes_ref, mix_ref, back_ref, twist_ref, lane_ref, lane_back_ref
):
    across = across_ref[0]
    stack_pair(across, mix_ref)
    stack_pair(across.T * (1.0 / (across.shape[0] * BLOCK)), back_ref)
    cos, sin = lanes_ref[0], lanes_ref[1]
    for part, (c, s, t) in enumerate(zip(split(cos), split(sin), split(-sin))):
        lane_ref[part, :LANES, :LANES] = c
        lane_ref[part, :LANES, LANES:] = s
        lane_ref[part, LANES:, :LANES] = t
        lane_ref[part, LANES:, LANES:] = c
        lane_back_ref[part, :LANES, :LANES] = c
        lane_back_ref[part, :LANES, LANES:] = t
        lane_back_ref[part, LANES:, :LANES] = s
        lane_back_ref[part, LANES:, LANES:] = c
    lane_re, lane_im = by_lane_ref[0, 0], by_lane_ref[0, 1]
    row_re, row_im = by_row_ref[0, 0], by_row_ref[0, 1]
    for row in range(ROWS):
        re, im = times(lane_re, lane_im, row_re[:, row : row + 1], row_im[:, row : row + 1])
        twist_ref[0, row] = re
        twist_ref[1, row] = im


def dot(left, right):
    return jnp.dot(left, right, preferred_element_type=jnp.float32)


def split(values):
    high = values.astype(jnp.bfloat16)
    low = (values - high.astype(jnp.float32)).astype(jnp.bfloat16)
    return high, low


def times(a, b, re, im):
    return a * re - b * im, a * im + b * re


def scaled(a, b, number, sign):
    re, im = math.cos(number), sign * math.sin(number)
    if abs(im) < 1e-12 and re > 0:
        return a, b
    if abs(re) < 1e-12:
        return (-b, a) if im > 0 else (b, -a)
    return a * re - b * im, a * im + b * re


def four_points(vals, sign):
    (ar, ai), (br, bi), (cr, ci), (dr, di) = vals
    sr, si = ar + cr, ai + ci
    tr, ti = ar - cr, ai - ci
    ur, ui = br + dr, bi + di
    vr, vi = br - dr, bi - di
    if sign < 0:
        vr, vi = vi, -vr
    else:
        vr, vi = -vi, vr
    return [(sr + ur, si + ui), (tr + vr, ti + vi), (sr - ur, si - ui), (tr - vr, ti - vi)]


def eight_points(vals, sign):
    even = four_points(vals[0::2], sign)
    odd = four_points(vals[1::2], sign)
    low, high = [], []
    for index in range(4):
        er, ei = even[index]
        tr, ti = scaled(*odd[index], 2.0 * math.pi * index / 8, sign)
        low.append((er + tr, ei + ti))
        high.append((er - tr, ei - ti))
    return low + high


def short_transform(re_ref, im_ref, points, sign, finish):
    def tile(index, carry):
        rows = pl.ds(pl.multiple_of(index * 8, 8), 8)
        for second in range(8):
            vals = [(re_ref[8 * n + second, rows, :], im_ref[8 * n + second, rows, :]) for n in range(4)]
            vals = four_points(vals, sign)
            for k in range(4):
                re, im = scaled(*vals[k], 2.0 * math.pi * k * second / ROWS, sign)
                re_ref[8 * k + second, rows, :] = re
                im_ref[8 * k + second, rows, :] = im
        for k in range(4):
            vals = [(re_ref[8 * k + n, rows, :], im_ref[8 * k + n, rows, :]) for n in range(8)]
            vals = eight_points(vals, sign)
            for j in range(8):
                finish(k + 4 * j, rows, *vals[j])
        return carry

    lax.fori_loop(0, points // 8, tile, 0)


def forward(load, points, mix_ref, twist_ref, inner_ref, re_ref, im_ref, lane_in_ref):
    count = 2 * points
    for row in range(HALF):
        high, low = split(jnp.concatenate(load(row), axis=1))
        full = dot(mix_ref[...], jnp.concatenate([high, low], axis=0))
        full = full[:count] + full[count:]
        for part in range(2):
            place = row + part * HALF
            lanes = slice(part * LANES, (part + 1) * LANES)
            re, im = times(
                full[:points, lanes],
                full[points:, lanes],
                twist_ref[0, place],
                twist_ref[1, place],
            )
            re_ref[place] = re
            im_ref[place] = im

    def finish(k, rows, re, im):
        re, im = times(re, im, inner_ref[0, k : k + 1, :], inner_ref[1, k : k + 1, :])
        lane_in_ref[k, rows, :LANES] = re
        lane_in_ref[k, rows, LANES:] = im

    short_transform(re_ref, im_ref, points, -1.0, finish)


def lane_product(values, lane_ref):
    high, low = split(values)
    return dot(high, lane_ref[0]) + dot(low, lane_ref[0]) + dot(high, lane_ref[1])


def spread_rows(values):
    return jnp.broadcast_to(values, (LANES, values.shape[1])).T


def window_tile(rate_tile, first, row, total):
    lane = lax.broadcasted_iota(jnp.int32, rate_tile.shape, 1)
    place = (first + row * LANES + lane).astype(jnp.float32) * (1.0 / total)
    return jnp.exp(-rate_tile * place) + SHIFT


def prepare_kernel(
    total,
    ids,
    grad_hbm,
    input_hbm,
    feat_hbm,
    weight_hbm,
    rates_hbm,
    out_hbm,
    grad_ref,
    input_ref,
    feat_ref,
    weight_ref,
    rates_ref,
    out_ref,
    weight_t,
    rate_t,
    small_sems,
    feat_sems,
    grad_sems,
    input_sems,
    out_sems,
):
    channels = grad_ref.shape[0]
    groups = channels // 8
    pieces = feat_sems.shape[0]
    span = BLOCK // pieces

    def copy(source, target, sems, index, *where):
        return pltpu.make_async_copy(source.at[where], target.at[where], sems.at[index])

    weight_copy = copy(weight_hbm, weight_ref, small_sems, 0)
    rates_copy = copy(rates_hbm, rates_ref, small_sems, 1)
    weight_copy.start()
    rates_copy.start()
    grad_copies = [copy(grad_hbm, grad_ref, grad_sems, g, pl.ds(g * 8, 8)) for g in range(groups)]
    input_copies = [
        copy(input_hbm, input_ref, input_sems, g, pl.ds(g * 8, 8)) for g in range(groups)
    ]
    for g in range(groups):
        input_copies[g].start()
        grad_copies[g].start()
    feat_copies = [
        copy(feat_hbm, feat_ref, feat_sems, k, slice(None), pl.ds(k * span, span))
        for k in range(pieces)
    ]
    for feat_copy in feat_copies:
        feat_copy.start()

    first = ids[3] * BLOCK
    start = pl.multiple_of(ids[2] * channels, 8)
    weight_copy.wait()
    rates_copy.wait()
    weight_t[...] = weight_ref[...].T
    rate_t[...] = spread_rows(rates_ref[...])
    high, low = split(weight_t[pl.ds(start, channels), :])
    both = jnp.concatenate([high, low], axis=0)
    rate_tile = rate_t[pl.ds(start, channels), :]
    wide = 2 * LANES
    out_copies = []

    def put(g, part, row, values):
        out_ref[part, g * 8 : g * 8 + 8, row, :] = values

    def send(g, part):
        place = g * 2 + part
        done = pltpu.make_async_copy(
            out_ref.at[part, pl.ds(g * 8, 8)], out_hbm.at[pl.ds(g * 8, 8), part], out_sems.at[place]
        )
        done.start()
        out_copies.append(done)

    for g in range(groups):
        rows = slice(g * 8, g * 8 + 8)
        input_copies[g].wait()
        grad_copies[g].wait()
        for row in range(ROWS):
            here = slice(row * LANES, (row + 1) * LANES)
            put(g, 1, row, input_ref[rows, here])
            put(g, row // HALF, ROWS + row % HALF, grad_ref[rows, here])
        send(g, 1)
    for k in range(pieces):
        feat_copies[k].wait()
        for begin in range(k * span, (k + 1) * span, wide):
            feat_high, feat_low = split(feat_ref[:, begin : begin + wide])
            full = dot(both, feat_high)
            full = full[:channels] + full[channels:] + dot(high, feat_low)
            for part in range(2):
                row = begin // LANES + part
                filt = full[:, part * LANES : (part + 1) * LANES]
                filt = filt * window_tile(rate_tile, first, row, total)
                for g in range(groups):
                    put(g, 0, row, filt[g * 8 : g * 8 + 8])
    for g in range(groups):
        send(g, 0)
    for done in out_copies:
        done.wait()


def prepare(total, ids, operands):
    channels, columns = operands[0].shape
    outer = pl.BlockSpec(memory_space=pltpu.HBM)
    weight_shape = operands[3].shape
    scratch = [operand.shape for operand in operands] + [
        (2, channels, CHUNK, LANES),
        weight_shape[::-1],
        (weight_shape[1], LANES),
    ]
    return pl.pallas_call(
        functools.partial(prepare_kernel, total),
        grid_spec=pltpu.PrefetchScalarGridSpec(
            num_scalar_prefetch=1,
            grid=(1,),
            in_specs=[outer] * len(operands),
            out_specs=outer,
            scratch_shapes=[pltpu.VMEM(shape, jnp.float32) for shape in scratch]
            + [pltpu.SemaphoreType.DMA((n,)) for n in (2, 4, channels // 8, channels // 8, channels // 4)],
        ),
        out_shape=jax.ShapeDtypeStruct((channels, 2, CHUNK, LANES), jnp.float32),
        compiler_params=pltpu.CompilerParams(vmem_limit_bytes=VMEM_MOST),
    )(ids, *operands)


def first_kernel(
    ids, halves_ref, mix_ref, twist_ref, inner_ref, lane_ref, out_ref, re_ref, im_ref, mid_ref
):
    count = halves_ref.shape[0] // CHUNK
    points = count // 2

    def load(row):
        return [
            halves_ref[pl.ds(place, count, stride=CHUNK), :] for place in (row, row + HALF)
        ]

    forward(load, points, mix_ref, twist_ref, inner_ref, re_ref, im_ref, mid_ref)
    step = max(1, 256 // points)
    for k in range(0, ROWS, step):
        values = mid_ref[k : k + step].reshape(step * points, 2 * LANES)
        out_ref[k * points : (k + step) * points, :] = lane_product(values, lane_ref)


def second_kernel(
    ids,
    halves_ref,
    near_pair_ref,
    far_pair_ref,
    spec_ref,
    mix_ref,
    back_ref,
    twist_ref,
    inner_ref,
    lane_ref,
    lane_back_ref,
    given_ref,
    mid_ref,
    re_ref,
    im_ref,
):
    count = halves_ref.shape[0] // CHUNK
    points = count // 2
    upper = ids[0] == 1
    second = ids[1] == 1

    def load(row):
        here = pl.ds(row, points, stride=HALF)
        near, far = near_pair_ref[here, :], far_pair_ref[here, :]
        pair = jnp.concatenate(
            [jnp.where(upper, far, near), jnp.where(upper, near, far)], axis=0
        )
        own = halves_ref[pl.ds(ROWS + row, count, stride=CHUNK), :]
        return [jnp.where(second, pair, own), jnp.where(second, own, pair)]

    forward(load, points, mix_ref, twist_ref, inner_ref, re_ref, im_ref, mid_ref)
    step = max(1, 256 // points)
    for k in range(0, ROWS, step):
        values = mid_ref[k : k + step].reshape(step * points, 2 * LANES)
        values = lane_product(values, lane_ref)
        spec = spec_ref[k * points : (k + step) * points, :]
        re, im = times(
            values[:, :LANES], values[:, LANES:], spec[:, :LANES], -spec[:, LANES:]
        )
        values = lane_product(jnp.concatenate([re, im], axis=1), lane_back_ref)
        for j in range(step):
            rows = slice(j * points, (j + 1) * points)
            re, im = times(
                values[rows, :LANES],
                values[rows, LANES:],
                inner_ref[0, k + j : k + j + 1, :],
                -inner_ref[1, k + j : k + j + 1, :],
            )
            re_ref[k + j] = re
            im_ref[k + j] = im

    def finish(k, rows, re, im):
        re, im = times(re, im, twist_ref[0, k, rows, :], -twist_ref[1, k, rows, :])
        mid_ref[k, rows, :LANES] = re
        mid_ref[k, rows, LANES:] = im

    short_transform(re_ref, im_ref, points, 1.0, finish)
    back_half(mid_ref, back_ref, given_ref, 1 - ids[0])


def back_half(mid_ref, back_ref, out_ref, core):
    count = back_ref.shape[0] // 2
    points = count // 2
    start = pl.multiple_of(core * points, points)
    matrix = jnp.concatenate(
        [back_ref[pl.ds(start, points), :], back_ref[pl.ds(count + start, points), :]], axis=0
    )
    for row in range(0, ROWS, 2):
        both = []
        for place in (row, row + 1):
            values = mid_ref[place]
            both.append(jnp.concatenate([values[:, :LANES], values[:, LANES:]], axis=0))
        high, low = split(jnp.concatenate(both, axis=1))
        full = dot(matrix, jnp.concatenate([high, low], axis=0))
        full = full[:points] + full[points:]
        for part in range(2):
            here = pl.ds(row + part, points, stride=ROWS)
            out_ref[here, :] = full[:, part * LANES : (part + 1) * LANES]


def third_kernel(ids, mid_ref, back_ref, kept_ref):
    back_half(mid_ref, back_ref, kept_ref, ids[0])


def finish_kernel(ids, back_ref, grad_ref, bias_ref, in_grad_ref, bias_t):
    channels = grad_ref.shape[0]
    own = pl.ds(pl.multiple_of(ids[2] * channels, 8), channels)
    bias_t[...] = spread_rows(bias_ref[...])
    bias_tile = bias_t[own, :]
    for row in range(ROWS):
        here = slice(row * LANES, (row + 1) * LANES)
        conv = back_ref[pl.ds(row, channels, stride=4 * HALF), :]
        in_grad_ref[:, here] = conv + bias_tile * grad_ref[:, here]


def project_kernel(total, ids, weight_ref, lag_ref, rates_ref, out_ref):
    rows, channels = weight_ref.shape
    per_group = lag_ref.shape[0] // channels
    first = ids[3] * BLOCK + ids[2] * (per_group * LANES)
    high, low = split(weight_ref[...])
    both = jnp.concatenate([high, low], axis=0)
    rate_tile = spread_rows(rates_ref[...])
    for row in range(0, per_group, 2):
        tiles = [
            lag_ref[pl.ds(row + part, channels, stride=per_group), :]
            * window_tile(rate_tile, first, row + part, total)
            for part in range(2)
        ]
        value_high, value_low = split(jnp.concatenate(tiles, axis=1))
        full = dot(both, value_high)
        full = full[:rows] + full[rows:] + dot(high, value_low)
        out_ref[:, row * LANES : (row + 2) * LANES] = full


def whole(array):
    return pl.BlockSpec(array.shape, lambda i, ids: (0,) * array.ndim)


def by_core(array):
    return pl.BlockSpec((1,) + array.shape[1:], lambda i, ids: (ids[0],) + (0,) * (array.ndim - 1))


def call(kernel, ids, operands, kinds, out_shapes, scratch, cost_us=0):
    specs = [by_core(a) if kind else whole(a) for a, kind in zip(operands, kinds)]
    outs = [
        jax.ShapeDtypeStruct(shape[1:], shape[0])
        if shape[0] == jnp.bfloat16
        else jax.ShapeDtypeStruct(shape, jnp.float32)
        for shape in out_shapes
    ]
    out_specs = [whole(out) for out in outs]
    return pl.pallas_call(
        kernel,
        grid_spec=pltpu.PrefetchScalarGridSpec(
            num_scalar_prefetch=1,
            grid=(1,),
            in_specs=specs,
            out_specs=out_specs,
            scratch_shapes=[pltpu.VMEM(shape, jnp.float32) for shape in scratch],
        ),
        out_shape=outs,
        cost_estimate=pl.CostEstimate(
            flops=cost_us * 500_000_000, bytes_accessed=cost_us * 2_000_000, transcendentals=0
        ),
        compiler_params=pltpu.CompilerParams(vmem_limit_bytes=VMEM_BYTES),
    )(ids, *operands)


def local(out_grad, gated_input, features, filter_weight, rates, skip_bias):
    channels = out_grad.shape[0]
    seq_count = lax.axis_size("seq")
    groups = lax.axis_size("ch")
    all_channels = channels * groups
    points = seq_count // 2
    total = seq_count * BLOCK
    place = lax.axis_index("seq")
    ids = jnp.stack([place % 2, (place // 2) % 2, lax.axis_index("ch"), place]).astype(jnp.int32)
    across, by_lane, by_row, inner, lanes = (jnp.asarray(table) for table in tables(seq_count))
    swap_core = [(i, i ^ 1) for i in range(seq_count)]
    swap_chip = [(i, i ^ 2) for i in range(seq_count)]
    rates = rates.reshape(1, all_channels)
    skip_bias = skip_bias.reshape(1, all_channels)

    half = jnp.bfloat16
    mix_in, mix_out, twist, lane_in, lane_out = call(
        build_tables,
        ids,
        (across, by_lane, by_row, lanes),
        (1, 1, 1, 0),
        [
            (half, 2 * seq_count, 2 * seq_count),
            (half, 2 * seq_count, 2 * seq_count),
            (2, ROWS, points, LANES),
            (half, 2, 2 * LANES, 2 * LANES),
            (half, 2, 2 * LANES, 2 * LANES),
        ],
        [],
        cost_us=1,
    )
    packed = prepare(
        total,
        ids,
        (out_grad, gated_input, features, filter_weight, rates),
    )
    same_core = [list(range(core, seq_count, 2)) for core in range(2)]

    def exchange(array):
        return lax.all_to_all(
            array, "seq", split_axis=0, concat_axis=0, tiled=True, axis_index_groups=same_core
        )

    received = exchange(packed.reshape(points, CHUNK, LANES))
    def flat(array):
        return array.reshape(-1, LANES)

    received, near, mix_in = lax.optimization_barrier((received, received[:, ROWS:], mix_in))
    near_pair = lax.ppermute(near, "seq", swap_chip)
    halves = lax.all_to_all(
        jnp.broadcast_to(received, (2,) + received.shape),
        "seq",
        split_axis=0,
        concat_axis=0,
        tiled=True,
        axis_index_groups=[[i, i + 1] for i in range(0, seq_count, 2)],
    )
    halves = flat(halves)
    shape = (ROWS, points, LANES)
    wide = (ROWS, points, 2 * LANES)
    (spec,) = call(
        first_kernel,
        ids,
        (halves, mix_in, twist, inner, lane_in),
        (0, 0, 0, 0, 0),
        [(ROWS * points, 2 * LANES)],
        [shape, shape, wide],
        cost_us=4,
    )
    near_pair, spec = lax.optimization_barrier((near_pair, spec))
    far_pair = lax.ppermute(near_pair, "seq", swap_core)
    given, mid = call(
        second_kernel,
        ids,
        (
            halves,
            flat(near_pair),
            flat(far_pair),
            spec,
            mix_in,
            mix_out,
            twist,
            inner,
            lane_in,
            lane_out,
        ),
        (0,) * 10,
        [(seq_count * HALF, LANES), wide],
        [shape, shape],
        cost_us=6,
    )
    (kept,) = call(
        third_kernel,
        ids,
        (mid, mix_out),
        (0, 0),
        [(seq_count * HALF, LANES)],
        [],
        cost_us=2,
    )
    result = kept + lax.ppermute(given, "seq", swap_core)
    result = exchange(result.reshape(points, ROWS, LANES))
    per_group = ROWS // groups
    lag = result.reshape(channels, 2, groups, per_group, LANES)[:, 1].transpose(1, 0, 2, 3)
    lag = lax.all_to_all(lag, "ch", split_axis=0, concat_axis=0, tiled=True)
    (in_grad,) = call(
        finish_kernel,
        ids,
        (flat(result), out_grad, skip_bias),
        (0, 0, 0),
        [(channels, BLOCK)],
        [(all_channels, LANES)],
        cost_us=2,
    )
    (feat_grad,) = call(
        functools.partial(project_kernel, total),
        ids,
        (filter_weight, flat(lag), rates),
        (0, 0, 0),
        [(filter_weight.shape[0], BLOCK // groups)],
        [],
        cost_us=1,
    )
    return (in_grad, feat_grad)


def solution(mesh):
    in_specs = (P("ch", "seq"), P("ch", "seq"), P(None, "seq"), P(), P(), P())
    out_specs = (P("ch", "seq"), P(None, ("seq", "ch")))
    return jax.shard_map(local, mesh=mesh, in_specs=in_specs, out_specs=out_specs, check_vma=False)
```

```python
import functools
import math

import jax
import jax.numpy as jnp
import numpy as np
from jax import lax
from jax.experimental import pallas as pl
from jax.experimental.pallas import tpu as pltpu
from jax.sharding import PartitionSpec as P

SHIFT = 0.05
LANES = 128
ROWS = 32
BLOCK = ROWS * LANES
HALF = ROWS // 2
CHUNK = ROWS + HALF
VMEM_BYTES = 40 * 1024 * 1024
VMEM_MOST = 63 * 1024 * 1024


@functools.lru_cache(maxsize=None)
def tables(seq_count):
    points = seq_count // 2
    circle = 2.0 * np.pi

    def waves(turns):
        return np.stack([np.cos(circle * turns), -np.sin(circle * turns)]).astype(np.float32)

    dev = np.arange(seq_count).reshape(points, 2).T.reshape(-1)
    lane, row = np.arange(LANES), np.arange(ROWS)
    across, by_lane, by_row = [], [], []
    for half in range(2):
        freq = 4 * (2 * np.arange(points) + half) + 1
        step = np.outer(freq, dev) % (4 * seq_count) / (4.0 * seq_count)
        across.append(np.concatenate(list(waves(step))))
        by_lane.append(waves(np.outer(freq, lane) / (4.0 * seq_count * BLOCK)))
        by_row.append(waves(np.outer(freq, row) / (4.0 * seq_count * ROWS)))
    inner = waves(np.outer(row, lane) / BLOCK)
    lanes = waves(np.outer(lane, lane) % LANES / LANES)
    return np.stack(across), np.stack(by_lane), np.stack(by_row), inner, lanes


def stack_pair(matrix, out_ref):
    rows, columns = matrix.shape
    high, low = split(matrix)
    out_ref[:rows, :columns] = high
    out_ref[:rows, columns:] = high
    out_ref[rows:, :columns] = low
    out_ref[rows:, columns:] = jnp.zeros_like(low)


def build_tables(
    across_ref, by_lane_ref, by_row_ref, lanes_ref, mix_ref, back_ref, twist_ref, lane_ref, lane_back_ref
):
    across = across_ref[0]
    stack_pair(across, mix_ref)
    stack_pair(across.T * (1.0 / (across.shape[0] * BLOCK)), back_ref)
    cos, sin = lanes_ref[0], lanes_ref[1]
    for part, (c, s, t) in enumerate(zip(split(cos), split(sin), split(-sin))):
        lane_ref[part, :LANES, :LANES] = c
        lane_ref[part, :LANES, LANES:] = s
        lane_ref[part, LANES:, :LANES] = t
        lane_ref[part, LANES:, LANES:] = c
        lane_back_ref[part, :LANES, :LANES] = c
        lane_back_ref[part, :LANES, LANES:] = t
        lane_back_ref[part, LANES:, :LANES] = s
        lane_back_ref[part, LANES:, LANES:] = c
    lane_re, lane_im = by_lane_ref[0, 0], by_lane_ref[0, 1]
    row_re, row_im = by_row_ref[0, 0], by_row_ref[0, 1]
    for row in range(ROWS):
        re, im = times(lane_re, lane_im, row_re[:, row : row + 1], row_im[:, row : row + 1])
        twist_ref[0, row] = re
        twist_ref[1, row] = im


def dot(left, right):
    return jnp.dot(left, right, preferred_element_type=jnp.float32)


def split(values):
    high = values.astype(jnp.bfloat16)
    low = (values - high.astype(jnp.float32)).astype(jnp.bfloat16)
    return high, low


def times(a, b, re, im):
    return a * re - b * im, a * im + b * re


def scaled(a, b, number, sign):
    re, im = math.cos(number), sign * math.sin(number)
    if abs(im) < 1e-12 and re > 0:
        return a, b
    if abs(re) < 1e-12:
        return (-b, a) if im > 0 else (b, -a)
    return a * re - b * im, a * im + b * re


def four_points(vals, sign):
    (ar, ai), (br, bi), (cr, ci), (dr, di) = vals
    sr, si = ar + cr, ai + ci
    tr, ti = ar - cr, ai - ci
    ur, ui = br + dr, bi + di
    vr, vi = br - dr, bi - di
    if sign < 0:
        vr, vi = vi, -vr
    else:
        vr, vi = -vi, vr
    return [(sr + ur, si + ui), (tr + vr, ti + vi), (sr - ur, si - ui), (tr - vr, ti - vi)]


def eight_points(vals, sign):
    even = four_points(vals[0::2], sign)
    odd = four_points(vals[1::2], sign)
    low, high = [], []
    for index in range(4):
        er, ei = even[index]
        tr, ti = scaled(*odd[index], 2.0 * math.pi * index / 8, sign)
        low.append((er + tr, ei + ti))
        high.append((er - tr, ei - ti))
    return low + high


def short_transform(re_ref, im_ref, points, sign, finish):
    def tile(index, carry):
        rows = pl.ds(pl.multiple_of(index * 8, 8), 8)
        for second in range(8):
            vals = [(re_ref[8 * n + second, rows, :], im_ref[8 * n + second, rows, :]) for n in range(4)]
            vals = four_points(vals, sign)
            for k in range(4):
                re, im = scaled(*vals[k], 2.0 * math.pi * k * second / ROWS, sign)
                re_ref[8 * k + second, rows, :] = re
                im_ref[8 * k + second, rows, :] = im
        for k in range(4):
            vals = [(re_ref[8 * k + n, rows, :], im_ref[8 * k + n, rows, :]) for n in range(8)]
            vals = eight_points(vals, sign)
            for j in range(8):
                finish(k + 4 * j, rows, *vals[j])
        return carry

    lax.fori_loop(0, points // 8, tile, 0)


def forward(load, points, mix_ref, twist_ref, inner_ref, re_ref, im_ref, lane_in_ref):
    count = 2 * points
    for row in range(HALF):
        high, low = split(jnp.concatenate(load(row), axis=1))
        full = dot(mix_ref[...], jnp.concatenate([high, low], axis=0))
        full = full[:count] + full[count:]
        for part in range(2):
            place = row + part * HALF
            lanes = slice(part * LANES, (part + 1) * LANES)
            re, im = times(
                full[:points, lanes],
                full[points:, lanes],
                twist_ref[0, place],
                twist_ref[1, place],
            )
            re_ref[place] = re
            im_ref[place] = im

    def finish(k, rows, re, im):
        re, im = times(re, im, inner_ref[0, k : k + 1, :], inner_ref[1, k : k + 1, :])
        lane_in_ref[k, rows, :LANES] = re
        lane_in_ref[k, rows, LANES:] = im

    short_transform(re_ref, im_ref, points, -1.0, finish)


def lane_product(values, lane_ref):
    high, low = split(values)
    return dot(high, lane_ref[0]) + dot(low, lane_ref[0]) + dot(high, lane_ref[1])


def spread_rows(values):
    return jnp.broadcast_to(values, (LANES, values.shape[1])).T


def window_tile(rate_tile, first, row, total):
    lane = lax.broadcasted_iota(jnp.int32, rate_tile.shape, 1)
    place = (first + row * LANES + lane).astype(jnp.float32) * (1.0 / total)
    return jnp.exp(-rate_tile * place) + SHIFT


def prepare_kernel(
    total,
    ids,
    grad_hbm,
    input_hbm,
    feat_hbm,
    weight_hbm,
    rates_hbm,
    out_hbm,
    grad_ref,
    input_ref,
    feat_ref,
    weight_ref,
    rates_ref,
    out_ref,
    weight_t,
    rate_t,
    small_sems,
    feat_sems,
    grad_sems,
    input_sems,
    out_sems,
):
    channels = grad_ref.shape[0]
    groups = channels // 8
    pieces = feat_sems.shape[0]
    span = BLOCK // pieces

    def copy(source, target, sems, index, *where):
        return pltpu.make_async_copy(source.at[where], target.at[where], sems.at[index])

    weight_copy = copy(weight_hbm, weight_ref, small_sems, 0)
    rates_copy = copy(rates_hbm, rates_ref, small_sems, 1)
    weight_copy.start()
    rates_copy.start()
    grad_copies = [copy(grad_hbm, grad_ref, grad_sems, g, pl.ds(g * 8, 8)) for g in range(groups)]
    input_copies = [
        copy(input_hbm, input_ref, input_sems, g, pl.ds(g * 8, 8)) for g in range(groups)
    ]
    for g in range(groups):
        input_copies[g].start()
        grad_copies[g].start()
    feat_copies = [
        copy(feat_hbm, feat_ref, feat_sems, k, slice(None), pl.ds(k * span, span))
        for k in range(pieces)
    ]
    for feat_copy in feat_copies:
        feat_copy.start()

    first = ids[3] * BLOCK
    start = pl.multiple_of(ids[2] * channels, 8)
    weight_copy.wait()
    rates_copy.wait()
    weight_t[...] = weight_ref[...].T
    rate_t[...] = spread_rows(rates_ref[...])
    high, low = split(weight_t[pl.ds(start, channels), :])
    both = jnp.concatenate([high, low], axis=0)
    rate_tile = rate_t[pl.ds(start, channels), :]
    wide = 2 * LANES
    out_copies = []

    def put(g, part, row, values):
        out_ref[part, g * 8 : g * 8 + 8, row, :] = values

    def send(g, part):
        place = g * 2 + part
        done = pltpu.make_async_copy(
            out_ref.at[part, pl.ds(g * 8, 8)], out_hbm.at[pl.ds(g * 8, 8), part], out_sems.at[place]
        )
        done.start()
        out_copies.append(done)

    for g in range(groups):
        rows = slice(g * 8, g * 8 + 8)
        input_copies[g].wait()
        grad_copies[g].wait()
        for row in range(ROWS):
            here = slice(row * LANES, (row + 1) * LANES)
            put(g, 1, row, input_ref[rows, here])
            put(g, row // HALF, ROWS + row % HALF, grad_ref[rows, here])
        send(g, 1)
    for k in range(pieces):
        feat_copies[k].wait()
        for begin in range(k * span, (k + 1) * span, wide):
            feat_high, feat_low = split(feat_ref[:, begin : begin + wide])
            full = dot(both, feat_high)
            full = full[:channels] + full[channels:] + dot(high, feat_low)
            for part in range(2):
                row = begin // LANES + part
                filt = full[:, part * LANES : (part + 1) * LANES]
                filt = filt * window_tile(rate_tile, first, row, total)
                for g in range(groups):
                    put(g, 0, row, filt[g * 8 : g * 8 + 8])
    for g in range(groups):
        send(g, 0)
    for done in out_copies:
        done.wait()


def prepare(total, ids, operands):
    channels, columns = operands[0].shape
    outer = pl.BlockSpec(memory_space=pltpu.HBM)
    weight_shape = operands[3].shape
    scratch = [operand.shape for operand in operands] + [
        (2, channels, CHUNK, LANES),
        weight_shape[::-1],
        (weight_shape[1], LANES),
    ]
    return pl.pallas_call(
        functools.partial(prepare_kernel, total),
        grid_spec=pltpu.PrefetchScalarGridSpec(
            num_scalar_prefetch=1,
            grid=(1,),
            in_specs=[outer] * len(operands),
            out_specs=outer,
            scratch_shapes=[pltpu.VMEM(shape, jnp.float32) for shape in scratch]
            + [pltpu.SemaphoreType.DMA((n,)) for n in (2, 4, channels // 8, channels // 8, channels // 4)],
        ),
        out_shape=jax.ShapeDtypeStruct((channels, 2, CHUNK, LANES), jnp.float32),
        compiler_params=pltpu.CompilerParams(vmem_limit_bytes=VMEM_MOST),
    )(ids, *operands)


def first_kernel(
    ids,
    halves_ref,
    across_ref,
    by_lane_ref,
    by_row_ref,
    inner_ref,
    lanes_ref,
    out_ref,
    mix_ref,
    back_ref,
    twist_ref,
    lane_ref,
    lane_back_ref,
    re_ref,
    im_ref,
    mid_ref,
):
    build_tables(
        across_ref,
        by_lane_ref,
        by_row_ref,
        lanes_ref,
        mix_ref,
        back_ref,
        twist_ref,
        lane_ref,
        lane_back_ref,
    )
    count = halves_ref.shape[0] // CHUNK
    points = count // 2

    def load(row):
        return [
            halves_ref[pl.ds(place, count, stride=CHUNK), :] for place in (row, row + HALF)
        ]

    forward(load, points, mix_ref, twist_ref, inner_ref, re_ref, im_ref, mid_ref)
    step = max(1, 256 // points)
    for k in range(0, ROWS, step):
        values = mid_ref[k : k + step].reshape(step * points, 2 * LANES)
        out_ref[k * points : (k + step) * points, :] = lane_product(values, lane_ref)


def second_kernel(
    ids,
    halves_ref,
    near_pair_ref,
    far_pair_ref,
    spec_ref,
    mix_ref,
    back_ref,
    twist_ref,
    inner_ref,
    lane_ref,
    lane_back_ref,
    given_ref,
    mid_ref,
    re_ref,
    im_ref,
):
    count = halves_ref.shape[0] // CHUNK
    points = count // 2
    upper = ids[0] == 1
    second = ids[1] == 1

    def load(row):
        here = pl.ds(row, points, stride=HALF)
        near, far = near_pair_ref[here, :], far_pair_ref[here, :]
        pair = jnp.concatenate(
            [jnp.where(upper, far, near), jnp.where(upper, near, far)], axis=0
        )
        own = halves_ref[pl.ds(ROWS + row, count, stride=CHUNK), :]
        return [jnp.where(second, pair, own), jnp.where(second, own, pair)]

    forward(load, points, mix_ref, twist_ref, inner_ref, re_ref, im_ref, mid_ref)
    step = max(1, 256 // points)
    for k in range(0, ROWS, step):
        values = mid_ref[k : k + step].reshape(step * points, 2 * LANES)
        values = lane_product(values, lane_ref)
        spec = spec_ref[k * points : (k + step) * points, :]
        re, im = times(
            values[:, :LANES], values[:, LANES:], spec[:, :LANES], -spec[:, LANES:]
        )
        values = lane_product(jnp.concatenate([re, im], axis=1), lane_back_ref)
        for j in range(step):
            rows = slice(j * points, (j + 1) * points)
            re, im = times(
                values[rows, :LANES],
                values[rows, LANES:],
                inner_ref[0, k + j : k + j + 1, :],
                -inner_ref[1, k + j : k + j + 1, :],
            )
            re_ref[k + j] = re
            im_ref[k + j] = im

    def finish(k, rows, re, im):
        re, im = times(re, im, twist_ref[0, k, rows, :], -twist_ref[1, k, rows, :])
        mid_ref[k, rows, :LANES] = re
        mid_ref[k, rows, LANES:] = im

    short_transform(re_ref, im_ref, points, 1.0, finish)
    back_half(mid_ref, back_ref, given_ref, 1 - ids[0])


def back_half(mid_ref, back_ref, out_ref, core):
    count = back_ref.shape[0] // 2
    points = count // 2
    start = pl.multiple_of(core * points, points)
    matrix = jnp.concatenate(
        [back_ref[pl.ds(start, points), :], back_ref[pl.ds(count + start, points), :]], axis=0
    )
    for row in range(0, ROWS, 2):
        both = []
        for place in (row, row + 1):
            values = mid_ref[place]
            both.append(jnp.concatenate([values[:, :LANES], values[:, LANES:]], axis=0))
        high, low = split(jnp.concatenate(both, axis=1))
        full = dot(matrix, jnp.concatenate([high, low], axis=0))
        full = full[:points] + full[points:]
        for part in range(2):
            here = pl.ds(row + part, points, stride=ROWS)
            out_ref[here, :] = full[:, part * LANES : (part + 1) * LANES]


def third_kernel(ids, mid_ref, back_ref, kept_ref):
    back_half(mid_ref, back_ref, kept_ref, ids[0])


def finish_kernel(ids, back_ref, grad_ref, bias_ref, in_grad_ref, bias_t):
    channels = grad_ref.shape[0]
    own = pl.ds(pl.multiple_of(ids[2] * channels, 8), channels)
    bias_t[...] = spread_rows(bias_ref[...])
    bias_tile = bias_t[own, :]
    for row in range(ROWS):
        here = slice(row * LANES, (row + 1) * LANES)
        conv = back_ref[pl.ds(row, channels, stride=4 * HALF), :]
        in_grad_ref[:, here] = conv + bias_tile * grad_ref[:, here]


def project_kernel(total, ids, weight_ref, lag_ref, rates_ref, out_ref):
    rows, channels = weight_ref.shape
    per_group = lag_ref.shape[0] // channels
    first = ids[3] * BLOCK + ids[2] * (per_group * LANES)
    high, low = split(weight_ref[...])
    both = jnp.concatenate([high, low], axis=0)
    rate_tile = spread_rows(rates_ref[...])
    for row in range(0, per_group, 2):
        tiles = [
            lag_ref[pl.ds(row + part, channels, stride=per_group), :]
            * window_tile(rate_tile, first, row + part, total)
            for part in range(2)
        ]
        value_high, value_low = split(jnp.concatenate(tiles, axis=1))
        full = dot(both, value_high)
        full = full[:rows] + full[rows:] + dot(high, value_low)
        out_ref[:, row * LANES : (row + 2) * LANES] = full


def whole(array):
    return pl.BlockSpec(array.shape, lambda i, ids: (0,) * array.ndim)


def by_core(array):
    return pl.BlockSpec((1,) + array.shape[1:], lambda i, ids: (ids[0],) + (0,) * (array.ndim - 1))


def call(kernel, ids, operands, kinds, out_shapes, scratch, cost_us=0):
    specs = [by_core(a) if kind else whole(a) for a, kind in zip(operands, kinds)]
    outs = [
        jax.ShapeDtypeStruct(shape[1:], shape[0])
        if shape[0] == jnp.bfloat16
        else jax.ShapeDtypeStruct(shape, jnp.float32)
        for shape in out_shapes
    ]
    out_specs = [whole(out) for out in outs]
    return pl.pallas_call(
        kernel,
        grid_spec=pltpu.PrefetchScalarGridSpec(
            num_scalar_prefetch=1,
            grid=(1,),
            in_specs=specs,
            out_specs=out_specs,
            scratch_shapes=[pltpu.VMEM(shape, jnp.float32) for shape in scratch],
        ),
        out_shape=outs,
        cost_estimate=pl.CostEstimate(
            flops=cost_us * 500_000_000, bytes_accessed=cost_us * 2_000_000, transcendentals=0
        ),
        compiler_params=pltpu.CompilerParams(vmem_limit_bytes=VMEM_BYTES),
    )(ids, *operands)


def local(out_grad, gated_input, features, filter_weight, rates, skip_bias):
    channels = out_grad.shape[0]
    seq_count = lax.axis_size("seq")
    groups = lax.axis_size("ch")
    all_channels = channels * groups
    points = seq_count // 2
    total = seq_count * BLOCK
    place = lax.axis_index("seq")
    ids = jnp.stack([place % 2, (place // 2) % 2, lax.axis_index("ch"), place]).astype(jnp.int32)
    across, by_lane, by_row, inner, lanes = (jnp.asarray(table) for table in tables(seq_count))
    swap_core = [(i, i ^ 1) for i in range(seq_count)]
    swap_chip = [(i, i ^ 2) for i in range(seq_count)]
    rates = rates.reshape(1, all_channels)
    skip_bias = skip_bias.reshape(1, all_channels)

    packed = prepare(
        total,
        ids,
        (out_grad, gated_input, features, filter_weight, rates),
    )
    same_core = [list(range(core, seq_count, 2)) for core in range(2)]

    def exchange(array):
        return lax.all_to_all(
            array, "seq", split_axis=0, concat_axis=0, tiled=True, axis_index_groups=same_core
        )

    received = exchange(packed.reshape(points, CHUNK, LANES))
    def flat(array):
        return array.reshape(-1, LANES)

    received, near = lax.optimization_barrier((received, received[:, ROWS:]))
    near_pair = lax.ppermute(near, "seq", swap_chip)
    halves = lax.all_to_all(
        jnp.broadcast_to(received, (2,) + received.shape),
        "seq",
        split_axis=0,
        concat_axis=0,
        tiled=True,
        axis_index_groups=[[i, i + 1] for i in range(0, seq_count, 2)],
    )
    halves = flat(halves)
    shape = (ROWS, points, LANES)
    wide = (ROWS, points, 2 * LANES)
    half = jnp.bfloat16
    spec, mix_in, mix_out, twist, lane_in, lane_out = call(
        first_kernel,
        ids,
        (halves, across, by_lane, by_row, inner, lanes),
        (0, 1, 1, 1, 0, 0),
        [
            (ROWS * points, 2 * LANES),
            (half, 2 * seq_count, 2 * seq_count),
            (half, 2 * seq_count, 2 * seq_count),
            (2, ROWS, points, LANES),
            (half, 2, 2 * LANES, 2 * LANES),
            (half, 2, 2 * LANES, 2 * LANES),
        ],
        [shape, shape, wide],
        cost_us=4,
    )
    near_pair, spec = lax.optimization_barrier((near_pair, spec))
    far_pair = lax.ppermute(near_pair, "seq", swap_core)
    given, mid = call(
        second_kernel,
        ids,
        (
            halves,
            flat(near_pair),
            flat(far_pair),
            spec,
            mix_in,
            mix_out,
            twist,
            inner,
            lane_in,
            lane_out,
        ),
        (0,) * 10,
        [(seq_count * HALF, LANES), wide],
        [shape, shape],
        cost_us=6,
    )
    (kept,) = call(
        third_kernel,
        ids,
        (mid, mix_out),
        (0, 0),
        [(seq_count * HALF, LANES)],
        [],
        cost_us=2,
    )
    result = kept + lax.ppermute(given, "seq", swap_core)
    result = exchange(result.reshape(points, ROWS, LANES))
    per_group = ROWS // groups
    lag = result.reshape(channels, 2, groups, per_group, LANES)
    lag = jnp.concatenate([lag[None, :, 1, group] for group in range(groups)], axis=0)
    lag = lax.all_to_all(lag, "ch", split_axis=0, concat_axis=0, tiled=True)
    (in_grad,) = call(
        finish_kernel,
        ids,
        (flat(result), out_grad, skip_bias),
        (0, 0, 0),
        [(channels, BLOCK)],
        [(all_channels, LANES)],
        cost_us=2,
    )
    (feat_grad,) = call(
        functools.partial(project_kernel, total),
        ids,
        (filter_weight, flat(lag), rates),
        (0, 0, 0),
        [(filter_weight.shape[0], BLOCK // groups)],
        [],
        cost_us=1,
    )
    return (in_grad, feat_grad)


def solution(mesh):
    in_specs = (P("ch", "seq"), P("ch", "seq"), P(None, "seq"), P(), P(), P())
    out_specs = (P("ch", "seq"), P(None, ("seq", "ch")))
    return jax.shard_map(local, mesh=mesh, in_specs=in_specs, out_specs=out_specs, check_vma=False)
```

```python
import functools
import math

import jax
import jax.numpy as jnp
import numpy as np
from jax import lax
from jax.experimental import pallas as pl
from jax.experimental.pallas import tpu as pltpu
from jax.sharding import PartitionSpec as P

SHIFT = 0.05
LANES = 128
ROWS = 32
BLOCK = ROWS * LANES
HALF = ROWS // 2
CHUNK = ROWS + HALF
VMEM_BYTES = 40 * 1024 * 1024
VMEM_MOST = 63 * 1024 * 1024


@functools.lru_cache(maxsize=None)
def tables(seq_count):
    points = seq_count // 2
    circle = 2.0 * np.pi

    def waves(turns):
        return np.stack([np.cos(circle * turns), -np.sin(circle * turns)]).astype(np.float32)

    dev = np.arange(seq_count).reshape(points, 2).T.reshape(-1)
    lane, row = np.arange(LANES), np.arange(ROWS)
    across, by_lane, by_row = [], [], []
    for half in range(2):
        freq = 4 * (2 * np.arange(points) + half) + 1
        step = np.outer(freq, dev) % (4 * seq_count) / (4.0 * seq_count)
        across.append(np.concatenate(list(waves(step))))
        by_lane.append(waves(np.outer(freq, lane) / (4.0 * seq_count * BLOCK)))
        by_row.append(waves(np.outer(freq, row) / (4.0 * seq_count * ROWS)))
    inner = waves(np.outer(row, lane) / BLOCK)
    lanes = waves(np.outer(lane, lane) % LANES / LANES)
    return np.stack(across), np.stack(by_lane), np.stack(by_row), inner, lanes


def stack_pair(matrix, out_ref):
    rows, columns = matrix.shape
    high, low = split(matrix)
    out_ref[:rows, :columns] = high
    out_ref[:rows, columns:] = high
    out_ref[rows:, :columns] = low
    out_ref[rows:, columns:] = jnp.zeros_like(low)


def build_tables(
    across_ref, by_lane_ref, by_row_ref, lanes_ref, mix_ref, back_ref, twist_ref, lane_ref, lane_back_ref
):
    across = across_ref[0]
    stack_pair(across, mix_ref)
    stack_pair(across.T * (1.0 / (across.shape[0] * BLOCK)), back_ref)
    cos, sin = lanes_ref[0], lanes_ref[1]
    for part, (c, s, t) in enumerate(zip(split(cos), split(sin), split(-sin))):
        lane_ref[part, :LANES, :LANES] = c
        lane_ref[part, :LANES, LANES:] = s
        lane_ref[part, LANES:, :LANES] = t
        lane_ref[part, LANES:, LANES:] = c
        lane_back_ref[part, :LANES, :LANES] = c
        lane_back_ref[part, :LANES, LANES:] = t
        lane_back_ref[part, LANES:, :LANES] = s
        lane_back_ref[part, LANES:, LANES:] = c
    lane_re, lane_im = by_lane_ref[0, 0], by_lane_ref[0, 1]
    row_re, row_im = by_row_ref[0, 0], by_row_ref[0, 1]
    for row in range(ROWS):
        re, im = times(lane_re, lane_im, row_re[:, row : row + 1], row_im[:, row : row + 1])
        twist_ref[0, row] = re
        twist_ref[1, row] = im


def dot(left, right):
    return jnp.dot(left, right, preferred_element_type=jnp.float32)


def split(values):
    high = values.astype(jnp.bfloat16)
    low = (values - high.astype(jnp.float32)).astype(jnp.bfloat16)
    return high, low


def times(a, b, re, im):
    return a * re - b * im, a * im + b * re


def scaled(a, b, number, sign):
    re, im = math.cos(number), sign * math.sin(number)
    if abs(im) < 1e-12 and re > 0:
        return a, b
    if abs(re) < 1e-12:
        return (-b, a) if im > 0 else (b, -a)
    return a * re - b * im, a * im + b * re


def four_points(vals, sign):
    (ar, ai), (br, bi), (cr, ci), (dr, di) = vals
    sr, si = ar + cr, ai + ci
    tr, ti = ar - cr, ai - ci
    ur, ui = br + dr, bi + di
    vr, vi = br - dr, bi - di
    if sign < 0:
        vr, vi = vi, -vr
    else:
        vr, vi = -vi, vr
    return [(sr + ur, si + ui), (tr + vr, ti + vi), (sr - ur, si - ui), (tr - vr, ti - vi)]


def eight_points(vals, sign):
    even = four_points(vals[0::2], sign)
    odd = four_points(vals[1::2], sign)
    low, high = [], []
    for index in range(4):
        er, ei = even[index]
        tr, ti = scaled(*odd[index], 2.0 * math.pi * index / 8, sign)
        low.append((er + tr, ei + ti))
        high.append((er - tr, ei - ti))
    return low + high


def short_transform(re_ref, im_ref, points, sign, finish):
    def tile(index, carry):
        rows = pl.ds(pl.multiple_of(index * 8, 8), 8)
        for second in range(8):
            vals = [(re_ref[8 * n + second, rows, :], im_ref[8 * n + second, rows, :]) for n in range(4)]
            vals = four_points(vals, sign)
            for k in range(4):
                re, im = scaled(*vals[k], 2.0 * math.pi * k * second / ROWS, sign)
                re_ref[8 * k + second, rows, :] = re
                im_ref[8 * k + second, rows, :] = im
        for k in range(4):
            vals = [(re_ref[8 * k + n, rows, :], im_ref[8 * k + n, rows, :]) for n in range(8)]
            vals = eight_points(vals, sign)
            for j in range(8):
                finish(k + 4 * j, rows, *vals[j])
        return carry

    lax.fori_loop(0, points // 8, tile, 0)


def forward(load, points, mix_ref, twist_ref, inner_ref, re_ref, im_ref, lane_in_ref):
    count = 2 * points
    for row in range(HALF):
        high, low = split(jnp.concatenate(load(row), axis=1))
        full = dot(mix_ref[...], jnp.concatenate([high, low], axis=0))
        full = full[:count] + full[count:]
        for part in range(2):
            place = row + part * HALF
            lanes = slice(part * LANES, (part + 1) * LANES)
            re, im = times(
                full[:points, lanes],
                full[points:, lanes],
                twist_ref[0, place],
                twist_ref[1, place],
            )
            re_ref[place] = re
            im_ref[place] = im

    def finish(k, rows, re, im):
        re, im = times(re, im, inner_ref[0, k : k + 1, :], inner_ref[1, k : k + 1, :])
        lane_in_ref[k, rows, :LANES] = re
        lane_in_ref[k, rows, LANES:] = im

    short_transform(re_ref, im_ref, points, -1.0, finish)


def lane_product(values, lane_ref):
    high, low = split(values)
    return dot(high, lane_ref[0]) + dot(low, lane_ref[0]) + dot(high, lane_ref[1])


def spread_rows(values):
    return jnp.broadcast_to(values, (LANES, values.shape[1])).T


def window_tile(rate_tile, first, row, total):
    lane = lax.broadcasted_iota(jnp.int32, rate_tile.shape, 1)
    place = (first + row * LANES + lane).astype(jnp.float32) * (1.0 / total)
    return jnp.exp(-rate_tile * place) + SHIFT


def prepare_kernel(
    total,
    ids,
    grad_hbm,
    input_hbm,
    feat_hbm,
    weight_hbm,
    rates_hbm,
    out_hbm,
    grad_ref,
    input_ref,
    feat_ref,
    weight_ref,
    rates_ref,
    out_ref,
    weight_t,
    rate_t,
    small_sems,
    feat_sems,
    grad_sems,
    input_sems,
    out_sems,
):
    channels = grad_ref.shape[0]
    groups = channels // 8
    pieces = feat_sems.shape[0]
    span = BLOCK // pieces

    def copy(source, target, sems, index, *where):
        return pltpu.make_async_copy(source.at[where], target.at[where], sems.at[index])

    weight_copy = copy(weight_hbm, weight_ref, small_sems, 0)
    rates_copy = copy(rates_hbm, rates_ref, small_sems, 1)
    weight_copy.start()
    rates_copy.start()
    grad_copies = [copy(grad_hbm, grad_ref, grad_sems, g, pl.ds(g * 8, 8)) for g in range(groups)]
    input_copies = [
        copy(input_hbm, input_ref, input_sems, g, pl.ds(g * 8, 8)) for g in range(groups)
    ]
    for g in range(groups):
        input_copies[g].start()
        grad_copies[g].start()
    feat_copies = [
        copy(feat_hbm, feat_ref, feat_sems, k, slice(None), pl.ds(k * span, span))
        for k in range(pieces)
    ]
    for feat_copy in feat_copies:
        feat_copy.start()

    first = ids[3] * BLOCK
    start = pl.multiple_of(ids[2] * channels, 8)
    weight_copy.wait()
    rates_copy.wait()
    weight_t[...] = weight_ref[...].T
    rate_t[...] = spread_rows(rates_ref[...])
    high, low = split(weight_t[pl.ds(start, channels), :])
    both = jnp.concatenate([high, low], axis=0)
    rate_tile = rate_t[pl.ds(start, channels), :]
    wide = 2 * LANES
    out_copies = []

    def put(g, part, row, values):
        out_ref[part, g * 8 : g * 8 + 8, row, :] = values

    def send(g, part):
        place = g * 2 + part
        done = pltpu.make_async_copy(
            out_ref.at[part, pl.ds(g * 8, 8)], out_hbm.at[pl.ds(g * 8, 8), part], out_sems.at[place]
        )
        done.start()
        out_copies.append(done)

    for g in range(groups):
        rows = slice(g * 8, g * 8 + 8)
        input_copies[g].wait()
        grad_copies[g].wait()
        for row in range(ROWS):
            here = slice(row * LANES, (row + 1) * LANES)
            put(g, 1, row, input_ref[rows, here])
            put(g, row // HALF, ROWS + row % HALF, grad_ref[rows, here])
        send(g, 1)
    for k in range(pieces):
        feat_copies[k].wait()
        for begin in range(k * span, (k + 1) * span, wide):
            feat_high, feat_low = split(feat_ref[:, begin : begin + wide])
            full = dot(both, feat_high)
            full = full[:channels] + full[channels:] + dot(high, feat_low)
            for part in range(2):
                row = begin // LANES + part
                filt = full[:, part * LANES : (part + 1) * LANES]
                filt = filt * window_tile(rate_tile, first, row, total)
                for g in range(groups):
                    put(g, 0, row, filt[g * 8 : g * 8 + 8])
    for g in range(groups):
        send(g, 0)
    for done in out_copies:
        done.wait()


def prepare(total, ids, operands):
    channels, columns = operands[0].shape
    outer = pl.BlockSpec(memory_space=pltpu.HBM)
    weight_shape = operands[3].shape
    scratch = [operand.shape for operand in operands] + [
        (2, channels, CHUNK, LANES),
        weight_shape[::-1],
        (weight_shape[1], LANES),
    ]
    return pl.pallas_call(
        functools.partial(prepare_kernel, total),
        grid_spec=pltpu.PrefetchScalarGridSpec(
            num_scalar_prefetch=1,
            grid=(1,),
            in_specs=[outer] * len(operands),
            out_specs=outer,
            scratch_shapes=[pltpu.VMEM(shape, jnp.float32) for shape in scratch]
            + [pltpu.SemaphoreType.DMA((n,)) for n in (2, 4, channels // 8, channels // 8, channels // 4)],
        ),
        out_shape=jax.ShapeDtypeStruct((channels, 2, CHUNK, LANES), jnp.float32),
        compiler_params=pltpu.CompilerParams(vmem_limit_bytes=VMEM_MOST),
    )(ids, *operands)


def first_kernel(
    ids,
    halves_ref,
    across_ref,
    by_lane_ref,
    by_row_ref,
    inner_ref,
    lanes_ref,
    out_ref,
    mix_ref,
    back_ref,
    twist_ref,
    lane_ref,
    lane_back_ref,
    re_ref,
    im_ref,
    mid_ref,
):
    build_tables(
        across_ref,
        by_lane_ref,
        by_row_ref,
        lanes_ref,
        mix_ref,
        back_ref,
        twist_ref,
        lane_ref,
        lane_back_ref,
    )
    count = halves_ref.shape[0] // CHUNK
    points = count // 2

    def load(row):
        return [
            halves_ref[pl.ds(place, count, stride=CHUNK), :] for place in (row, row + HALF)
        ]

    forward(load, points, mix_ref, twist_ref, inner_ref, re_ref, im_ref, mid_ref)
    step = max(1, 256 // points)
    for k in range(0, ROWS, step):
        values = mid_ref[k : k + step].reshape(step * points, 2 * LANES)
        out_ref[k * points : (k + step) * points, :] = lane_product(values, lane_ref)


def second_kernel(
    ids,
    halves_ref,
    near_pair_ref,
    far_pair_ref,
    spec_ref,
    mix_ref,
    back_ref,
    twist_ref,
    inner_ref,
    lane_ref,
    lane_back_ref,
    given_ref,
    mid_ref,
    re_ref,
    im_ref,
):
    count = halves_ref.shape[0] // CHUNK
    points = count // 2
    upper = ids[0] == 1
    second = ids[1] == 1

    def load(row):
        here = pl.ds(row, points, stride=HALF)
        near, far = near_pair_ref[here, :], far_pair_ref[here, :]
        pair = jnp.concatenate(
            [jnp.where(upper, far, near), jnp.where(upper, near, far)], axis=0
        )
        own = halves_ref[pl.ds(ROWS + row, count, stride=CHUNK), :]
        return [jnp.where(second, pair, own), jnp.where(second, own, pair)]

    forward(load, points, mix_ref, twist_ref, inner_ref, re_ref, im_ref, mid_ref)
    step = max(1, 256 // points)
    for k in range(0, ROWS, step):
        values = mid_ref[k : k + step].reshape(step * points, 2 * LANES)
        values = lane_product(values, lane_ref)
        spec = spec_ref[k * points : (k + step) * points, :]
        re, im = times(
            values[:, :LANES], values[:, LANES:], spec[:, :LANES], -spec[:, LANES:]
        )
        values = lane_product(jnp.concatenate([re, im], axis=1), lane_back_ref)
        for j in range(step):
            rows = slice(j * points, (j + 1) * points)
            re, im = times(
                values[rows, :LANES],
                values[rows, LANES:],
                inner_ref[0, k + j : k + j + 1, :],
                -inner_ref[1, k + j : k + j + 1, :],
            )
            re_ref[k + j] = re
            im_ref[k + j] = im

    def finish(k, rows, re, im):
        re, im = times(re, im, twist_ref[0, k, rows, :], -twist_ref[1, k, rows, :])
        mid_ref[k, rows, :LANES] = re
        mid_ref[k, rows, LANES:] = im

    short_transform(re_ref, im_ref, points, 1.0, finish)
    back_half(mid_ref, back_ref, given_ref, 1 - ids[0])


def back_half(mid_ref, back_ref, out_ref, core):
    count = back_ref.shape[0] // 2
    points = count // 2
    start = pl.multiple_of(core * points, points)
    matrix = jnp.concatenate(
        [back_ref[pl.ds(start, points), :], back_ref[pl.ds(count + start, points), :]], axis=0
    )
    for row in range(0, ROWS, 2):
        both = []
        for place in (row, row + 1):
            values = mid_ref[place]
            both.append(jnp.concatenate([values[:, :LANES], values[:, LANES:]], axis=0))
        high, low = split(jnp.concatenate(both, axis=1))
        full = dot(matrix, jnp.concatenate([high, low], axis=0))
        full = full[:points] + full[points:]
        for part in range(2):
            here = pl.ds(row + part, points, stride=ROWS)
            out_ref[here, :] = full[:, part * LANES : (part + 1) * LANES]


def third_kernel(ids, mid_ref, back_ref, kept_ref):
    back_half(mid_ref, back_ref, kept_ref, ids[0])


def finish_kernel(
    total, ids, back_ref, grad_ref, bias_ref, rates_ref, in_grad_ref, window_ref, bias_t
):
    channels = grad_ref.shape[0]
    all_channels = rates_ref.shape[1]
    per_group = window_ref.shape[0] // all_channels
    begin = ids[3] * BLOCK + ids[2] * (per_group * LANES)
    rate_tile = spread_rows(rates_ref[...])
    for row in range(per_group):
        window_ref[row * all_channels : (row + 1) * all_channels, :] = window_tile(
            rate_tile, begin, row, total
        )
    own = pl.ds(pl.multiple_of(ids[2] * channels, 8), channels)
    bias_t[...] = spread_rows(bias_ref[...])
    bias_tile = bias_t[own, :]
    for row in range(ROWS):
        here = slice(row * LANES, (row + 1) * LANES)
        conv = back_ref[pl.ds(row, channels, stride=4 * HALF), :]
        in_grad_ref[:, here] = conv + bias_tile * grad_ref[:, here]


def project_kernel(ids, weight_ref, lag_ref, window_ref, out_ref):
    rows, channels = weight_ref.shape
    per_group = lag_ref.shape[0] // channels
    high, low = split(weight_ref[...])
    both = jnp.concatenate([high, low], axis=0)
    for row in range(0, per_group, 2):
        tiles = [
            lag_ref[pl.ds(row + part, channels, stride=per_group), :]
            * window_ref[(row + part) * channels : (row + part + 1) * channels, :]
            for part in range(2)
        ]
        value_high, value_low = split(jnp.concatenate(tiles, axis=1))
        full = dot(both, value_high)
        full = full[:rows] + full[rows:] + dot(high, value_low)
        out_ref[:, row * LANES : (row + 2) * LANES] = full


def whole(array):
    return pl.BlockSpec(array.shape, lambda i, ids: (0,) * array.ndim)


def by_core(array):
    return pl.BlockSpec((1,) + array.shape[1:], lambda i, ids: (ids[0],) + (0,) * (array.ndim - 1))


def call(kernel, ids, operands, kinds, out_shapes, scratch, cost_us=0):
    specs = [by_core(a) if kind else whole(a) for a, kind in zip(operands, kinds)]
    outs = [
        jax.ShapeDtypeStruct(shape[1:], shape[0])
        if shape[0] == jnp.bfloat16
        else jax.ShapeDtypeStruct(shape, jnp.float32)
        for shape in out_shapes
    ]
    out_specs = [whole(out) for out in outs]
    return pl.pallas_call(
        kernel,
        grid_spec=pltpu.PrefetchScalarGridSpec(
            num_scalar_prefetch=1,
            grid=(1,),
            in_specs=specs,
            out_specs=out_specs,
            scratch_shapes=[pltpu.VMEM(shape, jnp.float32) for shape in scratch],
        ),
        out_shape=outs,
        cost_estimate=pl.CostEstimate(
            flops=cost_us * 500_000_000, bytes_accessed=cost_us * 2_000_000, transcendentals=0
        ),
        compiler_params=pltpu.CompilerParams(vmem_limit_bytes=VMEM_BYTES),
    )(ids, *operands)


def local(out_grad, gated_input, features, filter_weight, rates, skip_bias):
    channels = out_grad.shape[0]
    seq_count = lax.axis_size("seq")
    groups = lax.axis_size("ch")
    all_channels = channels * groups
    points = seq_count // 2
    total = seq_count * BLOCK
    place = lax.axis_index("seq")
    ids = jnp.stack([place % 2, (place // 2) % 2, lax.axis_index("ch"), place]).astype(jnp.int32)
    across, by_lane, by_row, inner, lanes = (jnp.asarray(table) for table in tables(seq_count))
    swap_core = [(i, i ^ 1) for i in range(seq_count)]
    swap_chip = [(i, i ^ 2) for i in range(seq_count)]
    rates = rates.reshape(1, all_channels)
    skip_bias = skip_bias.reshape(1, all_channels)

    packed = prepare(
        total,
        ids,
        (out_grad, gated_input, features, filter_weight, rates),
    )
    same_core = [list(range(core, seq_count, 2)) for core in range(2)]

    def exchange(array):
        return lax.all_to_all(
            array, "seq", split_axis=0, concat_axis=0, tiled=True, axis_index_groups=same_core
        )

    received = exchange(packed.reshape(points, CHUNK, LANES))
    def flat(array):
        return array.reshape(-1, LANES)

    received, near = lax.optimization_barrier((received, received[:, ROWS:]))
    near_pair = lax.ppermute(near, "seq", swap_chip)
    halves = lax.all_to_all(
        jnp.broadcast_to(received, (2,) + received.shape),
        "seq",
        split_axis=0,
        concat_axis=0,
        tiled=True,
        axis_index_groups=[[i, i + 1] for i in range(0, seq_count, 2)],
    )
    halves = flat(halves)
    shape = (ROWS, points, LANES)
    wide = (ROWS, points, 2 * LANES)
    half = jnp.bfloat16
    spec, mix_in, mix_out, twist, lane_in, lane_out = call(
        first_kernel,
        ids,
        (halves, across, by_lane, by_row, inner, lanes),
        (0, 1, 1, 1, 0, 0),
        [
            (ROWS * points, 2 * LANES),
            (half, 2 * seq_count, 2 * seq_count),
            (half, 2 * seq_count, 2 * seq_count),
            (2, ROWS, points, LANES),
            (half, 2, 2 * LANES, 2 * LANES),
            (half, 2, 2 * LANES, 2 * LANES),
        ],
        [shape, shape, wide],
        cost_us=4,
    )
    near_pair, spec = lax.optimization_barrier((near_pair, spec))
    far_pair = lax.ppermute(near_pair, "seq", swap_core)
    given, mid = call(
        second_kernel,
        ids,
        (
            halves,
            flat(near_pair),
            flat(far_pair),
            spec,
            mix_in,
            mix_out,
            twist,
            inner,
            lane_in,
            lane_out,
        ),
        (0,) * 10,
        [(seq_count * HALF, LANES), wide],
        [shape, shape],
        cost_us=6,
    )
    (kept,) = call(
        third_kernel,
        ids,
        (mid, mix_out),
        (0, 0),
        [(seq_count * HALF, LANES)],
        [],
        cost_us=2,
    )
    result = kept + lax.ppermute(given, "seq", swap_core)
    result = exchange(result.reshape(points, ROWS, LANES))
    per_group = ROWS // groups
    lag = result.reshape(channels, 2, groups, per_group, LANES)[:, 1].transpose(1, 0, 2, 3)
    lag = lax.all_to_all(lag, "ch", split_axis=0, concat_axis=0, tiled=True)
    in_grad, window = call(
        functools.partial(finish_kernel, total),
        ids,
        (flat(result), out_grad, skip_bias, rates),
        (0, 0, 0, 0),
        [(channels, BLOCK), (all_channels * per_group, LANES)],
        [(all_channels, LANES)],
        cost_us=2,
    )
    (feat_grad,) = call(
        project_kernel,
        ids,
        (filter_weight, flat(lag), window),
        (0, 0, 0),
        [(filter_weight.shape[0], BLOCK // groups)],
        [],
        cost_us=1,
    )
    return (in_grad, feat_grad)


def solution(mesh):
    in_specs = (P("ch", "seq"), P("ch", "seq"), P(None, "seq"), P(), P(), P())
    out_specs = (P("ch", "seq"), P(None, ("seq", "ch")))
    return jax.shard_map(local, mesh=mesh, in_specs=in_specs, out_specs=out_specs, check_vma=False)
```
